32 devices in a mesh: group: 16 (over z, y, core), tp: 2 (over x).
Axes of the slice: x: 2, y: 2, z: 4, core: 2. Of those that a mesh axis runs over, the one named last changes fastest.
Arguments:
- queries: bfloat16 [1024, 2048], P('group', 'tp'), may hold values from -22 to 22
- new_kv: bfloat16 [1024, 1024], P('group', 'tp'), may hold values from -6 to 6
- local_cache: bfloat16 [4096, 1024], P('group', 'tp'), may hold values from -6 to 6
- remote_pool: bfloat16 [2048, 1024], P('group', 'tp'), may hold values from -6 to 6
- page_index: int32 [16, 16], P('group'), may hold values from 0 to 15, each once within a row
- lengths: int32 [16], P('group'), may hold values from 256 to 384, as said below
- sinks: float32 [32], P('tp'), may hold values from 4 to 8
- out_weight: bfloat16 [2048, 2880], P('tp'), may hold values from -0.125 to 0.125
- residual: bfloat16 [1024, 2880], P('group', 'tp'), may hold values from -6 to 6
- norm_gain: float32 [2880], replicated, may hold values from 0.5 to 2
- routes: int32 [1024, 4], P('group'), may hold values from 0 to 7, all different within a row; in each aligned block of 64 rows (0 to 63, 64 to 127, ...) at most 40 rows name the same one
- route_weights: float32 [1024, 4], P('group'), may hold values from 0.1 to 1
- expert_gate: bfloat16 [16, 2880, 1440], P('group', None, 'tp'), may hold values from -0.109375 to 0.109375
- expert_up: bfloat16 [16, 2880, 1440], P('group', None, 'tp'), may hold values from -0.109375 to 0.109375
- expert_down: bfloat16 [16, 1440, 2880], P('group', None, 'tp'), may hold values from -0.109375 to 0.109375
Outputs:
- layer_out: bfloat16 [1024, 2880], P('group', 'tp')
The draws below stay inside these ranges and needn't reach their ends.
Inputs may be any that keep to these rules, and one draw needn't show every extreme that they name: `lengths`: every request has at least 256 cached positions; some request has exactly 256, some exactly 384. `routes`: within the rows of one request no expert is named by more than 40 rows. `page_index`: each row is a permutation.
All inputs are finite; a program needn't handle non-finite values.
Results may differ from the reference program's by a relative error of at most 0.013.
Values may be sent and summed in bfloat16 or wider, within the bound.
No kernel may reach another device: no remote copies, remote signals or barrier semaphores. Data moves between devices by JAX's collectives and lax.ppermute only.
A program may use at most 128 MiB of HBM per device.

```python
import math
import jax
import jax.numpy as jnp
import numpy as np
from jax import lax

D = 2880
FF = 2880
HQ = 32
HK = 8
HEAD = 64
TOPK = 4
NEW_TOK = 64
LOCAL_LEN = 256
PAGE = 8
REQS = 16
TOKENS = 1024
EXPERTS = 8
CAP = 40


def cached_lengths(key):
    longest = LOCAL_LEN + REQS * PAGE
    values = jax.random.randint(jax.random.fold_in(key, 101), (REQS,), LOCAL_LEN, longest + 1, dtype=jnp.int32)
    chosen = jax.random.randint(jax.random.fold_in(key, 102), (), 0, REQS, dtype=jnp.int32)
    values = values.at[chosen].set(longest)
    values = values.at[(chosen + 1) % REQS].set(LOCAL_LEN)
    return values


def draw_lengths(key, part):
    return cached_lengths(key)


def draw_local_cache(key, part):
    base = jnp.clip(jax.random.normal(jax.random.fold_in(key, 201), (REQS * LOCAL_LEN, HK * 2 * HEAD), jnp.float32), -6.0, 6.0)
    return base.astype(jnp.bfloat16)


def draw_queries(key, part):
    base = 1.5 * jnp.clip(jax.random.normal(jax.random.fold_in(key, 301), (TOKENS, HQ * HEAD), jnp.float32), -6.0, 6.0)
    return base.astype(jnp.bfloat16)


def block_levels(own_key, dims, cuts, low, largest):
    def one(position, shards_of):
        steps = jax.random.uniform(jax.random.fold_in(jax.random.fold_in(own_key, 6), position), (shards_of,), jnp.float32, low / len(cuts), largest / len(cuts))
        return jnp.repeat(jnp.exp(steps), dims[position] // shards_of).reshape((-1,) + (1,) * (len(dims) - position - 1))

    factor_of = one(*cuts[0])
    for cut in cuts[1:]:
        factor_of = factor_of * one(*cut)
    return factor_of


def deal_out(own_key, own, number, rows, amount, top, most, slope):
    sequence = jax.random.permutation(own_key, amount)
    heavy_load, usual = portions_of(amount, rows * top, most, slope, True), portions_of(amount, rows * top, most, slope, False)
    places = jnp.arange(amount)

    def named(sizes, rotation):
        used = int((sizes > 0).sum())
        fixed = max(1, used // 4)
        passed = fixed + (places - fixed + rotation * (used - fixed)) % max(1, amount - fixed)
        return jnp.zeros((amount,), jnp.int32).at[sequence[jnp.where(places < fixed, places, passed)]].set(jnp.asarray(sizes, jnp.int32))

    sizes = jnp.where(number % 4 == 0, named(heavy_load, number // 4), named(usual, number - number // 4 - 1))
    mixed = jax.random.permutation(jax.random.fold_in(own, 3), amount)
    source_of, receiver = mixed[0:amount // 2 * 2:2], mixed[1:amount // 2 * 2:2]
    margin = jnp.minimum(sizes[source_of] - 1, most - sizes[receiver]) // 2
    margin = jnp.where((source_of == sequence[0]) | (receiver == sequence[0]) | (sizes[receiver] == 0), 0, jnp.maximum(margin, 0))
    passed = jax.random.randint(jax.random.fold_in(own, 4), (amount // 2,), 0, 1 << 20) % (margin + 1)
    sizes = sizes.at[source_of].add(-passed).at[receiver].add(passed)
    labels = jnp.searchsorted(jnp.cumsum(sizes), jnp.arange(rows * top), side="right").astype(jnp.int32)
    table = labels.reshape(top, rows).T
    table = table[jax.random.permutation(jax.random.fold_in(own, 1), rows)]
    rotation = jax.random.randint(jax.random.fold_in(own, 2), (rows, 1), 0, top)
    return jnp.take_along_axis(table, (jnp.arange(top)[None, :] + rotation) % top, axis=1)


def portions_of(count, total, most, lean, full):
    weights = [(1 << 20) // math.isqrt(grade ** lean) + 1 for grade in range(1, count + 1)]
    largest = most if full else min(most, max(-(-total // count), total * weights[0] // sum(weights)))
    least = 1 if total - largest >= count - 1 else 0
    holding, rest = [largest] + [least] * (count - 1), total - largest - least * (count - 1)
    while rest > 0:
        candidates = [i for i in range(1, count) if holding[i] < largest] or [i for i in range(1, count) if holding[i] < most]
        mass, remaining = sum([weights[i] for i in candidates]), rest
        for i in candidates:
            more = min(most - holding[i], max(1, remaining * weights[i] // mass), rest)
            holding[i] = holding[i] + more
            rest = rest - more
    return np.array(holding)


def gaussian(rng, shape, spread, most, shards=(), held_as=jnp.bfloat16):
    values = spread * jax.random.normal(rng, shape, jnp.float32)
    if shards:
        values = values * block_levels(rng, shape, shards, -0.22, 0.18)
    return jnp.clip(values, -most, most).astype(held_as)


def setup_inputs(seed: int = 0) -> dict:
    keys = jax.random.split(jax.random.key(seed), 16)
    queries = draw_queries(jax.random.fold_in(keys[15], 71), 0)
    new_kv = gaussian(keys[1], (TOKENS, HK * 2 * HEAD), 1.0, 6.0, ((0, 16), (1, 2)))
    local_cache = draw_local_cache(jax.random.fold_in(keys[15], 71), 0)
    remote_pool = gaussian(keys[3], (REQS * REQS * PAGE, HK * 2 * HEAD), 1.0, 6.0, ((0, 16), (1, 2)))
    page_index = jax.vmap(lambda own: jax.random.permutation(own, REQS))(jax.random.split(keys[4], REQS)).reshape((REQS, REQS)).astype(jnp.int32)
    lengths = draw_lengths(jax.random.fold_in(keys[15], 71), 0)
    sinks = jnp.clip(4.0 + 4.0 * jax.random.uniform(keys[6], (HQ,), jnp.float32) ** block_levels(keys[6], (HQ,), ((0, 2),), -0.2, 0.2), 4.0, 8.0)
    out_weight = gaussian(keys[7], (HQ * HEAD, D), (HQ * HEAD) ** -0.5, 0.125, ((0, 2),))
    residual = gaussian(keys[8], (TOKENS, D), 1.0, 6.0, ((0, 16), (1, 2)))
    norm_gain = jnp.clip(jnp.exp(jax.random.uniform(keys[9], (D,), jnp.float32, math.log(0.5), math.log(2.0))), 0.5, 2.0)
    routes_keys = jax.random.split(jax.random.fold_in(keys[10], 1), TOKENS // NEW_TOK)
    routes_turns = jax.random.permutation(jax.random.fold_in(keys[10], 3), TOKENS // NEW_TOK)
    routes = jax.vmap(lambda own, number: deal_out(jax.random.fold_in(keys[10], 2), own, number, NEW_TOK, EXPERTS, TOPK, CAP, 2))(routes_keys, routes_turns).reshape((TOKENS, TOPK))
    route_weights = jnp.clip(jnp.exp(math.log(1.0) - 2.3025851 * jax.random.uniform(keys[11], (TOKENS, TOPK), jnp.float32) ** block_levels(keys[11], (TOKENS, TOPK), ((0, 16),), -0.2, 0.2)), 0.1, 1.0)
    expert_gate = gaussian(keys[12], (2 * EXPERTS, D, FF // 2), D ** -0.5, 0.109375, ((0, 16), (2, 2)))
    expert_up = gaussian(keys[13], (2 * EXPERTS, D, FF // 2), D ** -0.5, 0.109375, ((0, 16), (2, 2)))
    expert_down = gaussian(keys[14], (2 * EXPERTS, FF // 2, D), FF ** -0.5, 0.109375, ((0, 16), (2, 2)))
    return dict(queries=queries, new_kv=new_kv, local_cache=local_cache, remote_pool=remote_pool, page_index=page_index, lengths=lengths, sinks=sinks, out_weight=out_weight, residual=residual, norm_gain=norm_gain, routes=routes, route_weights=route_weights, expert_gate=expert_gate, expert_up=expert_up, expert_down=expert_down)


THETA = 150000.0
ALPHA = 1.702
EPSILON = 1e-05

def rotate(values, positions):
    half_dim = values.shape[-1] // 2
    inverse = THETA ** (-2.0 * jnp.arange(half_dim, dtype=jnp.float32) / values.shape[-1])
    angles = positions[:, None, None] * inverse[None, None, :]
    cosine = jnp.cos(angles)
    sine_part = jnp.sin(angles)
    first_part = values[..., :half_dim]
    second_part = values[..., half_dim:]
    return jnp.concatenate([first_part * cosine - second_part * sine_part, second_part * cosine + first_part * sine_part], axis=-1)

def attend(query_rows, kv_rows, cache_kv, cache_valid, sinks, length):
    block_len = query_rows.shape[0]
    kv_heads = kv_rows.shape[1] // (2 * HEAD)
    query_heads = query_rows.shape[1] // HEAD
    group_size = query_heads // kv_heads
    positions = (length + jnp.arange(block_len, dtype=jnp.int32)).astype(jnp.float32)
    query_rot = rotate(query_rows.astype(jnp.float32).reshape(block_len, query_heads, HEAD), positions).astype(jnp.bfloat16)
    kv_parts = kv_rows.reshape(block_len, kv_heads, 2, HEAD)
    key_rot = rotate(kv_parts[:, :, 0].astype(jnp.float32), positions).astype(jnp.bfloat16)
    cache_parts = cache_kv.reshape(cache_kv.shape[0], kv_heads, 2, HEAD)
    all_keys = jnp.concatenate([cache_parts[:, :, 0], key_rot], axis=0)
    all_values = jnp.concatenate([cache_parts[:, :, 1], kv_parts[:, :, 1]], axis=0)
    token_order = jnp.arange(block_len, dtype=jnp.int32)
    causal = token_order[None, :] <= token_order[:, None]
    allowed = jnp.concatenate([jnp.broadcast_to(cache_valid[None, :], (block_len, cache_valid.shape[0])), causal], axis=1)
    row_allowed = jnp.repeat(allowed, group_size, axis=0)
    score_scale = HEAD ** (-0.5)
    outputs = []
    for kv_head in range(kv_heads):
        query_block = query_rot[:, kv_head * group_size:(kv_head + 1) * group_size].reshape(block_len * group_size, HEAD)
        scores = jnp.dot(query_block, all_keys[:, kv_head].T, preferred_element_type=jnp.float32) * score_scale
        scores = jnp.where(row_allowed, scores, -jnp.inf)
        sink_rows = jnp.tile(sinks[kv_head * group_size:(kv_head + 1) * group_size], block_len)
        row_max = jnp.maximum(lax.optimization_barrier(jnp.max(scores, axis=1)), sink_rows)
        weights = jnp.exp(scores - row_max[:, None])
        denominator = lax.optimization_barrier(jnp.sum(weights, axis=1)) + jnp.exp(sink_rows - row_max)
        blended = jnp.dot(weights.astype(jnp.bfloat16), all_values[:, kv_head], preferred_element_type=jnp.float32) / denominator[:, None]
        outputs.append(blended.astype(jnp.bfloat16).reshape(block_len, group_size * HEAD))
    return jnp.concatenate(outputs, axis=1)

def reference(queries, new_kv, local_cache, remote_pool, page_index, lengths, sinks, out_weight, residual, norm_gain, routes, route_weights, expert_gate, expert_up, expert_down):
    lane_count = new_kv.shape[1]
    remote_rows = remote_pool.reshape(REQS, REQS, PAGE, lane_count).transpose(1, 0, 2, 3).reshape(REQS, REQS * PAGE, lane_count)
    local_rows = local_cache.reshape(REQS, LOCAL_LEN, lane_count)
    offsets = jnp.arange(PAGE, dtype=jnp.int32)

    def one_request(request_items):
        query_rows, kv_rows, local_part, remote_part, page_row, length = request_items
        remote_pos = LOCAL_LEN + page_row[:, None] * PAGE + offsets[None, :]
        cache_valid = jnp.concatenate([jnp.ones((LOCAL_LEN,), jnp.bool_), (remote_pos < length).reshape(-1)])
        cache_kv = jnp.concatenate([local_part, remote_part], axis=0)
        return attend(query_rows, kv_rows, cache_kv, cache_valid, sinks, length)
    attended = lax.map(one_request, (queries.reshape(REQS, NEW_TOK, -1), new_kv.reshape(REQS, NEW_TOK, lane_count), local_rows, remote_rows, page_index, lengths))
    attended = attended.reshape(TOKENS, -1)
    hidden_state = residual.astype(jnp.float32) + jnp.dot(attended, out_weight, preferred_element_type=jnp.float32)
    mean_square = lax.optimization_barrier(jnp.mean(hidden_state * hidden_state, axis=1, keepdims=True))
    normed = (hidden_state * lax.rsqrt(mean_square + EPSILON) * norm_gain).astype(jnp.bfloat16)
    mixing = route_weights / lax.optimization_barrier(jnp.sum(route_weights, axis=1, keepdims=True))
    capacity = REQS * CAP

    def one_expert(running, expert):
        chosen = routes == expert
        member = jnp.any(chosen, axis=1)
        weight = lax.optimization_barrier(jnp.sum(jnp.where(chosen, mixing, 0.0), axis=1))
        token_index = jnp.nonzero(member, size=capacity, fill_value=0)[0].astype(jnp.int32)
        filled = (jnp.arange(capacity, dtype=jnp.int32) < jnp.sum(member.astype(jnp.int32))).astype(jnp.float32)
        token_rows = normed[token_index]
        summed = jnp.zeros((capacity, D), jnp.float32)
        for which_half in range(2):
            slot_id = 2 * expert + which_half
            gate_val = jnp.dot(token_rows, expert_gate[slot_id], preferred_element_type=jnp.float32)
            up_val = jnp.dot(token_rows, expert_up[slot_id], preferred_element_type=jnp.float32)
            active = (gate_val * jax.nn.sigmoid(ALPHA * gate_val) * (up_val + 1.0)).astype(jnp.bfloat16)
            half_out = jnp.dot(active, expert_down[slot_id], preferred_element_type=jnp.float32).astype(jnp.bfloat16)
            summed = summed + half_out.astype(jnp.float32)
        contrib = (weight[token_index] * filled)[:, None] * summed
        return (running.at[token_index].add(contrib), None)
    moe_out, unused = lax.scan(one_expert, jnp.zeros((TOKENS, D), jnp.float32), jnp.arange(EXPERTS, dtype=jnp.int32))
    return (hidden_state + moe_out).astype(jnp.bfloat16)
```

```python
import functools

import jax
import jax.numpy as jnp
from jax import lax
from jax.experimental import pallas as pl
from jax.experimental.pallas import tpu as pltpu
from jax.sharding import PartitionSpec as P

HEAD = 64
CHUNKS = 2
VMEM_LIMIT = 56 * 1024 * 1024


THETA = 150000.0
ALPHA = 1.702
EPSILON = 1e-05


def rotate(values, positions):
    half_dim = values.shape[-1] // 2
    inverse = THETA ** (-2.0 * jnp.arange(half_dim, dtype=jnp.float32) / values.shape[-1])
    angles = positions[:, None, None] * inverse[None, None, :]
    cosine = jnp.cos(angles)
    sine_part = jnp.sin(angles)
    first_part = values[..., :half_dim]
    second_part = values[..., half_dim:]
    return jnp.concatenate(
        [
            first_part * cosine - second_part * sine_part,
            second_part * cosine + first_part * sine_part,
        ],
        axis=-1,
    )


def attend(query_rows, kv_rows, cache_kv, cache_valid, sinks, length):
    block_len = query_rows.shape[0]
    kv_heads = kv_rows.shape[1] // (2 * HEAD)
    query_heads = query_rows.shape[1] // HEAD
    group_size = query_heads // kv_heads
    positions = (length + jnp.arange(block_len, dtype=jnp.int32)).astype(jnp.float32)
    query_rot = rotate(
        query_rows.astype(jnp.float32).reshape(block_len, query_heads, HEAD), positions
    ).astype(jnp.bfloat16)
    kv_parts = kv_rows.reshape(block_len, kv_heads, 2, HEAD)
    key_rot = rotate(kv_parts[:, :, 0].astype(jnp.float32), positions).astype(jnp.bfloat16)
    cache_parts = cache_kv.reshape(cache_kv.shape[0], kv_heads, 2, HEAD)
    all_keys = jnp.concatenate([cache_parts[:, :, 0], key_rot], axis=0)
    all_values = jnp.concatenate([cache_parts[:, :, 1], kv_parts[:, :, 1]], axis=0)
    token_order = jnp.arange(block_len, dtype=jnp.int32)
    causal = token_order[None, :] <= token_order[:, None]
    allowed = jnp.concatenate(
        [jnp.broadcast_to(cache_valid[None, :], (block_len, cache_valid.shape[0])), causal], axis=1
    )
    row_allowed = jnp.repeat(allowed, group_size, axis=0)
    score_scale = HEAD ** (-0.5)
    outputs = []
    for kv_head in range(kv_heads):
        query_block = query_rot[:, kv_head * group_size : (kv_head + 1) * group_size].reshape(
            block_len * group_size, HEAD
        )
        scores = (
            jnp.dot(query_block, all_keys[:, kv_head].T, preferred_element_type=jnp.float32)
            * score_scale
        )
        scores = jnp.where(row_allowed, scores, -jnp.inf)
        sink_rows = jnp.tile(sinks[kv_head * group_size : (kv_head + 1) * group_size], block_len)
        row_max = jnp.maximum(jnp.max(scores, axis=1), sink_rows)
        weights = jnp.exp(scores - row_max[:, None])
        denominator = jnp.sum(weights, axis=1) + jnp.exp(sink_rows - row_max)
        blended = (
            jnp.dot(
                weights.astype(jnp.bfloat16),
                all_values[:, kv_head],
                preferred_element_type=jnp.float32,
            )
            / denominator[:, None]
        )
        outputs.append(blended.astype(jnp.bfloat16).reshape(block_len, group_size * HEAD))
    return jnp.concatenate(outputs, axis=1)


def exchange(value, axis, offset):
    if offset == 0:
        return value
    size = lax.axis_size(axis)
    return lax.ppermute(value, axis, [(i, i ^ offset) for i in range(size)])


def gate_up_kernel(parts, me_ref, gain_ref, gate_ref, up_ref, *refs):
    out_ref = refs[-1]
    rows = refs[0].shape[0]
    features = gate_ref.shape[0] * gate_ref.shape[1]
    me = me_ref[0]
    for s in range(len(refs[:-1]) // parts):
        held = [refs[s * parts + j][...].astype(jnp.float32) for j in range(parts)]
        square = sum(jnp.sum(h * h, axis=1, keepdims=True) for h in held)
        scale = lax.rsqrt(square / features + EPSILON)
        gate_val = up_val = None
        for j in range(parts):
            place = me ^ j
            normed = (held[j] * scale * gain_ref[place]).astype(jnp.bfloat16)
            g = jnp.dot(normed, gate_ref[place], preferred_element_type=jnp.float32)
            u = jnp.dot(normed, up_ref[place], preferred_element_type=jnp.float32)
            gate_val = g if gate_val is None else gate_val + g
            up_val = u if up_val is None else up_val + u
        active = gate_val * jax.nn.sigmoid(ALPHA * gate_val) * (up_val + 1.0)
        out_ref[pl.ds(s * rows, rows), :] = active.astype(jnp.bfloat16)


def down_kernel(me_ref, down_ref, *refs):
    own_ref, other_ref = refs[-2:]
    rows = own_ref.shape[0]
    me = me_ref[0]
    total = None
    for j, ref in enumerate(refs[:-2]):
        term = jnp.dot(ref[...], down_ref[me ^ j], preferred_element_type=jnp.float32)
        total = term if total is None else total + term
    own_ref[...] = total[:rows].astype(jnp.bfloat16)
    other_ref[...] = total[rows:].astype(jnp.bfloat16)


def vmem_call(kernel, out_shape, scalar, *operands):
    return pl.pallas_call(
        kernel,
        out_shape=out_shape,
        in_specs=[pl.BlockSpec(memory_space=pltpu.SMEM)]
        + [pl.BlockSpec(memory_space=pltpu.VMEM)] * len(operands),
        out_specs=jax.tree.map(lambda _: pl.BlockSpec(memory_space=pltpu.VMEM), out_shape),
        compiler_params=pltpu.CompilerParams(vmem_limit_bytes=VMEM_LIMIT),
    )(scalar, *operands)


def on_device(
    queries,
    new_kv,
    local_cache,
    remote_pool,
    page_index,
    lengths,
    sinks,
    out_weight,
    residual,
    norm_gain,
    routes,
    route_weights,
    expert_gate,
    expert_up,
    expert_down,
):
    groups = lax.axis_size("group")
    tp = lax.axis_size("tp")
    me_tp = lax.axis_index("tp")
    experts = groups // 2
    me_expert = lax.axis_index("group") // 2
    tp_scalar = me_tp.astype(jnp.int32).reshape(1)
    lane_count = remote_pool.shape[1]
    local_len = local_cache.shape[0]
    fetched = lax.all_to_all(
        remote_pool.reshape(groups, -1, lane_count),
        "group",
        split_axis=0,
        concat_axis=0,
        tiled=True,
    )
    page_len = fetched.shape[1]
    length = lengths[0]
    offsets = jnp.arange(page_len, dtype=jnp.int32)
    remote_pos = local_len + page_index[0][:, None] * page_len + offsets[None, :]
    cache_valid = jnp.concatenate(
        [jnp.ones((local_len,), jnp.bool_), (remote_pos < length).reshape(-1)]
    )
    cache_kv = jnp.concatenate([local_cache, fetched.reshape(-1, lane_count)], axis=0)
    attended = attend(queries, new_kv, cache_kv, cache_valid, sinks, length)
    block_len, width = residual.shape
    partial_sum = jnp.dot(attended, out_weight, preferred_element_type=jnp.float32)

    def columns(place):
        return lax.dynamic_slice_in_dim(partial_sum, place * width, width, 1)

    own_state = columns(me_tp) + residual.astype(jnp.float32)
    for j in range(1, tp):
        own_state = own_state + exchange(
            columns(me_tp ^ j).astype(jnp.bfloat16), "tp", j
        ).astype(jnp.float32)
    state_sent = own_state.astype(jnp.bfloat16)

    top_count = routes.shape[1]
    capacity = 5 * block_len * top_count // (4 * experts)
    mixing = route_weights / jnp.sum(route_weights, axis=1, keepdims=True)
    chosen = (routes ^ me_expert)[:, :, None] == jnp.arange(experts, dtype=jnp.int32)
    member = jnp.any(chosen, axis=1)
    mix = jnp.sum(jnp.where(chosen, mixing[:, :, None], 0.0), axis=1)
    earlier = jnp.arange(block_len)[:, None] > jnp.arange(block_len)[None, :]
    rank = jnp.dot(
        earlier.astype(jnp.bfloat16), member.astype(jnp.bfloat16), preferred_element_type=jnp.float32
    ).astype(jnp.int32)
    hit = member.T[:, None, :] & (
        rank.T[:, None, :] == jnp.arange(capacity, dtype=jnp.int32)[None, :, None]
    )
    pick = hit.astype(jnp.bfloat16).reshape(experts * capacity, block_len)
    spread = jnp.where(hit, mix.T[:, None, :], 0.0).reshape(experts * capacity, block_len)
    spread_high = spread.astype(jnp.bfloat16)
    spread_low = (spread - spread_high.astype(jnp.float32)).astype(jnp.bfloat16)

    send = jnp.dot(pick, state_sent, preferred_element_type=jnp.float32).astype(jnp.bfloat16)
    send = send.reshape(experts, capacity, width)
    hidden = expert_gate.shape[2]
    gate = expert_gate.reshape(tp, width, hidden)
    up = expert_up.reshape(tp, width, hidden)
    down = expert_down.reshape(tp, hidden, width)
    gain = norm_gain.reshape(tp, 1, width)
    per_chunk = experts // CHUNKS
    rows = per_chunk * capacity
    back = []
    for c in range(CHUNKS):
        steps = range(c * per_chunk, (c + 1) * per_chunk)
        held = jnp.concatenate([exchange(send[d], "group", 2 * d) for d in steps], axis=0)
        blocks = [exchange(held, "tp", j) for j in range(tp)]
        others = [exchange(block, "group", 1) for block in blocks]
        active = vmem_call(
            functools.partial(gate_up_kernel, tp),
            jax.ShapeDtypeStruct((2 * rows, hidden), jnp.bfloat16),
            tp_scalar,
            gain,
            gate,
            up,
            *blocks,
            *others,
        )
        actives = [exchange(active, "tp", j) for j in range(tp)]
        out_type = jax.ShapeDtypeStruct((rows, width), jnp.bfloat16)
        mine, theirs = vmem_call(down_kernel, [out_type, out_type], tp_scalar, down, *actives)
        summed = mine.astype(jnp.float32) + exchange(theirs, "group", 1).astype(jnp.float32)
        summed = summed.astype(jnp.bfloat16).reshape(per_chunk, capacity, width)
        back += [exchange(summed[i], "group", 2 * d) for i, d in enumerate(steps)]
    returned = jnp.concatenate(back, axis=0)
    rows_first = (((0,), (0,)), ((), ()))
    moe_out = lax.dot_general(
        spread_high, returned, rows_first, preferred_element_type=jnp.float32
    ) + lax.dot_general(spread_low, returned, rows_first, preferred_element_type=jnp.float32)
    return (own_state + moe_out).astype(jnp.bfloat16)


def solution(mesh):
    return jax.shard_map(
        on_device,
        mesh=mesh,
        in_specs=(
            P("group", "tp"),
            P("group", "tp"),
            P("group", "tp"),
            P("group", "tp"),
            P("group", None),
            P("group"),
            P("tp"),
            P("tp", None),
            P("group", "tp"),
            P(),
            P("group", None),
            P("group", None),
            P("group", None, "tp"),
            P("group", None, "tp"),
            P("group", None, "tp"),
        ),
        out_specs=P("group", "tp"),
        check_vma=False,
    )
```

```python
import functools

import jax
import jax.numpy as jnp
from jax import lax
from jax.experimental import pallas as pl
from jax.experimental.pallas import tpu as pltpu
from jax.sharding import PartitionSpec as P

HEAD = 64
CHUNKS = 2
TILE = 256
VMEM_LIMIT = 24 * 1024 * 1024


THETA = 150000.0
ALPHA = 1.702
EPSILON = 1e-05


def exchange(value, axis, offset):
    if offset == 0:
        return value
    size = lax.axis_size(axis)
    return lax.ppermute(value, axis, [(i, i ^ offset) for i in range(size)])


NT = (((1,), (1,)), ((), ()))


def dot_nt(left, right):
    return lax.dot_general(left, right, NT, preferred_element_type=jnp.float32)


def swapped_halves(value):
    lanes = value.shape[1]
    lane = lax.broadcasted_iota(jnp.int32, value.shape, 1)
    return jnp.where(
        lane % HEAD < HEAD // 2,
        pltpu.roll(value, lanes - HEAD // 2, 1),
        pltpu.roll(value, HEAD // 2, 1),
    )


def attention_kernel(
    tp, me_ref, sink_ref, query_ref, kv_ref, local_ref, page_ref, valid_ref, cos_ref, sin_ref, weight_ref, *refs
):
    attended_ref, other_refs = refs[0], refs[1:]
    tokens = query_ref.shape[0]
    pair = 2 * HEAD
    kv_heads = kv_ref.shape[1] // pair
    group_size = query_ref.shape[1] // HEAD // kv_heads
    cosine, sine = cos_ref[...], sin_ref[...]
    low = lax.broadcasted_iota(jnp.int32, (tokens, pair), 1) < HEAD

    def rotated(value):
        return value * cosine + swapped_halves(value) * sine

    token_row = lax.broadcasted_iota(jnp.int32, (group_size * tokens, tokens), 0) % tokens
    causal = lax.broadcasted_iota(jnp.int32, (group_size * tokens, tokens), 1) <= token_row
    page_valid = valid_ref[...] > 0.0
    for h in range(kv_heads):
        lanes = slice(h * pair, (h + 1) * pair)
        own = kv_ref[:, lanes]
        own = jnp.where(low, rotated(own.astype(jnp.float32)).astype(jnp.bfloat16), own)
        queries = []
        for i in range(group_size // 2):
            start = (h * group_size + 2 * i) * HEAD
            both = rotated(query_ref[:, start : start + pair].astype(jnp.float32)) * HEAD**-0.5
            queries.append(jnp.where(low, both, 0.0))
            queries.append(jnp.where(low, pltpu.roll(both, HEAD, 1), 0.0))
        query = jnp.concatenate(queries, axis=0).astype(jnp.bfloat16)
        sink = jnp.concatenate(
            [jnp.full((tokens, 1), sink_ref[h * group_size + i]) for i in range(group_size)], axis=0
        )
        sources = [local_ref[:, lanes], page_ref[:, lanes], own]
        scores = [dot_nt(query, source) for source in sources]
        scores[1] = jnp.where(page_valid, scores[1], -jnp.inf)
        scores[2] = jnp.where(causal, scores[2], -jnp.inf)
        row_max = sink
        for score in scores:
            row_max = jnp.maximum(row_max, jnp.max(score, axis=1, keepdims=True))
        denominator = jnp.exp(sink - row_max)
        blended = None
        for score, source in zip(scores, sources):
            weights = jnp.exp(score - row_max)
            denominator = denominator + jnp.sum(weights, axis=1, keepdims=True)
            term = jnp.dot(weights.astype(jnp.bfloat16), source, preferred_element_type=jnp.float32)
            blended = term if blended is None else blended + term
        blended = blended / denominator
        for i in range(group_size // 2):
            even = blended[2 * i * tokens : (2 * i + 1) * tokens]
            odd = blended[(2 * i + 1) * tokens : (2 * i + 2) * tokens]
            start = (h * group_size + 2 * i) * HEAD
            attended_ref[:, start : start + pair] = jnp.where(
                low, pltpu.roll(even, HEAD, 1), odd
            ).astype(jnp.bfloat16)
    attended = attended_ref[...]
    for j, ref in enumerate(other_refs):
        ref[...] = dot_nt(attended, weight_ref[me_ref[0] ^ (j + 1)]).astype(jnp.bfloat16)


def own_columns_kernel(me_ref, attended_ref, weight_ref, residual_ref, out_ref):
    out_ref[...] = residual_ref[...].astype(jnp.float32) + dot_nt(attended_ref[...], weight_ref[me_ref[0]])


def gate_up_kernel(parts, me_ref, gain_ref, gate_ref, up_ref, *refs):
    out_ref, place_ref, row_ref = refs[-3:]
    rows, width = refs[0].shape
    features, hidden = gate_ref.shape[1], gate_ref.shape[0]
    me = me_ref[0]
    for s in range(len(refs[:-3]) // parts):
        held = [refs[s * parts + j][...].astype(jnp.float32) for j in range(parts)]
        square = sum(jnp.sum(h * h, axis=1, keepdims=True) for h in held)
        scale = lax.rsqrt(square / features + EPSILON)
        for j in range(parts):
            place_ref[me ^ j] = held[j] * scale
        whole = jnp.concatenate([place_ref[p] for p in range(parts)], axis=1)
        row_ref[pl.ds(s * rows, rows), :] = (whole * gain_ref[...]).astype(jnp.bfloat16)
    for start in range(0, hidden, TILE):
        tile = slice(start, min(start + TILE, hidden))
        gate_val = dot_nt(row_ref[...], gate_ref[tile])
        up_val = dot_nt(row_ref[...], up_ref[tile])
        active = gate_val * jax.nn.sigmoid(ALPHA * gate_val) * (up_val + 1.0)
        out_ref[:, tile] = active.astype(jnp.bfloat16)


def down_kernel(me_ref, down_ref, *refs):
    own_ref, other_ref = refs[-2:]
    rows, width = own_ref.shape
    me = me_ref[0]
    for start in range(0, width, TILE):
        tile = slice(start, min(start + TILE, width))
        total = None
        for j, ref in enumerate(refs[:-2]):
            term = jnp.dot(ref[...], down_ref[me ^ j, :, tile], preferred_element_type=jnp.float32)
            total = term if total is None else total + term
        own_ref[:, tile] = total[:rows].astype(jnp.bfloat16)
        other_ref[:, tile] = total[rows:].astype(jnp.bfloat16)


def vmem_call(kernel, out_types, scalars, *operands, scratch=()):
    in_vmem = pl.BlockSpec(memory_space=pltpu.VMEM)
    return pl.pallas_call(
        kernel,
        out_shape=[pltpu.VMEM(shape, dtype) for shape, dtype in out_types],
        in_specs=[pl.BlockSpec(memory_space=pltpu.SMEM)] * len(scalars) + [in_vmem] * len(operands),
        out_specs=[in_vmem] * len(out_types),
        scratch_shapes=scratch,
        compiler_params=pltpu.CompilerParams(vmem_limit_bytes=VMEM_LIMIT),
    )(*scalars, *[pltpu.with_memory_space_constraint(value, pltpu.VMEM) for value in operands])


def on_device(
    queries,
    new_kv,
    local_cache,
    remote_pool,
    page_index,
    lengths,
    sinks,
    out_weight,
    residual,
    norm_gain,
    routes,
    route_weights,
    expert_gate,
    expert_up,
    expert_down,
):
    groups = lax.axis_size("group")
    tp = lax.axis_size("tp")
    me_tp = lax.axis_index("tp")
    experts = groups // 2
    me_expert = lax.axis_index("group") // 2
    tp_scalar = me_tp.astype(jnp.int32).reshape(1)
    lane_count = remote_pool.shape[1]
    local_len = local_cache.shape[0]
    fetched = lax.all_to_all(
        remote_pool.reshape(groups, -1, lane_count),
        "group",
        split_axis=0,
        concat_axis=0,
        tiled=True,
    )
    page_len = fetched.shape[1]
    length = lengths[0]
    offsets = jnp.arange(page_len, dtype=jnp.int32)
    remote_pos = local_len + page_index[0][:, None] * page_len + offsets[None, :]
    page_valid = (remote_pos < length).astype(jnp.float32).reshape(1, -1)
    block_len, width = residual.shape
    positions = (length + jnp.arange(block_len, dtype=jnp.int32)).astype(jnp.float32)
    lane = jnp.arange(2 * HEAD, dtype=jnp.int32) % HEAD
    inverse = THETA ** (-2.0 * (lane % (HEAD // 2)).astype(jnp.float32) / HEAD)
    angles = positions[:, None] * inverse[None, :]
    sine = jnp.where(lane < HEAD // 2, -1.0, 1.0)[None, :] * jnp.sin(angles)
    weight = out_weight.T.reshape(tp, width, out_weight.shape[0])
    attended, *others = vmem_call(
        functools.partial(attention_kernel, tp),
        [(queries.shape, jnp.bfloat16)] + [(residual.shape, jnp.bfloat16)] * (tp - 1),
        [tp_scalar, sinks],
        queries,
        new_kv,
        local_cache,
        fetched.reshape(-1, lane_count),
        page_valid,
        jnp.cos(angles),
        sine,
        weight,
    )
    arriving = [exchange(other, "tp", j + 1) for j, other in enumerate(others)]
    (own_state,) = vmem_call(
        own_columns_kernel, [(residual.shape, jnp.float32)], [tp_scalar], attended, weight, residual
    )
    for term in arriving:
        own_state = own_state + term.astype(jnp.float32)
    state_sent = own_state.astype(jnp.bfloat16)

    top_count = routes.shape[1]
    capacity = 5 * block_len * top_count // (4 * experts)
    mixing = route_weights / jnp.sum(route_weights, axis=1, keepdims=True)
    chosen = (routes ^ me_expert)[:, :, None] == jnp.arange(experts, dtype=jnp.int32)
    member = jnp.any(chosen, axis=1)
    mix = jnp.sum(jnp.where(chosen, mixing[:, :, None], 0.0), axis=1)
    earlier = jnp.arange(block_len)[:, None] > jnp.arange(block_len)[None, :]
    rank = jnp.dot(
        earlier.astype(jnp.bfloat16), member.astype(jnp.bfloat16), preferred_element_type=jnp.float32
    ).astype(jnp.int32)
    hit = member.T[:, None, :] & (
        rank.T[:, None, :] == jnp.arange(capacity, dtype=jnp.int32)[None, :, None]
    )
    pick = hit.astype(jnp.bfloat16).reshape(experts * capacity, block_len)
    spread = jnp.where(hit, mix.T[:, None, :], 0.0).reshape(experts * capacity, block_len)
    spread_high = spread.astype(jnp.bfloat16)
    spread_low = (spread - spread_high.astype(jnp.float32)).astype(jnp.bfloat16)

    send = jnp.dot(pick, state_sent, preferred_element_type=jnp.float32).astype(jnp.bfloat16)
    send = send.reshape(experts, capacity, width)
    hidden = expert_gate.shape[2]
    gate, up = expert_gate[0].T, expert_up[0].T
    down = expert_down.reshape(tp, hidden, width)
    gain = norm_gain.reshape(1, tp * width)
    per_chunk = experts // CHUNKS
    rows = per_chunk * capacity
    back = []
    for c in range(CHUNKS):
        steps = range(c * per_chunk, (c + 1) * per_chunk)
        held = jnp.concatenate([exchange(send[d], "group", 2 * d) for d in steps], axis=0)
        blocks = [exchange(held, "tp", j) for j in range(tp)]
        others = [exchange(block, "group", 1) for block in blocks]
        (active,) = vmem_call(
            functools.partial(gate_up_kernel, tp),
            [((2 * rows, hidden), jnp.bfloat16)],
            [tp_scalar],
            gain,
            gate,
            up,
            *blocks,
            *others,
            scratch=[
                pltpu.VMEM((tp, rows, width), jnp.float32),
                pltpu.VMEM((2 * rows, tp * width), jnp.bfloat16),
            ],
        )
        actives = [exchange(active, "tp", j) for j in range(tp)]
        mine, theirs = vmem_call(
            down_kernel, [((rows, width), jnp.bfloat16)] * 2, [tp_scalar], down, *actives
        )
        summed = mine.astype(jnp.float32) + exchange(theirs, "group", 1).astype(jnp.float32)
        summed = summed.astype(jnp.bfloat16).reshape(per_chunk, capacity, width)
        back += [exchange(summed[i], "group", 2 * d) for i, d in enumerate(steps)]
    returned = jnp.concatenate(back, axis=0)
    rows_first = (((0,), (0,)), ((), ()))
    moe_out = lax.dot_general(
        spread_high, returned, rows_first, preferred_element_type=jnp.float32
    ) + lax.dot_general(spread_low, returned, rows_first, preferred_element_type=jnp.float32)
    return (own_state + moe_out).astype(jnp.bfloat16)


def solution(mesh):
    return jax.shard_map(
        on_device,
        mesh=mesh,
        in_specs=(
            P("group", "tp"),
            P("group", "tp"),
            P("group", "tp"),
            P("group", "tp"),
            P("group", None),
            P("group"),
            P("tp"),
            P("tp", None),
            P("group", "tp"),
            P(),
            P("group", None),
            P("group", None),
            P("group", None, "tp"),
            P("group", None, "tp"),
            P("group", None, "tp"),
        ),
        out_specs=P("group", "tp"),
        check_vma=False,
    )
```

```python
import functools

import jax
import jax.numpy as jnp
from jax import lax
from jax.experimental import pallas as pl
from jax.experimental.pallas import tpu as pltpu
from jax.sharding import PartitionSpec as P

HEAD = 64
CHUNKS = 4
TILE = 256
VMEM_LIMIT = 24 * 1024 * 1024


THETA = 150000.0
ALPHA = 1.702
EPSILON = 1e-05


def exchange(value, axis, offset):
    if offset == 0:
        return value
    size = lax.axis_size(axis)
    return lax.ppermute(value, axis, [(i, i ^ offset) for i in range(size)])


NT = (((1,), (1,)), ((), ()))


def dot_nt(left, right):
    return lax.dot_general(left, right, NT, preferred_element_type=jnp.float32)


def swapped_halves(value):
    lanes = value.shape[1]
    lane = lax.broadcasted_iota(jnp.int32, value.shape, 1)
    return jnp.where(
        lane % HEAD < HEAD // 2,
        pltpu.roll(value, lanes - HEAD // 2, 1),
        pltpu.roll(value, HEAD // 2, 1),
    )


def attention_kernel(
    tp, me_ref, sink_ref, query_ref, kv_ref, local_ref, page_ref, valid_ref, cos_ref, sin_ref, weight_ref, *refs
):
    attended_ref, other_refs = refs[0], refs[1:]
    tokens = query_ref.shape[0]
    pair = 2 * HEAD
    kv_heads = kv_ref.shape[1] // pair
    group_size = query_ref.shape[1] // HEAD // kv_heads
    cosine, sine = cos_ref[...], sin_ref[...]
    low = lax.broadcasted_iota(jnp.int32, (tokens, pair), 1) < HEAD

    def rotated(value):
        return value * cosine + swapped_halves(value) * sine

    token_row = lax.broadcasted_iota(jnp.int32, (group_size * tokens, tokens), 0) % tokens
    causal = lax.broadcasted_iota(jnp.int32, (group_size * tokens, tokens), 1) <= token_row
    page_valid = valid_ref[...] > 0.0
    for h in range(kv_heads):
        lanes = slice(h * pair, (h + 1) * pair)
        own = kv_ref[:, lanes]
        own = jnp.where(low, rotated(own.astype(jnp.float32)).astype(jnp.bfloat16), own)
        queries = []
        for i in range(group_size // 2):
            start = (h * group_size + 2 * i) * HEAD
            both = rotated(query_ref[:, start : start + pair].astype(jnp.float32)) * HEAD**-0.5
            queries.append(jnp.where(low, both, 0.0))
            queries.append(jnp.where(low, pltpu.roll(both, HEAD, 1), 0.0))
        query = jnp.concatenate(queries, axis=0).astype(jnp.bfloat16)
        sink = jnp.concatenate(
            [jnp.full((tokens, 1), sink_ref[h * group_size + i]) for i in range(group_size)], axis=0
        )
        sources = [local_ref[:, lanes], page_ref[:, lanes], own]
        scores = [dot_nt(query, source) for source in sources]
        scores[1] = jnp.where(page_valid, scores[1], -jnp.inf)
        scores[2] = jnp.where(causal, scores[2], -jnp.inf)
        row_max = sink
        for score in scores:
            row_max = jnp.maximum(row_max, jnp.max(score, axis=1, keepdims=True))
        denominator = jnp.exp(sink - row_max)
        blended = None
        for score, source in zip(scores, sources):
            weights = jnp.exp(score - row_max)
            denominator = denominator + jnp.sum(weights, axis=1, keepdims=True)
            term = jnp.dot(weights.astype(jnp.bfloat16), source, preferred_element_type=jnp.float32)
            blended = term if blended is None else blended + term
        blended = blended / denominator
        for i in range(group_size // 2):
            even = blended[2 * i * tokens : (2 * i + 1) * tokens]
            odd = blended[(2 * i + 1) * tokens : (2 * i + 2) * tokens]
            start = (h * group_size + 2 * i) * HEAD
            attended_ref[:, start : start + pair] = jnp.where(
                low, pltpu.roll(even, HEAD, 1), odd
            ).astype(jnp.bfloat16)
    attended = attended_ref[...]
    for j, ref in enumerate(other_refs):
        ref[...] = dot_nt(attended, weight_ref[me_ref[0] ^ (j + 1)]).astype(jnp.bfloat16)


def own_columns_kernel(me_ref, attended_ref, weight_ref, residual_ref, out_ref):
    out_ref[...] = residual_ref[...].astype(jnp.float32) + dot_nt(attended_ref[...], weight_ref[me_ref[0]])


def gate_up_kernel(parts, me_ref, gain_ref, gate_ref, up_ref, *refs):
    out_ref, place_ref, row_ref = refs[-3:]
    rows, width = refs[0].shape
    features, hidden = gate_ref.shape[1], gate_ref.shape[0]
    me = me_ref[0]
    for s in range(len(refs[:-3]) // parts):
        held = [refs[s * parts + j][...].astype(jnp.float32) for j in range(parts)]
        square = sum(jnp.sum(h * h, axis=1, keepdims=True) for h in held)
        scale = lax.rsqrt(square / features + EPSILON)
        for j in range(parts):
            place_ref[me ^ j] = held[j] * scale
        whole = jnp.concatenate([place_ref[p] for p in range(parts)], axis=1)
        row_ref[pl.ds(s * rows, rows), :] = (whole * gain_ref[...]).astype(jnp.bfloat16)
    for start in range(0, hidden, TILE):
        tile = slice(start, min(start + TILE, hidden))
        gate_val = dot_nt(row_ref[...], gate_ref[tile])
        up_val = dot_nt(row_ref[...], up_ref[tile])
        active = gate_val * jax.nn.sigmoid(ALPHA * gate_val) * (up_val + 1.0)
        out_ref[:, tile] = active.astype(jnp.bfloat16)


def down_kernel(me_ref, down_ref, *refs):
    own_ref, other_ref = refs[-2:]
    rows, width = own_ref.shape
    me = me_ref[0]
    for start in range(0, width, TILE):
        tile = slice(start, min(start + TILE, width))
        total = None
        for j, ref in enumerate(refs[:-2]):
            term = jnp.dot(ref[...], down_ref[me ^ j, :, tile], preferred_element_type=jnp.float32)
            total = term if total is None else total + term
        own_ref[:, tile] = total[:rows].astype(jnp.bfloat16)
        other_ref[:, tile] = total[rows:].astype(jnp.bfloat16)


def vmem_call(kernel, out_types, scalars, *operands, scratch=()):
    in_vmem = pl.BlockSpec(memory_space=pltpu.VMEM)
    return pl.pallas_call(
        kernel,
        out_shape=[pltpu.VMEM(shape, dtype) for shape, dtype in out_types],
        in_specs=[pl.BlockSpec(memory_space=pltpu.SMEM)] * len(scalars) + [in_vmem] * len(operands),
        out_specs=[in_vmem] * len(out_types),
        scratch_shapes=scratch,
        compiler_params=pltpu.CompilerParams(vmem_limit_bytes=VMEM_LIMIT),
    )(*scalars, *[pltpu.with_memory_space_constraint(value, pltpu.VMEM) for value in operands])


def on_device(
    queries,
    new_kv,
    local_cache,
    remote_pool,
    page_index,
    lengths,
    sinks,
    out_weight,
    residual,
    norm_gain,
    routes,
    route_weights,
    expert_gate,
    expert_up,
    expert_down,
):
    groups = lax.axis_size("group")
    tp = lax.axis_size("tp")
    me_tp = lax.axis_index("tp")
    experts = groups // 2
    me_expert = lax.axis_index("group") // 2
    tp_scalar = me_tp.astype(jnp.int32).reshape(1)
    lane_count = remote_pool.shape[1]
    local_len = local_cache.shape[0]
    fetched = lax.all_to_all(
        remote_pool.reshape(groups, -1, lane_count),
        "group",
        split_axis=0,
        concat_axis=0,
        tiled=True,
    )
    page_len = fetched.shape[1]
    length = lengths[0]
    offsets = jnp.arange(page_len, dtype=jnp.int32)
    remote_pos = local_len + page_index[0][:, None] * page_len + offsets[None, :]
    page_valid = (remote_pos < length).astype(jnp.float32).reshape(1, -1)
    block_len, width = residual.shape
    positions = (length + jnp.arange(block_len, dtype=jnp.int32)).astype(jnp.float32)
    lane = jnp.arange(2 * HEAD, dtype=jnp.int32) % HEAD
    inverse = THETA ** (-2.0 * (lane % (HEAD // 2)).astype(jnp.float32) / HEAD)
    angles = positions[:, None] * inverse[None, :]
    sine = jnp.where(lane < HEAD // 2, -1.0, 1.0)[None, :] * jnp.sin(angles)
    weight = out_weight.T.reshape(tp, width, out_weight.shape[0])
    attended, *others = vmem_call(
        functools.partial(attention_kernel, tp),
        [(queries.shape, jnp.bfloat16)] + [(residual.shape, jnp.bfloat16)] * (tp - 1),
        [tp_scalar, sinks],
        queries,
        new_kv,
        local_cache,
        fetched.reshape(-1, lane_count),
        page_valid,
        jnp.cos(angles),
        sine,
        weight,
    )
    arriving = [exchange(other, "tp", j + 1) for j, other in enumerate(others)]
    (own_state,) = vmem_call(
        own_columns_kernel, [(residual.shape, jnp.float32)], [tp_scalar], attended, weight, residual
    )
    for term in arriving:
        own_state = own_state + term.astype(jnp.float32)
    state_sent = own_state.astype(jnp.bfloat16)

    top_count = routes.shape[1]
    capacity = 5 * block_len * top_count // (4 * experts)
    mixing = route_weights / jnp.sum(route_weights, axis=1, keepdims=True)
    chosen = (routes ^ me_expert)[:, :, None] == jnp.arange(experts, dtype=jnp.int32)
    member = jnp.any(chosen, axis=1)
    mix = jnp.sum(jnp.where(chosen, mixing[:, :, None], 0.0), axis=1)
    earlier = jnp.arange(block_len)[:, None] > jnp.arange(block_len)[None, :]
    rank = jnp.dot(
        earlier.astype(jnp.bfloat16), member.astype(jnp.bfloat16), preferred_element_type=jnp.float32
    ).astype(jnp.int32)
    hit = member.T[:, None, :] & (
        rank.T[:, None, :] == jnp.arange(capacity, dtype=jnp.int32)[None, :, None]
    )
    pick = hit.astype(jnp.bfloat16).reshape(experts * capacity, block_len)
    spread = jnp.where(hit, mix.T[:, None, :], 0.0).reshape(experts * capacity, block_len)
    spread_high = spread.astype(jnp.bfloat16)
    spread_low = (spread - spread_high.astype(jnp.float32)).astype(jnp.bfloat16)

    send = jnp.dot(pick, state_sent, preferred_element_type=jnp.float32).astype(jnp.bfloat16)
    send = send.reshape(experts, capacity, width)
    hidden = expert_gate.shape[2]
    gate, up = expert_gate[0].T, expert_up[0].T
    down = expert_down.reshape(tp, hidden, width)
    gain = norm_gain.reshape(1, tp * width)
    half = experts // 2
    chunk_count = min(CHUNKS, half)
    chunks = [
        [d for d in range(experts) if d % half * chunk_count // half == c] for c in range(chunk_count)
    ]

    def gather_rows(steps):
        return jnp.concatenate([exchange(send[d], "group", 2 * d) for d in steps], axis=0)

    def whole_rows(held):
        blocks = [exchange(held, "tp", j) for j in range(tp)]
        return blocks, [exchange(block, "group", 1) for block in blocks]

    def activate(blocks, others):
        rows = blocks[0].shape[0]
        (active,) = vmem_call(
            functools.partial(gate_up_kernel, tp),
            [((2 * rows, hidden), jnp.bfloat16)],
            [tp_scalar],
            gain,
            gate,
            up,
            *blocks,
            *others,
            scratch=[
                pltpu.VMEM((tp, rows, width), jnp.float32),
                pltpu.VMEM((2 * rows, tp * width), jnp.bfloat16),
            ],
        )
        return active

    def project_down(actives):
        rows = actives[0].shape[0] // 2
        return vmem_call(
            down_kernel, [((rows, width), jnp.bfloat16)] * 2, [tp_scalar], down, *actives
        )

    def send_back(steps, mine, theirs):
        summed = mine.astype(jnp.float32) + exchange(theirs, "group", 1).astype(jnp.float32)
        summed = summed.astype(jnp.bfloat16).reshape(len(steps), capacity, width)
        return [exchange(summed[i], "group", 2 * d) for i, d in enumerate(steps)]

    def after(value, *earlier):
        return lax.optimization_barrier((value, *earlier))[0]

    rows_of, actives_of, back = {}, {}, {}
    last = None

    def ordered(values):
        return values if last is None else [after(values[0], last), *values[1:]]

    for i in range(chunk_count + 2):
        if i < chunk_count:
            held = gather_rows(chunks[i])
            rows_of[i] = whole_rows(held if last is None else after(held, last))
        if 0 <= i - 1 < chunk_count:
            blocks, others = rows_of[i - 1]
            last = activate(ordered(blocks), others)
            actives_of[i - 1] = [exchange(last, "tp", j) for j in range(tp)]
        if 0 <= i - 2 < chunk_count:
            mine, theirs = project_down(ordered(actives_of[i - 2]))
            last = mine
            for d, rows in zip(chunks[i - 2], send_back(chunks[i - 2], mine, theirs)):
                back[d] = rows
    back = [back[d] for d in range(experts)]
    returned = jnp.concatenate(back, axis=0)
    rows_first = (((0,), (0,)), ((), ()))
    moe_out = lax.dot_general(
        spread_high, returned, rows_first, preferred_element_type=jnp.float32
    ) + lax.dot_general(spread_low, returned, rows_first, preferred_element_type=jnp.float32)
    return (own_state + moe_out).astype(jnp.bfloat16)


def solution(mesh):
    return jax.shard_map(
        on_device,
        mesh=mesh,
        in_specs=(
            P("group", "tp"),
            P("group", "tp"),
            P("group", "tp"),
            P("group", "tp"),
            P("group", None),
            P("group"),
            P("tp"),
            P("tp", None),
            P("group", "tp"),
            P(),
            P("group", None),
            P("group", None),
            P("group", None, "tp"),
            P("group", None, "tp"),
            P("group", None, "tp"),
        ),
        out_specs=P("group", "tp"),
        check_vma=False,
    )
```

```python
import functools

import jax
import jax.numpy as jnp
from jax import lax
from jax.experimental import pallas as pl
from jax.experimental.pallas import tpu as pltpu
from jax.sharding import PartitionSpec as P

HEAD = 64
TILE = 256
VMEM_LIMIT = 24 * 1024 * 1024


THETA = 150000.0
ALPHA = 1.702
EPSILON = 1e-05


def exchange(value, axis, offset):
    if offset == 0:
        return value
    size = lax.axis_size(axis)
    return lax.ppermute(value, axis, [(i, i ^ offset) for i in range(size)])


NT = (((1,), (1,)), ((), ()))


def dot_nt(left, right):
    return lax.dot_general(left, right, NT, preferred_element_type=jnp.float32)


def swapped_halves(value):
    lanes = value.shape[1]
    lane = lax.broadcasted_iota(jnp.int32, value.shape, 1)
    return jnp.where(
        lane % HEAD < HEAD // 2,
        pltpu.roll(value, lanes - HEAD // 2, 1),
        pltpu.roll(value, HEAD // 2, 1),
    )


def local_kernel(loads, sink_ref, query_ref, kv_ref, local_ref, cos_ref, sin_ref, *refs):
    sources, (rotated_ref, state_ref), targets = refs[:loads], refs[loads : loads + 2], refs[loads + 2 : -1]
    copies = [
        pltpu.make_async_copy(source, target, refs[-1].at[i])
        for i, (source, target) in enumerate(zip(sources, targets))
    ]
    for copy in copies:
        copy.start()
    tokens = query_ref.shape[0]
    pair = 2 * HEAD
    kv_heads = kv_ref.shape[1] // pair
    group_size = query_ref.shape[1] // HEAD // kv_heads
    rows = group_size * tokens
    cosine, sine = cos_ref[...], sin_ref[...]
    low = lax.broadcasted_iota(jnp.int32, (tokens, pair), 1) < HEAD
    lane = lax.broadcasted_iota(jnp.int32, (rows, pair), 1)

    def rotated(value):
        return value * cosine + swapped_halves(value) * sine

    token_row = lax.broadcasted_iota(jnp.int32, (rows, tokens), 0) % tokens
    causal = lax.broadcasted_iota(jnp.int32, (rows, tokens), 1) <= token_row
    for h in range(kv_heads):
        lanes = slice(h * pair, (h + 1) * pair)
        own = kv_ref[:, lanes]
        own = jnp.where(low, rotated(own.astype(jnp.float32)).astype(jnp.bfloat16), own)
        queries = []
        for i in range(group_size // 2):
            start = (h * group_size + 2 * i) * HEAD
            both = rotated(query_ref[:, start : start + pair].astype(jnp.float32)) * HEAD**-0.5
            queries.append(jnp.where(low, both, 0.0))
            queries.append(jnp.where(low, pltpu.roll(both, HEAD, 1), 0.0))
        query = jnp.concatenate(queries, axis=0).astype(jnp.bfloat16)
        sink = jnp.concatenate(
            [jnp.full((tokens, 1), sink_ref[h * group_size + i]) for i in range(group_size)], axis=0
        )
        sources = [local_ref[:, lanes], own]
        scores = [dot_nt(query, source) for source in sources]
        scores[1] = jnp.where(causal, scores[1], -jnp.inf)
        row_max = sink
        for score in scores:
            row_max = jnp.maximum(row_max, jnp.max(score, axis=1, keepdims=True))
        denominator = jnp.exp(sink - row_max)
        blended = None
        for score, source in zip(scores, sources):
            weights = jnp.exp(score - row_max)
            denominator = denominator + jnp.sum(weights, axis=1, keepdims=True)
            term = jnp.dot(weights.astype(jnp.bfloat16), source, preferred_element_type=jnp.float32)
            blended = term if blended is None else blended + term
        place = slice(h * rows, (h + 1) * rows)
        rotated_ref[place, :] = query
        state_ref[place, :] = jnp.where(lane == 0, row_max, jnp.where(lane == 1, denominator, blended))
    for copy in copies:
        copy.wait()


def page_kernel(me_ref, rotated_ref, state_ref, page_ref, valid_ref, weight_ref, attended_ref, *other_refs):
    tokens = attended_ref.shape[0]
    pair = 2 * HEAD
    kv_heads = page_ref.shape[1] // pair
    rows = rotated_ref.shape[0] // kv_heads
    group_size = rows // tokens
    low = lax.broadcasted_iota(jnp.int32, (tokens, pair), 1) < HEAD
    page_valid = valid_ref[...] > 0.0
    for h in range(kv_heads):
        place = slice(h * rows, (h + 1) * rows)
        source = page_ref[:, h * pair : (h + 1) * pair]
        state = state_ref[place, :]
        score = jnp.where(page_valid, dot_nt(rotated_ref[place, :], source), -jnp.inf)
        row_max = jnp.maximum(state[:, 0:1], jnp.max(score, axis=1, keepdims=True))
        weights = jnp.exp(score - row_max)
        kept = jnp.exp(state[:, 0:1] - row_max)
        denominator = state[:, 1:2] * kept + jnp.sum(weights, axis=1, keepdims=True)
        term = jnp.dot(weights.astype(jnp.bfloat16), source, preferred_element_type=jnp.float32)
        blended = (state * kept + term) / denominator
        for i in range(group_size // 2):
            even = blended[2 * i * tokens : (2 * i + 1) * tokens]
            odd = blended[(2 * i + 1) * tokens : (2 * i + 2) * tokens]
            start = (h * group_size + 2 * i) * HEAD
            attended_ref[:, start : start + pair] = jnp.where(
                low, pltpu.roll(even, HEAD, 1), odd
            ).astype(jnp.bfloat16)
    attended = attended_ref[...]
    for j, ref in enumerate(other_refs):
        ref[...] = dot_nt(attended, weight_ref[me_ref[0] ^ (j + 1)]).astype(jnp.bfloat16)


def own_columns_kernel(me_ref, attended_ref, weight_ref, residual_ref, out_ref):
    out_ref[...] = residual_ref[...].astype(jnp.float32) + dot_nt(attended_ref[...], weight_ref[me_ref[0]])


def gate_up_kernel(parts, me_ref, gain_ref, gate_ref, up_ref, *refs):
    out_ref, place_ref, row_ref = refs[-3:]
    rows, width = refs[0].shape
    features, hidden = gate_ref.shape[1], gate_ref.shape[0]
    me = me_ref[0]
    for s in range(len(refs[:-3]) // parts):
        held = [refs[s * parts + j][...].astype(jnp.float32) for j in range(parts)]
        square = sum(jnp.sum(h * h, axis=1, keepdims=True) for h in held)
        scale = lax.rsqrt(square / features + EPSILON)
        for j in range(parts):
            place_ref[me ^ j] = held[j] * scale
        whole = jnp.concatenate([place_ref[p] for p in range(parts)], axis=1)
        row_ref[pl.ds(s * rows, rows), :] = (whole * gain_ref[...]).astype(jnp.bfloat16)
    for start in range(0, hidden, TILE):
        tile = slice(start, min(start + TILE, hidden))
        gate_val = dot_nt(row_ref[...], gate_ref[tile])
        up_val = dot_nt(row_ref[...], up_ref[tile])
        active = gate_val * jax.nn.sigmoid(ALPHA * gate_val) * (up_val + 1.0)
        out_ref[:, tile] = active.astype(jnp.bfloat16)


def down_kernel(me_ref, down_ref, *refs):
    own_ref, other_ref = refs[-2:]
    rows, width = own_ref.shape
    me = me_ref[0]
    for start in range(0, width, TILE):
        tile = slice(start, min(start + TILE, width))
        total = None
        for j, ref in enumerate(refs[:-2]):
            term = jnp.dot(ref[...], down_ref[me ^ j, :, tile], preferred_element_type=jnp.float32)
            total = term if total is None else total + term
        own_ref[:, tile] = total[:rows].astype(jnp.bfloat16)
        other_ref[:, tile] = total[rows:].astype(jnp.bfloat16)


def vmem_call(kernel, out_types, scalars, *operands, scratch=()):
    in_vmem = pl.BlockSpec(memory_space=pltpu.VMEM)
    return pl.pallas_call(
        kernel,
        out_shape=[pltpu.VMEM(shape, dtype) for shape, dtype in out_types],
        in_specs=[pl.BlockSpec(memory_space=pltpu.SMEM)] * len(scalars) + [in_vmem] * len(operands),
        out_specs=[in_vmem] * len(out_types),
        scratch_shapes=scratch,
        compiler_params=pltpu.CompilerParams(vmem_limit_bytes=VMEM_LIMIT),
    )(*scalars, *[pltpu.with_memory_space_constraint(value, pltpu.VMEM) for value in operands])


def on_device(
    queries,
    new_kv,
    local_cache,
    remote_pool,
    page_index,
    lengths,
    sinks,
    out_weight,
    residual,
    norm_gain,
    routes,
    route_weights,
    expert_gate,
    expert_up,
    expert_down,
):
    groups = lax.axis_size("group")
    tp = lax.axis_size("tp")
    me_tp = lax.axis_index("tp")
    experts = groups // 2
    me_expert = lax.axis_index("group") // 2
    tp_scalar = me_tp.astype(jnp.int32).reshape(1)
    lane_count = remote_pool.shape[1]
    local_len = local_cache.shape[0]
    fetched = lax.all_to_all(
        remote_pool.reshape(groups, -1, lane_count),
        "group",
        split_axis=0,
        concat_axis=0,
        tiled=True,
    )
    page_len = fetched.shape[1]
    length = lengths[0]
    offsets = jnp.arange(page_len, dtype=jnp.int32)
    remote_pos = local_len + page_index[0][:, None] * page_len + offsets[None, :]
    page_valid = (remote_pos < length).astype(jnp.float32).reshape(1, -1)
    block_len, width = residual.shape
    positions = (length + jnp.arange(block_len, dtype=jnp.int32)).astype(jnp.float32)
    lane = jnp.arange(2 * HEAD, dtype=jnp.int32) % HEAD
    inverse = THETA ** (-2.0 * (lane % (HEAD // 2)).astype(jnp.float32) / HEAD)
    angles = positions[:, None] * inverse[None, :]
    sine = jnp.where(lane < HEAD // 2, -1.0, 1.0)[None, :] * jnp.sin(angles)
    hidden = expert_gate.shape[2]
    to_load = [
        out_weight.T.reshape(tp, width, out_weight.shape[0]),
        residual,
        norm_gain.reshape(1, tp * width),
        expert_gate[0].T,
        expert_up[0].T,
        expert_down.reshape(tp, hidden, width),
    ]
    in_vmem = pl.BlockSpec(memory_space=pltpu.VMEM)
    states = block_len * queries.shape[1] // HEAD
    rotated, state, weight, residual, gain, gate, up, down = pl.pallas_call(
        functools.partial(local_kernel, len(to_load)),
        out_shape=[
            pltpu.VMEM((states, 2 * HEAD), jnp.bfloat16),
            pltpu.VMEM((states, 2 * HEAD), jnp.float32),
        ]
        + [pltpu.VMEM(value.shape, value.dtype) for value in to_load],
        in_specs=[pl.BlockSpec(memory_space=pltpu.SMEM)]
        + [in_vmem] * 5
        + [pl.BlockSpec(memory_space=pltpu.HBM)] * len(to_load),
        out_specs=[in_vmem] * (2 + len(to_load)),
        scratch_shapes=[pltpu.SemaphoreType.DMA((len(to_load),))],
        compiler_params=pltpu.CompilerParams(vmem_limit_bytes=VMEM_LIMIT),
    )(
        sinks,
        *[pltpu.with_memory_space_constraint(value, pltpu.HBM) for value in (queries, new_kv, local_cache)],
        *[pltpu.with_memory_space_constraint(value, pltpu.VMEM) for value in (jnp.cos(angles), sine)],
        *[pltpu.with_memory_space_constraint(value, pltpu.HBM) for value in to_load],
    )
    attended, *others = vmem_call(
        page_kernel,
        [(queries.shape, jnp.bfloat16)] + [(residual.shape, jnp.bfloat16)] * (tp - 1),
        [tp_scalar],
        rotated,
        state,
        fetched.reshape(-1, lane_count),
        page_valid,
        weight,
    )
    arriving = [exchange(other, "tp", j + 1) for j, other in enumerate(others)]
    (own_state,) = vmem_call(
        own_columns_kernel, [(residual.shape, jnp.float32)], [tp_scalar], attended, weight, residual
    )
    for term in arriving:
        own_state = own_state + term.astype(jnp.float32)
    state_sent = own_state.astype(jnp.bfloat16)

    top_count = routes.shape[1]
    capacity = 5 * block_len * top_count // (4 * experts)
    mixing = route_weights / jnp.sum(route_weights, axis=1, keepdims=True)
    chosen = (routes ^ me_expert)[:, :, None] == jnp.arange(experts, dtype=jnp.int32)
    member = jnp.any(chosen, axis=1)
    mix = jnp.sum(jnp.where(chosen, mixing[:, :, None], 0.0), axis=1)
    earlier = jnp.arange(block_len)[:, None] > jnp.arange(block_len)[None, :]
    rank = jnp.dot(
        earlier.astype(jnp.bfloat16), member.astype(jnp.bfloat16), preferred_element_type=jnp.float32
    ).astype(jnp.int32)
    hit = member.T[:, None, :] & (
        rank.T[:, None, :] == jnp.arange(capacity, dtype=jnp.int32)[None, :, None]
    )
    pick = hit.astype(jnp.bfloat16)
    spread = jnp.where(hit, mix.T[:, None, :], 0.0).reshape(experts * capacity, block_len)
    spread_high = spread.astype(jnp.bfloat16)
    spread_low = (spread - spread_high.astype(jnp.float32)).astype(jnp.bfloat16)

    half, quarter = experts // 2, experts // 4
    chunks = [range(half), range(half, half + quarter), range(half + quarter, experts)]

    def gather_rows(steps, sent):
        chosen_rows = pick[steps[0] : steps[-1] + 1].reshape(len(steps) * capacity, block_len)
        send = jnp.dot(chosen_rows, sent, preferred_element_type=jnp.float32).astype(jnp.bfloat16)
        send = send.reshape(len(steps), capacity, width)
        return jnp.concatenate([exchange(send[i], "group", 2 * d) for i, d in enumerate(steps)], axis=0)

    def whole_rows(held):
        blocks = [exchange(held, "tp", j) for j in range(tp)]
        return blocks, [exchange(block, "group", 1) for block in blocks]

    def activate(blocks, others):
        rows = blocks[0].shape[0]
        (active,) = vmem_call(
            functools.partial(gate_up_kernel, tp),
            [((2 * rows, hidden), jnp.bfloat16)],
            [tp_scalar],
            gain,
            gate,
            up,
            *blocks,
            *others,
            scratch=[
                pltpu.VMEM((tp, rows, width), jnp.float32),
                pltpu.VMEM((2 * rows, tp * width), jnp.bfloat16),
            ],
        )
        return active

    def project_down(actives):
        rows = actives[0].shape[0] // 2
        return vmem_call(
            down_kernel, [((rows, width), jnp.bfloat16)] * 2, [tp_scalar], down, *actives
        )

    def send_back(steps, mine, theirs):
        summed = mine.astype(jnp.float32) + exchange(theirs, "group", 1).astype(jnp.float32)
        summed = summed.astype(jnp.bfloat16).reshape(len(steps), capacity, width)
        return [exchange(summed[i], "group", 2 * d) for i, d in enumerate(steps)]

    def after(value, *earlier):
        return lax.optimization_barrier((value, *earlier))[0]

    near, first, second = chunks
    near_held = gather_rows(near, state_sent)
    near_rows = whole_rows(near_held)
    first_rows = whole_rows(gather_rows(first, state_sent))
    near_active = activate(*near_rows)
    second_rows = whole_rows(after(gather_rows(second, after(state_sent, near_held)), near_active))
    near_actives = [exchange(near_active, "tp", j) for j in range(tp)]
    first_active = activate(*first_rows)
    first_actives = [exchange(first_active, "tp", j) for j in range(tp)]
    second_active = activate(*second_rows)
    second_actives = [exchange(second_active, "tp", j) for j in range(tp)]
    first_actives[0] = after(first_actives[0], second_active)
    first_out = project_down(first_actives)
    first_back = send_back(first, *first_out)
    near_actives[0] = after(near_actives[0], first_out[0])
    near_out = project_down(near_actives)
    near_back = send_back(near, *near_out)
    second_out = project_down(second_actives)
    second_back = send_back(second, *second_out)
    back = near_back + first_back + second_back
    returned = jnp.concatenate(back, axis=0)
    rows_first = (((0,), (0,)), ((), ()))
    moe_out = lax.dot_general(
        spread_high, returned, rows_first, preferred_element_type=jnp.float32
    ) + lax.dot_general(spread_low, returned, rows_first, preferred_element_type=jnp.float32)
    return (own_state + moe_out).astype(jnp.bfloat16)


def solution(mesh):
    return jax.shard_map(
        on_device,
        mesh=mesh,
        in_specs=(
            P("group", "tp"),
            P("group", "tp"),
            P("group", "tp"),
            P("group", "tp"),
            P("group", None),
            P("group"),
            P("tp"),
            P("tp", None),
            P("group", "tp"),
            P(),
            P("group", None),
            P("group", None),
            P("group", None, "tp"),
            P("group", None, "tp"),
            P("group", None, "tp"),
        ),
        out_specs=P("group", "tp"),
        check_vma=False,
    )
```

```python
import functools

import jax
import jax.numpy as jnp
from jax import lax
from jax.experimental import pallas as pl
from jax.experimental.pallas import tpu as pltpu
from jax.sharding import PartitionSpec as P

HEAD = 64
TILE = 256
VMEM_LIMIT = 24 * 1024 * 1024


THETA = 150000.0
ALPHA = 1.702
EPSILON = 1e-05


def exchange(value, axis, offset):
    if offset == 0:
        return value
    size = lax.axis_size(axis)
    return lax.ppermute(value, axis, [(i, i ^ offset) for i in range(size)])


NT = (((1,), (1,)), ((), ()))


def dot_nt(left, right):
    return lax.dot_general(left, right, NT, preferred_element_type=jnp.float32)


def swapped_halves(value):
    lanes = value.shape[1]
    lane = lax.broadcasted_iota(jnp.int32, value.shape, 1)
    return jnp.where(
        lane % HEAD < HEAD // 2,
        pltpu.roll(value, lanes - HEAD // 2, 1),
        pltpu.roll(value, HEAD // 2, 1),
    )


def local_kernel(sink_ref, query_ref, kv_ref, local_ref, cos_ref, sin_ref, rotated_ref, state_ref):
    tokens = query_ref.shape[0]
    pair = 2 * HEAD
    kv_heads = kv_ref.shape[1] // pair
    group_size = query_ref.shape[1] // HEAD // kv_heads
    rows = group_size * tokens
    cosine, sine = cos_ref[...], sin_ref[...]
    low = lax.broadcasted_iota(jnp.int32, (tokens, pair), 1) < HEAD
    lane = lax.broadcasted_iota(jnp.int32, (rows, pair), 1)

    def rotated(value):
        return value * cosine + swapped_halves(value) * sine

    token_row = lax.broadcasted_iota(jnp.int32, (rows, tokens), 0) % tokens
    causal = lax.broadcasted_iota(jnp.int32, (rows, tokens), 1) <= token_row
    for h in range(kv_heads):
        lanes = slice(h * pair, (h + 1) * pair)
        own = kv_ref[:, lanes]
        own = jnp.where(low, rotated(own.astype(jnp.float32)).astype(jnp.bfloat16), own)
        queries = []
        for i in range(group_size // 2):
            start = (h * group_size + 2 * i) * HEAD
            both = rotated(query_ref[:, start : start + pair].astype(jnp.float32)) * HEAD**-0.5
            queries.append(jnp.where(low, both, 0.0))
            queries.append(jnp.where(low, pltpu.roll(both, HEAD, 1), 0.0))
        query = jnp.concatenate(queries, axis=0).astype(jnp.bfloat16)
        sink = jnp.concatenate(
            [jnp.full((tokens, 1), sink_ref[h * group_size + i]) for i in range(group_size)], axis=0
        )
        sources = [local_ref[:, lanes], own]
        scores = [dot_nt(query, source) for source in sources]
        scores[1] = jnp.where(causal, scores[1], -jnp.inf)
        row_max = sink
        for score in scores:
            row_max = jnp.maximum(row_max, jnp.max(score, axis=1, keepdims=True))
        denominator = jnp.exp(sink - row_max)
        blended = None
        for score, source in zip(scores, sources):
            weights = jnp.exp(score - row_max)
            denominator = denominator + jnp.sum(weights, axis=1, keepdims=True)
            term = jnp.dot(weights.astype(jnp.bfloat16), source, preferred_element_type=jnp.float32)
            blended = term if blended is None else blended + term
        place = slice(h * rows, (h + 1) * rows)
        rotated_ref[place, :] = query
        state_ref[place, :] = jnp.where(lane == 0, row_max, jnp.where(lane == 1, denominator, blended))


def page_kernel(me_ref, weight_ref, rotated_ref, state_ref, page_ref, valid_ref, attended_ref, *refs):
    other_refs, held_ref, sems = refs[:-2], refs[-2], refs[-1]
    copies = [
        pltpu.make_async_copy(weight_ref.at[me_ref[0] ^ (j + 1)], held_ref.at[j], sems.at[j])
        for j in range(len(other_refs))
    ]
    for copy in copies:
        copy.start()
    tokens = attended_ref.shape[0]
    pair = 2 * HEAD
    kv_heads = page_ref.shape[1] // pair
    rows = rotated_ref.shape[0] // kv_heads
    group_size = rows // tokens
    low = lax.broadcasted_iota(jnp.int32, (tokens, pair), 1) < HEAD
    page_valid = valid_ref[...] > 0.0
    for h in range(kv_heads):
        place = slice(h * rows, (h + 1) * rows)
        source = page_ref[:, h * pair : (h + 1) * pair]
        state = state_ref[place, :]
        score = jnp.where(page_valid, dot_nt(rotated_ref[place, :], source), -jnp.inf)
        row_max = jnp.maximum(state[:, 0:1], jnp.max(score, axis=1, keepdims=True))
        weights = jnp.exp(score - row_max)
        kept = jnp.exp(state[:, 0:1] - row_max)
        denominator = state[:, 1:2] * kept + jnp.sum(weights, axis=1, keepdims=True)
        term = jnp.dot(weights.astype(jnp.bfloat16), source, preferred_element_type=jnp.float32)
        blended = (state * kept + term) / denominator
        for i in range(group_size // 2):
            even = blended[2 * i * tokens : (2 * i + 1) * tokens]
            odd = blended[(2 * i + 1) * tokens : (2 * i + 2) * tokens]
            start = (h * group_size + 2 * i) * HEAD
            attended_ref[:, start : start + pair] = jnp.where(
                low, pltpu.roll(even, HEAD, 1), odd
            ).astype(jnp.bfloat16)
    attended = attended_ref[...]
    for j, ref in enumerate(other_refs):
        copies[j].wait()
        ref[...] = dot_nt(attended, held_ref[j]).astype(jnp.bfloat16)


def own_columns_kernel(me_ref, weight_ref, residual_ref, attended_ref, out_ref, held_ref, rows_ref, sems):
    copies = [
        pltpu.make_async_copy(weight_ref.at[me_ref[0]], held_ref, sems.at[0]),
        pltpu.make_async_copy(residual_ref, rows_ref, sems.at[1]),
    ]
    for copy in copies:
        copy.start()
    for copy in copies:
        copy.wait()
    out_ref[...] = rows_ref[...].astype(jnp.float32) + dot_nt(attended_ref[...], held_ref[...])


def tiles(size):
    return [slice(start, min(start + TILE, size)) for start in range(0, size, TILE)]


def gate_up_kernel(parts, me_ref, gate_ref, up_ref, gain_ref, *refs):
    out_ref, place_ref, row_ref, gate_held, up_held, gain_held, sems = refs[-7:]
    rows, width = refs[0].shape
    features, hidden = gate_ref.shape[1], gate_ref.shape[0]
    gain_copy = pltpu.make_async_copy(gain_ref, gain_held, sems.at[0])
    gain_copy.start()
    copies = []
    for t, tile in enumerate(tiles(hidden)):
        copies.append(
            [
                pltpu.make_async_copy(gate_ref.at[tile], gate_held.at[tile], sems.at[1 + 2 * t]),
                pltpu.make_async_copy(up_ref.at[tile], up_held.at[tile], sems.at[2 + 2 * t]),
            ]
        )
        for copy in copies[-1]:
            copy.start()
    me = me_ref[0]
    gain_copy.wait()
    for s in range(len(refs[:-7]) // parts):
        held = [refs[s * parts + j][...].astype(jnp.float32) for j in range(parts)]
        square = sum(jnp.sum(h * h, axis=1, keepdims=True) for h in held)
        scale = lax.rsqrt(square / features + EPSILON)
        for j in range(parts):
            place_ref[me ^ j] = held[j] * scale
        whole = jnp.concatenate([place_ref[p] for p in range(parts)], axis=1)
        row_ref[pl.ds(s * rows, rows), :] = (whole * gain_held[...]).astype(jnp.bfloat16)
    for t, tile in enumerate(tiles(hidden)):
        for copy in copies[t]:
            copy.wait()
        gate_val = dot_nt(row_ref[...], gate_held[tile])
        up_val = dot_nt(row_ref[...], up_held[tile])
        active = gate_val * jax.nn.sigmoid(ALPHA * gate_val) * (up_val + 1.0)
        out_ref[:, tile] = active.astype(jnp.bfloat16)


def down_kernel(me_ref, down_ref, *refs):
    own_ref, other_ref, held_ref, total_ref, sems = refs[-5:]
    actives = refs[:-5]
    rows, width = own_ref.shape
    copies = [
        pltpu.make_async_copy(down_ref.at[me_ref[0] ^ j], held_ref.at[j], sems.at[j])
        for j in range(len(actives))
    ]
    for copy in copies:
        copy.start()
    for j, ref in enumerate(actives):
        copies[j].wait()
        for tile in tiles(width):
            term = jnp.dot(ref[...], held_ref[j, :, tile], preferred_element_type=jnp.float32)
            if j > 0:
                term = term + total_ref[:, tile]
            if j < len(actives) - 1:
                total_ref[:, tile] = term
            else:
                own_ref[:, tile] = term[:rows].astype(jnp.bfloat16)
                other_ref[:, tile] = term[rows:].astype(jnp.bfloat16)


def kernel_call(kernel, out_types, scalars, sources, *operands, scratch=()):
    in_vmem = pl.BlockSpec(memory_space=pltpu.VMEM)
    in_hbm = pl.BlockSpec(memory_space=pltpu.HBM)
    return pl.pallas_call(
        kernel,
        out_shape=[pltpu.VMEM(shape, dtype) for shape, dtype in out_types],
        in_specs=[pl.BlockSpec(memory_space=pltpu.SMEM)] * len(scalars)
        + [in_hbm] * len(sources)
        + [in_vmem] * len(operands),
        out_specs=[in_vmem] * len(out_types),
        scratch_shapes=scratch,
        compiler_params=pltpu.CompilerParams(vmem_limit_bytes=VMEM_LIMIT),
    )(
        *scalars,
        *[pltpu.with_memory_space_constraint(value, pltpu.HBM) for value in sources],
        *[pltpu.with_memory_space_constraint(value, pltpu.VMEM) for value in operands],
    )


def on_device(
    queries,
    new_kv,
    local_cache,
    remote_pool,
    page_index,
    lengths,
    sinks,
    out_weight,
    residual,
    norm_gain,
    routes,
    route_weights,
    expert_gate,
    expert_up,
    expert_down,
):
    groups = lax.axis_size("group")
    tp = lax.axis_size("tp")
    me_tp = lax.axis_index("tp")
    experts = groups // 2
    me_expert = lax.axis_index("group") // 2
    tp_scalar = me_tp.astype(jnp.int32).reshape(1)
    lane_count = remote_pool.shape[1]
    local_len = local_cache.shape[0]
    fetched = lax.all_to_all(
        remote_pool.reshape(groups, -1, lane_count),
        "group",
        split_axis=0,
        concat_axis=0,
        tiled=True,
    )
    page_len = fetched.shape[1]
    length = lengths[0]
    offsets = jnp.arange(page_len, dtype=jnp.int32)
    remote_pos = local_len + page_index[0][:, None] * page_len + offsets[None, :]
    page_valid = (remote_pos < length).astype(jnp.float32).reshape(1, -1)
    block_len, width = residual.shape
    positions = (length + jnp.arange(block_len, dtype=jnp.int32)).astype(jnp.float32)
    lane = jnp.arange(2 * HEAD, dtype=jnp.int32) % HEAD
    inverse = THETA ** (-2.0 * (lane % (HEAD // 2)).astype(jnp.float32) / HEAD)
    angles = positions[:, None] * inverse[None, :]
    sine = jnp.where(lane < HEAD // 2, -1.0, 1.0)[None, :] * jnp.sin(angles)
    hidden = expert_gate.shape[2]
    weight = out_weight.T.reshape(tp, width, out_weight.shape[0])
    gate, up = expert_gate[0].T, expert_up[0].T
    down = expert_down.reshape(tp, hidden, width)
    gain = norm_gain.reshape(1, tp * width)
    dma = pltpu.SemaphoreType.DMA
    in_vmem = pl.BlockSpec(memory_space=pltpu.VMEM)
    states = block_len * queries.shape[1] // HEAD
    rotated, state = pl.pallas_call(
        local_kernel,
        out_shape=[
            pltpu.VMEM((states, 2 * HEAD), jnp.bfloat16),
            pltpu.VMEM((states, 2 * HEAD), jnp.float32),
        ],
        in_specs=[pl.BlockSpec(memory_space=pltpu.SMEM)] + [in_vmem] * 5,
        out_specs=[in_vmem] * 2,
        compiler_params=pltpu.CompilerParams(vmem_limit_bytes=VMEM_LIMIT),
    )(
        sinks,
        *[pltpu.with_memory_space_constraint(value, pltpu.HBM) for value in (queries, new_kv, local_cache)],
        *[pltpu.with_memory_space_constraint(value, pltpu.VMEM) for value in (jnp.cos(angles), sine)],
    )
    attended, *others = kernel_call(
        page_kernel,
        [(queries.shape, jnp.bfloat16)] + [(residual.shape, jnp.bfloat16)] * (tp - 1),
        [tp_scalar],
        [weight],
        rotated,
        state,
        fetched.reshape(-1, lane_count),
        page_valid,
        scratch=[pltpu.VMEM((tp - 1, *weight.shape[1:]), jnp.bfloat16), dma((tp - 1,))],
    )
    arriving = [exchange(other, "tp", j + 1) for j, other in enumerate(others)]
    (own_state,) = kernel_call(
        own_columns_kernel,
        [(residual.shape, jnp.float32)],
        [tp_scalar],
        [weight, residual],
        attended,
        scratch=[
            pltpu.VMEM(weight.shape[1:], jnp.bfloat16),
            pltpu.VMEM(residual.shape, jnp.bfloat16),
            dma((2,)),
        ],
    )
    for term in arriving:
        own_state = own_state + term.astype(jnp.float32)
    state_sent = own_state.astype(jnp.bfloat16)

    top_count = routes.shape[1]
    capacity = 5 * block_len * top_count // (4 * experts)
    mixing = route_weights / jnp.sum(route_weights, axis=1, keepdims=True)
    chosen = (routes ^ me_expert)[:, :, None] == jnp.arange(experts, dtype=jnp.int32)
    member = jnp.any(chosen, axis=1)
    mix = jnp.sum(jnp.where(chosen, mixing[:, :, None], 0.0), axis=1)
    earlier = jnp.arange(block_len)[:, None] > jnp.arange(block_len)[None, :]
    rank = jnp.dot(
        earlier.astype(jnp.bfloat16), member.astype(jnp.bfloat16), preferred_element_type=jnp.float32
    ).astype(jnp.int32)
    hit = member.T[:, None, :] & (
        rank.T[:, None, :] == jnp.arange(capacity, dtype=jnp.int32)[None, :, None]
    )
    pick = hit.astype(jnp.bfloat16)
    spread = jnp.where(hit, mix.T[:, None, :], 0.0).reshape(experts * capacity, block_len)
    spread_high = spread.astype(jnp.bfloat16)
    spread_low = (spread - spread_high.astype(jnp.float32)).astype(jnp.bfloat16)

    quarter = experts // 4
    chunks = [
        [*range(c * quarter, (c + 1) * quarter), *range((c + 2) * quarter, (c + 3) * quarter)]
        for c in range(2)
    ]

    def gather_rows(steps, sent):
        chosen_rows = jnp.concatenate([pick[d] for d in steps], axis=0)
        send = jnp.dot(chosen_rows, sent, preferred_element_type=jnp.float32).astype(jnp.bfloat16)
        send = send.reshape(len(steps), capacity, width)
        return jnp.concatenate([exchange(send[i], "group", 2 * d) for i, d in enumerate(steps)], axis=0)

    def activate(blocks, others):
        rows = blocks[0].shape[0]
        (active,) = kernel_call(
            functools.partial(gate_up_kernel, tp),
            [((2 * rows, hidden), jnp.bfloat16)],
            [tp_scalar],
            [gate, up, gain],
            *blocks,
            *others,
            scratch=[
                pltpu.VMEM((tp, rows, width), jnp.float32),
                pltpu.VMEM((2 * rows, tp * width), jnp.bfloat16),
                pltpu.VMEM(gate.shape, jnp.bfloat16),
                pltpu.VMEM(up.shape, jnp.bfloat16),
                pltpu.VMEM(gain.shape, jnp.float32),
                dma((1 + 2 * len(tiles(hidden)),)),
            ],
        )
        return active

    def project_down(actives):
        rows = actives[0].shape[0] // 2
        return kernel_call(
            down_kernel,
            [((rows, width), jnp.bfloat16)] * 2,
            [tp_scalar],
            [down],
            *actives,
            scratch=[
                pltpu.VMEM(down.shape, jnp.bfloat16),
                pltpu.VMEM((2 * rows, width), jnp.float32),
                dma((tp,)),
            ],
        )

    def send_back(steps, mine, theirs):
        summed = mine.astype(jnp.float32) + exchange(theirs, "group", 1).astype(jnp.float32)
        summed = summed.astype(jnp.bfloat16).reshape(len(steps), capacity, width)
        return [exchange(summed[i], "group", 2 * d) for i, d in enumerate(steps)]

    def after(value, *earlier):
        return lax.optimization_barrier((value, *earlier))[0]

    held = [gather_rows(steps, state_sent) for steps in chunks]
    blocks = [[exchange(rows, "tp", j) for j in range(tp)] for rows in held]
    others = [exchange(block, "group", 1) for block in blocks[0]]
    first_active = activate(blocks[0], others)
    first_actives = [exchange(first_active, "tp", j) for j in range(tp)]
    others = [exchange(blocks[1][0], "group", 1)]
    others += [exchange(after(block, first_active), "group", 1) for block in blocks[1][1:]]
    second_active = activate(blocks[1], others)
    second_actives = [exchange(second_active, "tp", j) for j in range(tp)]
    first_actives[0] = after(first_actives[0], second_active)
    first_back = send_back(chunks[0], *project_down(first_actives))
    second_actives[0] = after(second_actives[0], *first_back)
    second_back = send_back(chunks[1], *project_down(second_actives))
    back = dict(zip(chunks[0] + chunks[1], first_back + second_back))
    back = [back[d] for d in range(experts)]
    returned = jnp.concatenate(back, axis=0)
    rows_first = (((0,), (0,)), ((), ()))
    moe_out = lax.dot_general(
        spread_high, returned, rows_first, preferred_element_type=jnp.float32
    ) + lax.dot_general(spread_low, returned, rows_first, preferred_element_type=jnp.float32)
    return (own_state + moe_out).astype(jnp.bfloat16)


def solution(mesh):
    return jax.shard_map(
        on_device,
        mesh=mesh,
        in_specs=(
            P("group", "tp"),
            P("group", "tp"),
            P("group", "tp"),
            P("group", "tp"),
            P("group", None),
            P("group"),
            P("tp"),
            P("tp", None),
            P("group", "tp"),
            P(),
            P("group", None),
            P("group", None),
            P("group", None, "tp"),
            P("group", None, "tp"),
            P("group", None, "tp"),
        ),
        out_specs=P("group", "tp"),
        check_vma=False,
    )
```

```python
import functools

import jax
import jax.numpy as jnp
from jax import lax
from jax.experimental import pallas as pl
from jax.experimental.pallas import tpu as pltpu
from jax.sharding import PartitionSpec as P

HEAD = 64
TILE = 256
VMEM_LIMIT = 24 * 1024 * 1024


THETA = 150000.0
ALPHA = 1.702
EPSILON = 1e-05


def exchange(value, axis, offset):
    if offset == 0:
        return value
    size = lax.axis_size(axis)
    return lax.ppermute(value, axis, [(i, i ^ offset) for i in range(size)])


NT = (((1,), (1,)), ((), ()))


def dot_nt(left, right):
    return lax.dot_general(left, right, NT, preferred_element_type=jnp.float32)


def swapped_halves(value):
    lanes = value.shape[1]
    lane = lax.broadcasted_iota(jnp.int32, value.shape, 1)
    return jnp.where(
        lane % HEAD < HEAD // 2,
        pltpu.roll(value, lanes - HEAD // 2, 1),
        pltpu.roll(value, HEAD // 2, 1),
    )


def local_kernel(sink_ref, query_ref, kv_ref, local_ref, cos_ref, sin_ref, rotated_ref, state_ref):
    tokens = query_ref.shape[0]
    pair = 2 * HEAD
    kv_heads = kv_ref.shape[1] // pair
    group_size = query_ref.shape[1] // HEAD // kv_heads
    rows = group_size * tokens
    cosine, sine = cos_ref[...], sin_ref[...]
    low = lax.broadcasted_iota(jnp.int32, (tokens, pair), 1) < HEAD
    lane = lax.broadcasted_iota(jnp.int32, (rows, pair), 1)

    def rotated(value):
        return value * cosine + swapped_halves(value) * sine

    token_row = lax.broadcasted_iota(jnp.int32, (rows, tokens), 0) % tokens
    causal = lax.broadcasted_iota(jnp.int32, (rows, tokens), 1) <= token_row
    for h in range(kv_heads):
        lanes = slice(h * pair, (h + 1) * pair)
        own = kv_ref[:, lanes]
        own = jnp.where(low, rotated(own.astype(jnp.float32)).astype(jnp.bfloat16), own)
        queries = []
        for i in range(group_size // 2):
            start = (h * group_size + 2 * i) * HEAD
            both = rotated(query_ref[:, start : start + pair].astype(jnp.float32)) * HEAD**-0.5
            queries.append(jnp.where(low, both, 0.0))
            queries.append(jnp.where(low, pltpu.roll(both, HEAD, 1), 0.0))
        query = jnp.concatenate(queries, axis=0).astype(jnp.bfloat16)
        sink = jnp.concatenate(
            [jnp.full((tokens, 1), sink_ref[h * group_size + i]) for i in range(group_size)], axis=0
        )
        sources = [local_ref[:, lanes], own]
        scores = [dot_nt(query, source) for source in sources]
        scores[1] = jnp.where(causal, scores[1], -jnp.inf)
        row_max = sink
        for score in scores:
            row_max = jnp.maximum(row_max, jnp.max(score, axis=1, keepdims=True))
        denominator = jnp.exp(sink - row_max)
        blended = None
        for score, source in zip(scores, sources):
            weights = jnp.exp(score - row_max)
            denominator = denominator + jnp.sum(weights, axis=1, keepdims=True)
            term = jnp.dot(weights.astype(jnp.bfloat16), source, preferred_element_type=jnp.float32)
            blended = term if blended is None else blended + term
        place = slice(h * rows, (h + 1) * rows)
        rotated_ref[place, :] = query
        state_ref[place, :] = jnp.where(lane == 0, row_max, jnp.where(lane == 1, denominator, blended))


def page_kernel(me_ref, weight_ref, rotated_ref, state_ref, page_ref, valid_ref, attended_ref, *refs):
    other_refs, held_ref, sems = refs[:-2], refs[-2], refs[-1]
    copies = [
        pltpu.make_async_copy(weight_ref.at[me_ref[0] ^ (j + 1)], held_ref.at[j], sems.at[j])
        for j in range(len(other_refs))
    ]
    for copy in copies:
        copy.start()
    tokens = attended_ref.shape[0]
    pair = 2 * HEAD
    kv_heads = page_ref.shape[1] // pair
    rows = rotated_ref.shape[0] // kv_heads
    group_size = rows // tokens
    low = lax.broadcasted_iota(jnp.int32, (tokens, pair), 1) < HEAD
    page_valid = valid_ref[...] > 0.0
    for h in range(kv_heads):
        place = slice(h * rows, (h + 1) * rows)
        source = page_ref[:, h * pair : (h + 1) * pair]
        state = state_ref[place, :]
        score = jnp.where(page_valid, dot_nt(rotated_ref[place, :], source), -jnp.inf)
        row_max = jnp.maximum(state[:, 0:1], jnp.max(score, axis=1, keepdims=True))
        weights = jnp.exp(score - row_max)
        kept = jnp.exp(state[:, 0:1] - row_max)
        denominator = state[:, 1:2] * kept + jnp.sum(weights, axis=1, keepdims=True)
        term = jnp.dot(weights.astype(jnp.bfloat16), source, preferred_element_type=jnp.float32)
        blended = (state * kept + term) / denominator
        for i in range(group_size // 2):
            even = blended[2 * i * tokens : (2 * i + 1) * tokens]
            odd = blended[(2 * i + 1) * tokens : (2 * i + 2) * tokens]
            start = (h * group_size + 2 * i) * HEAD
            attended_ref[:, start : start + pair] = jnp.where(
                low, pltpu.roll(even, HEAD, 1), odd
            ).astype(jnp.bfloat16)
    attended = attended_ref[...]
    for j, ref in enumerate(other_refs):
        copies[j].wait()
        ref[...] = dot_nt(attended, held_ref[j]).astype(jnp.bfloat16)


def own_columns_kernel(me_ref, weight_ref, residual_ref, attended_ref, out_ref, held_ref, rows_ref, sems):
    copies = [
        pltpu.make_async_copy(weight_ref.at[me_ref[0]], held_ref, sems.at[0]),
        pltpu.make_async_copy(residual_ref, rows_ref, sems.at[1]),
    ]
    for copy in copies:
        copy.start()
    for copy in copies:
        copy.wait()
    out_ref[...] = rows_ref[...].astype(jnp.float32) + dot_nt(attended_ref[...], held_ref[...])


def tiles(size):
    return [slice(start, min(start + TILE, size)) for start in range(0, size, TILE)]


def gate_up_kernel(parts, me_ref, gate_ref, up_ref, gain_ref, *refs):
    sets, (out_ref, place_ref, row_ref, gate_held, up_held, gain_held, sems) = refs[:-7], refs[-7:]
    rows, width = sets[0].shape[-2:]
    features, hidden = gate_ref.shape[1], gate_ref.shape[0]
    hidden_tiles = tiles(hidden)
    copies = [
        [
            pltpu.make_async_copy(source.at[tile], target.at[tile], sems.at[1 + 2 * t + i])
            for i, (source, target) in enumerate([(gate_ref, gate_held), (up_ref, up_held)])
        ]
        for t, tile in enumerate(hidden_tiles)
    ]

    def start(t):
        if t < len(copies):
            for copy in copies[t]:
                copy.start()

    gain_copy = pltpu.make_async_copy(gain_ref, gain_held, sems.at[0])
    gain_copy.start()
    start(0)
    me = me_ref[0]
    gain_copy.wait()
    place = 0
    index = 0
    while index < len(sets):
        if len(sets[index].shape) == 3:
            held = [sets[index][j].astype(jnp.float32) for j in range(parts)]
            index += 1
        else:
            held = [sets[index + j][...].astype(jnp.float32) for j in range(parts)]
            index += parts
        square = sum(jnp.sum(h * h, axis=1, keepdims=True) for h in held)
        scale = lax.rsqrt(square / features + EPSILON)
        for j in range(parts):
            place_ref[me ^ j] = held[j] * scale
        whole = jnp.concatenate([place_ref[p] for p in range(parts)], axis=1)
        row_ref[pl.ds(place, rows), :] = (whole * gain_held[...]).astype(jnp.bfloat16)
        place += rows
    for t, tile in enumerate(hidden_tiles):
        start(t + 1)
        for copy in copies[t]:
            copy.wait()
        gate_val = dot_nt(row_ref[...], gate_held[tile])
        up_val = dot_nt(row_ref[...], up_held[tile])
        active = gate_val * jax.nn.sigmoid(ALPHA * gate_val) * (up_val + 1.0)
        out_ref[:, tile] = active.astype(jnp.bfloat16)


def down_kernel(me_ref, down_ref, *refs):
    own_ref, other_ref, held_ref, total_ref, sems = refs[-5:]
    actives = refs[:-5]
    rows, width = own_ref.shape
    copies = [
        pltpu.make_async_copy(down_ref.at[me_ref[0] ^ j], held_ref.at[j], sems.at[j])
        for j in range(len(actives))
    ]
    copies[0].start()
    for j, ref in enumerate(actives):
        copies[j].wait()
        if j + 1 < len(actives):
            copies[j + 1].start()
        for tile in tiles(width):
            term = jnp.dot(ref[...], held_ref[j, :, tile], preferred_element_type=jnp.float32)
            if j > 0:
                term = term + total_ref[:, tile]
            if j < len(actives) - 1:
                total_ref[:, tile] = term
            else:
                own_ref[:, tile] = term[:rows].astype(jnp.bfloat16)
                other_ref[:, tile] = term[rows:].astype(jnp.bfloat16)


def kernel_call(kernel, out_types, scalars, sources, *operands, scratch=()):
    in_vmem = pl.BlockSpec(memory_space=pltpu.VMEM)
    in_hbm = pl.BlockSpec(memory_space=pltpu.HBM)
    return pl.pallas_call(
        kernel,
        out_shape=[pltpu.VMEM(shape, dtype) for shape, dtype in out_types],
        in_specs=[pl.BlockSpec(memory_space=pltpu.SMEM)] * len(scalars)
        + [in_hbm] * len(sources)
        + [in_vmem] * len(operands),
        out_specs=[in_vmem] * len(out_types),
        scratch_shapes=scratch,
        compiler_params=pltpu.CompilerParams(vmem_limit_bytes=VMEM_LIMIT),
    )(
        *scalars,
        *[pltpu.with_memory_space_constraint(value, pltpu.HBM) for value in sources],
        *[pltpu.with_memory_space_constraint(value, pltpu.VMEM) for value in operands],
    )


def on_device(
    queries,
    new_kv,
    local_cache,
    remote_pool,
    page_index,
    lengths,
    sinks,
    out_weight,
    residual,
    norm_gain,
    routes,
    route_weights,
    expert_gate,
    expert_up,
    expert_down,
):
    groups = lax.axis_size("group")
    tp = lax.axis_size("tp")
    me_tp = lax.axis_index("tp")
    experts = groups // 2
    me_expert = lax.axis_index("group") // 2
    tp_scalar = me_tp.astype(jnp.int32).reshape(1)
    lane_count = remote_pool.shape[1]
    local_len = local_cache.shape[0]
    fetched = lax.all_to_all(
        remote_pool.reshape(groups, -1, lane_count),
        "group",
        split_axis=0,
        concat_axis=0,
        tiled=True,
    )
    page_len = fetched.shape[1]
    length = lengths[0]
    offsets = jnp.arange(page_len, dtype=jnp.int32)
    remote_pos = local_len + page_index[0][:, None] * page_len + offsets[None, :]
    page_valid = (remote_pos < length).astype(jnp.float32).reshape(1, -1)
    block_len, width = residual.shape
    positions = (length + jnp.arange(block_len, dtype=jnp.int32)).astype(jnp.float32)
    lane = jnp.arange(2 * HEAD, dtype=jnp.int32) % HEAD
    inverse = THETA ** (-2.0 * (lane % (HEAD // 2)).astype(jnp.float32) / HEAD)
    angles = positions[:, None] * inverse[None, :]
    sine = jnp.where(lane < HEAD // 2, -1.0, 1.0)[None, :] * jnp.sin(angles)
    hidden = expert_gate.shape[2]
    weight = out_weight.T.reshape(tp, width, out_weight.shape[0])
    gate, up = expert_gate[0].T, expert_up[0].T
    down = expert_down.reshape(tp, hidden, width)
    gain = norm_gain.reshape(1, tp * width)
    dma = pltpu.SemaphoreType.DMA
    in_vmem = pl.BlockSpec(memory_space=pltpu.VMEM)
    states = block_len * queries.shape[1] // HEAD
    rotated, state = pl.pallas_call(
        local_kernel,
        out_shape=[
            pltpu.VMEM((states, 2 * HEAD), jnp.bfloat16),
            pltpu.VMEM((states, 2 * HEAD), jnp.float32),
        ],
        in_specs=[pl.BlockSpec(memory_space=pltpu.SMEM)] + [in_vmem] * 5,
        out_specs=[in_vmem] * 2,
        compiler_params=pltpu.CompilerParams(vmem_limit_bytes=VMEM_LIMIT),
    )(
        sinks,
        *[pltpu.with_memory_space_constraint(value, pltpu.HBM) for value in (queries, new_kv, local_cache)],
        *[pltpu.with_memory_space_constraint(value, pltpu.VMEM) for value in (jnp.cos(angles), sine)],
    )
    attended, *others = kernel_call(
        page_kernel,
        [(queries.shape, jnp.bfloat16)] + [(residual.shape, jnp.bfloat16)] * (tp - 1),
        [tp_scalar],
        [weight],
        rotated,
        state,
        fetched.reshape(-1, lane_count),
        page_valid,
        scratch=[pltpu.VMEM((tp - 1, *weight.shape[1:]), jnp.bfloat16), dma((tp - 1,))],
    )
    arriving = [exchange(other, "tp", j + 1) for j, other in enumerate(others)]
    (own_state,) = kernel_call(
        own_columns_kernel,
        [(residual.shape, jnp.float32)],
        [tp_scalar],
        [weight, residual],
        attended,
        scratch=[
            pltpu.VMEM(weight.shape[1:], jnp.bfloat16),
            pltpu.VMEM(residual.shape, jnp.bfloat16),
            dma((2,)),
        ],
    )
    for term in arriving:
        own_state = own_state + term.astype(jnp.float32)
    state_sent = own_state.astype(jnp.bfloat16)

    top_count = routes.shape[1]
    capacity = 5 * block_len * top_count // (4 * experts)
    mixing = route_weights / jnp.sum(route_weights, axis=1, keepdims=True)
    chosen = (routes ^ me_expert)[:, :, None] == jnp.arange(experts, dtype=jnp.int32)
    member = jnp.any(chosen, axis=1)
    mix = jnp.sum(jnp.where(chosen, mixing[:, :, None], 0.0), axis=1)
    earlier = jnp.arange(block_len)[:, None] > jnp.arange(block_len)[None, :]
    rank = jnp.dot(
        earlier.astype(jnp.bfloat16), member.astype(jnp.bfloat16), preferred_element_type=jnp.float32
    ).astype(jnp.int32)
    hit = member.T[:, None, :] & (
        rank.T[:, None, :] == jnp.arange(capacity, dtype=jnp.int32)[None, :, None]
    )
    pick = hit.astype(jnp.bfloat16)
    spread = jnp.where(hit, mix.T[:, None, :], 0.0).reshape(experts * capacity, block_len)
    spread_high = spread.astype(jnp.bfloat16)
    spread_low = (spread - spread_high.astype(jnp.float32)).astype(jnp.bfloat16)

    quarter = experts // 4
    near = [range(c * quarter, (c + 1) * quarter) for c in range(2)]
    far = [range((c + 2) * quarter, (c + 3) * quarter) for c in range(2)]
    chunks = [[*near[c], *far[c]] for c in range(2)]
    whole_state = [exchange(state_sent, "tp", j) for j in range(tp)]

    def picked(steps, value):
        chosen_rows = jnp.concatenate([pick[d] for d in steps], axis=0)
        rows = jnp.dot(chosen_rows, value, preferred_element_type=jnp.float32).astype(jnp.bfloat16)
        return rows.reshape(len(steps), capacity, width)

    def gather_far(steps):
        send = picked(steps, state_sent)
        return jnp.concatenate([exchange(send[i], "group", 2 * d) for i, d in enumerate(steps)], axis=0)

    def gather_near(steps, values):
        send = jnp.stack([picked(steps, value) for value in values], axis=1)
        return [exchange(send[i], "group", 2 * d) for i, d in enumerate(steps)]

    def after(value, *earlier):
        return lax.optimization_barrier((value, *earlier))[0]

    def activate(sets):
        rows = sets[0].shape[1]
        (active,) = kernel_call(
            functools.partial(gate_up_kernel, tp),
            [((4 * rows, hidden), jnp.bfloat16)],
            [tp_scalar],
            [gate, up, gain],
            *sets,
            scratch=[
                pltpu.VMEM((tp, rows, width), jnp.float32),
                pltpu.VMEM((4 * rows, tp * width), jnp.bfloat16),
                pltpu.VMEM(gate.shape, jnp.bfloat16),
                pltpu.VMEM(up.shape, jnp.bfloat16),
                pltpu.VMEM(gain.shape, jnp.float32),
                dma((1 + 2 * len(tiles(hidden)),)),
            ],
        )
        return active

    def project_down(actives):
        rows = actives[0].shape[0] // 2
        return kernel_call(
            down_kernel,
            [((rows, width), jnp.bfloat16)] * 2,
            [tp_scalar],
            [down],
            *actives,
            scratch=[
                pltpu.VMEM(down.shape, jnp.bfloat16),
                pltpu.VMEM((2 * rows, width), jnp.float32),
                dma((tp,)),
            ],
        )

    def send_back(steps, mine, theirs):
        summed = mine.astype(jnp.float32) + exchange(theirs, "group", 1).astype(jnp.float32)
        summed = summed.astype(jnp.bfloat16).reshape(len(steps), capacity, width)
        return [exchange(summed[i], "group", 2 * d) for i, d in enumerate(steps)]

    def core_pair(value):
        return exchange(value, "group", 1)

    far_held = [gather_far(steps) for steps in far]
    near_held = [jnp.concatenate(gather_near(near[0], whole_state), axis=1)]
    near_pieces = gather_near(near[1], whole_state)
    far_blocks = [[exchange(rows, "tp", j) for j in range(tp)] for rows in far_held]
    first_active = activate(
        [
            near_held[0],
            *far_blocks[0],
            core_pair(near_held[0]),
            *[core_pair(block) for block in far_blocks[0]],
        ]
    )
    first_actives = [exchange(first_active, "tp", j) for j in range(tp)]
    near_held.append(jnp.concatenate([after(piece, first_active) for piece in near_pieces], axis=1))
    second_active = activate(
        [
            near_held[1],
            *far_blocks[1],
            core_pair(near_held[1]),
            *[core_pair(after(block, first_active)) for block in far_blocks[1]],
        ]
    )
    second_actives = [exchange(second_active, "tp", j) for j in range(tp)]
    first_actives[0] = after(first_actives[0], second_active)
    first_back = send_back(chunks[0], *project_down(first_actives))
    second_back = send_back(chunks[1], *project_down(second_actives))
    back = dict(zip(chunks[0] + chunks[1], first_back + second_back))
    back = [back[d] for d in range(experts)]
    returned = jnp.concatenate(back, axis=0)
    rows_first = (((0,), (0,)), ((), ()))
    moe_out = lax.dot_general(
        spread_high, returned, rows_first, preferred_element_type=jnp.float32
    ) + lax.dot_general(spread_low, returned, rows_first, preferred_element_type=jnp.float32)
    return (own_state + moe_out).astype(jnp.bfloat16)


def solution(mesh):
    return jax.shard_map(
        on_device,
        mesh=mesh,
        in_specs=(
            P("group", "tp"),
            P("group", "tp"),
            P("group", "tp"),
            P("group", "tp"),
            P("group", None),
            P("group"),
            P("tp"),
            P("tp", None),
            P("group", "tp"),
            P(),
            P("group", None),
            P("group", None),
            P("group", None, "tp"),
            P("group", None, "tp"),
            P("group", None, "tp"),
        ),
        out_specs=P("group", "tp"),
        check_vma=False,
    )
```

```python
import functools

import jax
import jax.numpy as jnp
from jax import lax
from jax.experimental import pallas as pl
from jax.experimental.pallas import tpu as pltpu
from jax.sharding import PartitionSpec as P

HEAD = 64
TILE = 256
PARTS = 4
VMEM_LIMIT = 24 * 1024 * 1024


THETA = 150000.0
ALPHA = 1.702
EPSILON = 1e-05


def exchange(value, axis, offset):
    if offset == 0:
        return value
    size = lax.axis_size(axis)
    return lax.ppermute(value, axis, [(i, i ^ offset) for i in range(size)])


NT = (((1,), (1,)), ((), ()))


def dot_nt(left, right):
    return lax.dot_general(left, right, NT, preferred_element_type=jnp.float32)


def swapped_halves(value):
    lanes = value.shape[1]
    lane = lax.broadcasted_iota(jnp.int32, value.shape, 1)
    return jnp.where(
        lane % HEAD < HEAD // 2,
        pltpu.roll(value, lanes - HEAD // 2, 1),
        pltpu.roll(value, HEAD // 2, 1),
    )


def local_kernel(sink_ref, query_ref, kv_ref, local_ref, cos_ref, sin_ref, rotated_ref, state_ref):
    tokens = query_ref.shape[0]
    pair = 2 * HEAD
    kv_heads = kv_ref.shape[1] // pair
    group_size = query_ref.shape[1] // HEAD // kv_heads
    rows = group_size * tokens
    cosine, sine = cos_ref[...], sin_ref[...]
    low = lax.broadcasted_iota(jnp.int32, (tokens, pair), 1) < HEAD
    lane = lax.broadcasted_iota(jnp.int32, (rows, pair), 1)

    def rotated(value):
        return value * cosine + swapped_halves(value) * sine

    token_row = lax.broadcasted_iota(jnp.int32, (rows, tokens), 0) % tokens
    causal = lax.broadcasted_iota(jnp.int32, (rows, tokens), 1) <= token_row
    for h in range(kv_heads):
        lanes = slice(h * pair, (h + 1) * pair)
        own = kv_ref[:, lanes]
        own = jnp.where(low, rotated(own.astype(jnp.float32)).astype(jnp.bfloat16), own)
        queries = []
        for i in range(group_size // 2):
            start = (h * group_size + 2 * i) * HEAD
            both = rotated(query_ref[:, start : start + pair].astype(jnp.float32)) * HEAD**-0.5
            queries.append(jnp.where(low, both, 0.0))
            queries.append(jnp.where(low, pltpu.roll(both, HEAD, 1), 0.0))
        query = jnp.concatenate(queries, axis=0).astype(jnp.bfloat16)
        sink = jnp.concatenate(
            [jnp.full((tokens, 1), sink_ref[h * group_size + i]) for i in range(group_size)], axis=0
        )
        sources = [local_ref[:, lanes], own]
        scores = [dot_nt(query, source) for source in sources]
        scores[1] = jnp.where(causal, scores[1], -jnp.inf)
        row_max = sink
        for score in scores:
            row_max = jnp.maximum(row_max, jnp.max(score, axis=1, keepdims=True))
        denominator = jnp.exp(sink - row_max)
        blended = None
        for score, source in zip(scores, sources):
            weights = jnp.exp(score - row_max)
            denominator = denominator + jnp.sum(weights, axis=1, keepdims=True)
            term = jnp.dot(weights.astype(jnp.bfloat16), source, preferred_element_type=jnp.float32)
            blended = term if blended is None else blended + term
        place = slice(h * rows, (h + 1) * rows)
        rotated_ref[place, :] = query
        state_ref[place, :] = jnp.where(lane == 0, row_max, jnp.where(lane == 1, denominator, blended))


def split_copies(source, target, sems, first, parts):
    rows = source.shape[0]
    step = -(-rows // parts) // 16 * 16 + 16
    return [
        pltpu.make_async_copy(
            source.at[start : min(start + step, rows)],
            target.at[start : min(start + step, rows)],
            sems.at[first + i],
        )
        for i, start in enumerate(range(0, rows, step))
    ]


def start_all(copies):
    for copy in copies:
        copy.start()


def wait_all(copies):
    for copy in copies:
        copy.wait()


def page_kernel(me_ref, weight_ref, rotated_ref, state_ref, page_ref, valid_ref, attended_ref, *refs):
    other_refs, held_ref, sems = refs[:-2], refs[-2], refs[-1]
    copies = [
        split_copies(weight_ref.at[me_ref[0] ^ (j + 1)], held_ref.at[j], sems, PARTS * j, PARTS)
        for j in range(len(other_refs))
    ]
    for some in copies:
        start_all(some)
    tokens = attended_ref.shape[0]
    pair = 2 * HEAD
    kv_heads = page_ref.shape[1] // pair
    rows = rotated_ref.shape[0] // kv_heads
    group_size = rows // tokens
    low = lax.broadcasted_iota(jnp.int32, (tokens, pair), 1) < HEAD
    page_valid = valid_ref[...] > 0.0
    for h in range(kv_heads):
        place = slice(h * rows, (h + 1) * rows)
        source = page_ref[:, h * pair : (h + 1) * pair]
        state = state_ref[place, :]
        score = jnp.where(page_valid, dot_nt(rotated_ref[place, :], source), -jnp.inf)
        row_max = jnp.maximum(state[:, 0:1], jnp.max(score, axis=1, keepdims=True))
        weights = jnp.exp(score - row_max)
        kept = jnp.exp(state[:, 0:1] - row_max)
        denominator = state[:, 1:2] * kept + jnp.sum(weights, axis=1, keepdims=True)
        term = jnp.dot(weights.astype(jnp.bfloat16), source, preferred_element_type=jnp.float32)
        blended = (state * kept + term) / denominator
        for i in range(group_size // 2):
            even = blended[2 * i * tokens : (2 * i + 1) * tokens]
            odd = blended[(2 * i + 1) * tokens : (2 * i + 2) * tokens]
            start = (h * group_size + 2 * i) * HEAD
            attended_ref[:, start : start + pair] = jnp.where(
                low, pltpu.roll(even, HEAD, 1), odd
            ).astype(jnp.bfloat16)
    attended = attended_ref[...]
    for j, ref in enumerate(other_refs):
        wait_all(copies[j])
        ref[...] = dot_nt(attended, held_ref[j]).astype(jnp.bfloat16)


def own_columns_kernel(me_ref, weight_ref, residual_ref, attended_ref, out_ref, held_ref, rows_ref, sems):
    copies = split_copies(weight_ref.at[me_ref[0]], held_ref, sems, 0, PARTS)
    copies.append(pltpu.make_async_copy(residual_ref, rows_ref, sems.at[PARTS]))
    start_all(copies)
    wait_all(copies)
    out_ref[...] = rows_ref[...].astype(jnp.float32) + dot_nt(attended_ref[...], held_ref[...])


def tiles(size):
    return [slice(start, min(start + TILE, size)) for start in range(0, size, TILE)]


def gate_up_kernel(parts, me_ref, gate_ref, up_ref, gain_ref, *refs):
    sets, (out_ref, place_ref, row_ref, gate_held, up_held, gain_held, sems) = refs[:-7], refs[-7:]
    rows, width = sets[0].shape[1:]
    features, hidden = gate_ref.shape[1], gate_ref.shape[0]
    gain_copy = pltpu.make_async_copy(gain_ref, gain_held, sems.at[0])
    gain_copy.start()
    copies = []
    for t, tile in enumerate(tiles(hidden)):
        some = split_copies(gate_ref.at[tile], gate_held.at[tile], sems, 1 + 4 * t, 2)
        some += split_copies(up_ref.at[tile], up_held.at[tile], sems, 3 + 4 * t, 2)
        start_all(some)
        copies.append(some)
    me = me_ref[0]
    gain_copy.wait()
    for s, ref in enumerate(sets):
        held = [ref[j].astype(jnp.float32) for j in range(parts)]
        square = sum(jnp.sum(h * h, axis=1, keepdims=True) for h in held)
        scale = lax.rsqrt(square / features + EPSILON)
        for j in range(parts):
            place_ref[me ^ j] = held[j] * scale
        whole = jnp.concatenate([place_ref[p] for p in range(parts)], axis=1)
        row_ref[pl.ds(s * rows, rows), :] = (whole * gain_held[...]).astype(jnp.bfloat16)
    for t, tile in enumerate(tiles(hidden)):
        wait_all(copies[t])
        gate_val = dot_nt(row_ref[...], gate_held[tile])
        up_val = dot_nt(row_ref[...], up_held[tile])
        active = gate_val * jax.nn.sigmoid(ALPHA * gate_val) * (up_val + 1.0)
        out_ref[:, tile] = active.astype(jnp.bfloat16)


def down_kernel(me_ref, down_ref, *refs):
    own_ref, other_ref, held_ref, total_ref, sems = refs[-5:]
    actives = refs[:-5]
    rows, width = own_ref.shape
    copies = [
        split_copies(down_ref.at[me_ref[0] ^ j], held_ref.at[j], sems, PARTS * j, PARTS)
        for j in range(len(actives))
    ]
    for some in copies:
        start_all(some)
    for j, ref in enumerate(actives):
        wait_all(copies[j])
        for tile in tiles(width):
            term = jnp.dot(ref[...], held_ref[j, :, tile], preferred_element_type=jnp.float32)
            if j > 0:
                term = term + total_ref[:, tile]
            if j < len(actives) - 1:
                total_ref[:, tile] = term
            else:
                own_ref[:, tile] = term[:rows].astype(jnp.bfloat16)
                other_ref[:, tile] = term[rows:].astype(jnp.bfloat16)


def kernel_call(kernel, out_types, scalars, sources, *operands, scratch=()):
    in_vmem = pl.BlockSpec(memory_space=pltpu.VMEM)
    in_hbm = pl.BlockSpec(memory_space=pltpu.HBM)
    return pl.pallas_call(
        kernel,
        out_shape=[pltpu.VMEM(shape, dtype) for shape, dtype in out_types],
        in_specs=[pl.BlockSpec(memory_space=pltpu.SMEM)] * len(scalars)
        + [in_hbm] * len(sources)
        + [in_vmem] * len(operands),
        out_specs=[in_vmem] * len(out_types),
        scratch_shapes=scratch,
        compiler_params=pltpu.CompilerParams(vmem_limit_bytes=VMEM_LIMIT),
    )(
        *scalars,
        *[pltpu.with_memory_space_constraint(value, pltpu.HBM) for value in sources],
        *[pltpu.with_memory_space_constraint(value, pltpu.VMEM) for value in operands],
    )


def on_device(
    queries,
    new_kv,
    local_cache,
    remote_pool,
    page_index,
    lengths,
    sinks,
    out_weight,
    residual,
    norm_gain,
    routes,
    route_weights,
    expert_gate,
    expert_up,
    expert_down,
):
    groups = lax.axis_size("group")
    tp = lax.axis_size("tp")
    me_tp = lax.axis_index("tp")
    experts = groups // 2
    me_expert = lax.axis_index("group") // 2
    tp_scalar = me_tp.astype(jnp.int32).reshape(1)
    lane_count = remote_pool.shape[1]
    local_len = local_cache.shape[0]
    fetched = lax.all_to_all(
        remote_pool.reshape(groups, -1, lane_count),
        "group",
        split_axis=0,
        concat_axis=0,
        tiled=True,
    )
    page_len = fetched.shape[1]
    length = lengths[0]
    offsets = jnp.arange(page_len, dtype=jnp.int32)
    remote_pos = local_len + page_index[0][:, None] * page_len + offsets[None, :]
    page_valid = (remote_pos < length).astype(jnp.float32).reshape(1, -1)
    block_len, width = residual.shape
    positions = (length + jnp.arange(block_len, dtype=jnp.int32)).astype(jnp.float32)
    lane = jnp.arange(2 * HEAD, dtype=jnp.int32) % HEAD
    inverse = THETA ** (-2.0 * (lane % (HEAD // 2)).astype(jnp.float32) / HEAD)
    angles = positions[:, None] * inverse[None, :]
    sine = jnp.where(lane < HEAD // 2, -1.0, 1.0)[None, :] * jnp.sin(angles)
    hidden = expert_gate.shape[2]
    weight = out_weight.T.reshape(tp, width, out_weight.shape[0])
    gate, up = expert_gate[0].T, expert_up[0].T
    down = expert_down.reshape(tp, hidden, width)
    gain = norm_gain.reshape(1, tp * width)
    dma = pltpu.SemaphoreType.DMA
    in_vmem = pl.BlockSpec(memory_space=pltpu.VMEM)
    states = block_len * queries.shape[1] // HEAD
    rotated, state = pl.pallas_call(
        local_kernel,
        out_shape=[
            pltpu.VMEM((states, 2 * HEAD), jnp.bfloat16),
            pltpu.VMEM((states, 2 * HEAD), jnp.float32),
        ],
        in_specs=[pl.BlockSpec(memory_space=pltpu.SMEM)] + [in_vmem] * 5,
        out_specs=[in_vmem] * 2,
        compiler_params=pltpu.CompilerParams(vmem_limit_bytes=VMEM_LIMIT),
    )(
        sinks,
        *[pltpu.with_memory_space_constraint(value, pltpu.HBM) for value in (queries, new_kv, local_cache)],
        *[pltpu.with_memory_space_constraint(value, pltpu.VMEM) for value in (jnp.cos(angles), sine)],
    )
    attended, *others = kernel_call(
        page_kernel,
        [(queries.shape, jnp.bfloat16)] + [(residual.shape, jnp.bfloat16)] * (tp - 1),
        [tp_scalar],
        [weight],
        rotated,
        state,
        fetched.reshape(-1, lane_count),
        page_valid,
        scratch=[pltpu.VMEM((tp - 1, *weight.shape[1:]), jnp.bfloat16), dma((PARTS * (tp - 1),))],
    )
    arriving = [exchange(other, "tp", j + 1) for j, other in enumerate(others)]
    (own_state,) = kernel_call(
        own_columns_kernel,
        [(residual.shape, jnp.float32)],
        [tp_scalar],
        [weight, residual],
        attended,
        scratch=[
            pltpu.VMEM(weight.shape[1:], jnp.bfloat16),
            pltpu.VMEM(residual.shape, jnp.bfloat16),
            dma((PARTS + 1,)),
        ],
    )
    own_terms = own_state.astype(jnp.bfloat16)
    for term in arriving:
        own_state = own_state + term.astype(jnp.float32)
    state_sent = own_state.astype(jnp.bfloat16)
    if tp == 2:
        other_state = exchange(own_terms, "tp", 1).astype(jnp.float32) + others[0].astype(jnp.float32)
        own_blocks = [state_sent, other_state.astype(jnp.bfloat16)]
    else:
        own_blocks = [exchange(state_sent, "tp", j) for j in range(tp)]

    top_count = routes.shape[1]
    capacity = 5 * block_len * top_count // (4 * experts)
    half = experts // 2
    mixing = route_weights / jnp.sum(route_weights, axis=1, keepdims=True)
    plan = jnp.concatenate([routes.astype(jnp.float32), mixing], axis=1)
    far_plan = exchange(plan, "group", experts)

    def slots(chosen_experts, weights):
        chosen = (chosen_experts ^ me_expert)[:, :, None] == jnp.arange(half, dtype=jnp.int32)
        member = jnp.any(chosen, axis=1)
        mix = jnp.sum(jnp.where(chosen, weights[:, :, None], 0.0), axis=1)
        earlier = jnp.arange(block_len)[:, None] > jnp.arange(block_len)[None, :]
        rank = jnp.dot(
            earlier.astype(jnp.bfloat16), member.astype(jnp.bfloat16), preferred_element_type=jnp.float32
        ).astype(jnp.int32)
        hit = member.T[:, None, :] & (
            rank.T[:, None, :] == jnp.arange(capacity, dtype=jnp.int32)[None, :, None]
        )
        pick = hit.astype(jnp.bfloat16).reshape(half * capacity, block_len)
        spread = jnp.where(hit, mix.T[:, None, :], 0.0).reshape(half * capacity, block_len)
        high = spread.astype(jnp.bfloat16)
        return pick, (high, (spread - high.astype(jnp.float32)).astype(jnp.bfloat16))

    own_pick, own_spread = slots(routes, mixing)
    far_pick, far_spread = slots(
        far_plan[:, :top_count].astype(jnp.int32), far_plan[:, top_count:]
    )

    def after(value, *earlier):
        return lax.optimization_barrier((value, *earlier))[0]

    def whole(value):
        return [exchange(value, "tp", j) for j in range(tp)]

    def picked(pick, values):
        parts = [
            jnp.dot(pick, value, preferred_element_type=jnp.float32)
            .astype(jnp.bfloat16)
            .reshape(half, capacity, width)
            for value in values
        ]
        return jnp.stack(parts, axis=1)

    def send_rows(rows):
        return [exchange(rows[d], "group", 2 * d) for d in range(half)]

    def blend(spread, pieces):
        rows = jnp.concatenate(pieces, axis=0)
        rows_first = (((0,), (0,)), ((), ()))
        return sum(
            lax.dot_general(part, rows, rows_first, preferred_element_type=jnp.float32)
            for part in spread
        )

    def activate(sets):
        rows = sets[0].shape[1]
        (active,) = kernel_call(
            functools.partial(gate_up_kernel, tp),
            [((2 * rows, hidden), jnp.bfloat16)],
            [tp_scalar],
            [gate, up, gain],
            *sets,
            scratch=[
                pltpu.VMEM((tp, rows, width), jnp.float32),
                pltpu.VMEM((2 * rows, tp * width), jnp.bfloat16),
                pltpu.VMEM(gate.shape, jnp.bfloat16),
                pltpu.VMEM(up.shape, jnp.bfloat16),
                pltpu.VMEM(gain.shape, jnp.float32),
                dma((1 + 4 * len(tiles(hidden)),)),
            ],
        )
        return active

    def project_down(actives):
        rows = actives[0].shape[0] // 2
        return kernel_call(
            down_kernel,
            [((rows, width), jnp.bfloat16)] * 2,
            [tp_scalar],
            [down],
            *actives,
            scratch=[
                pltpu.VMEM(down.shape, jnp.bfloat16),
                pltpu.VMEM((2 * rows, width), jnp.float32),
                dma((PARTS * tp,)),
            ],
        )

    def send_back(mine, theirs):
        summed = mine.astype(jnp.float32) + exchange(theirs, "group", 1).astype(jnp.float32)
        summed = summed.astype(jnp.bfloat16).reshape(half, capacity, width)
        return [exchange(summed[d], "group", 2 * d) for d in range(half)]

    far_blocks = [exchange(block, "group", experts) for block in own_blocks]
    own_pieces = send_rows(picked(own_pick, own_blocks))
    far_sent = picked(far_pick, far_blocks)
    far_pieces = send_rows(far_sent)
    own_rows = jnp.concatenate([after(piece, far_sent) for piece in own_pieces], axis=1)
    own_active = activate([own_rows, exchange(own_rows, "group", 1)])
    own_actives = whole(own_active)
    far_rows = jnp.concatenate([after(piece, own_active) for piece in far_pieces], axis=1)
    far_active = activate([far_rows, exchange(far_rows, "group", 1)])
    far_actives = whole(far_active)
    own_actives[0] = after(own_actives[0], far_active)
    own_back = send_back(*project_down(own_actives))
    far_back = send_back(*project_down(far_actives))
    far_sum = exchange(blend(far_spread, far_back).astype(jnp.bfloat16), "group", experts)
    total = own_state + blend(own_spread, own_back) + far_sum.astype(jnp.float32)
    return total.astype(jnp.bfloat16)


def solution(mesh):
    return jax.shard_map(
        on_device,
        mesh=mesh,
        in_specs=(
            P("group", "tp"),
            P("group", "tp"),
            P("group", "tp"),
            P("group", "tp"),
            P("group", None),
            P("group"),
            P("tp"),
            P("tp", None),
            P("group", "tp"),
            P(),
            P("group", None),
            P("group", None),
            P("group", None, "tp"),
            P("group", None, "tp"),
            P("group", None, "tp"),
        ),
        out_specs=P("group", "tp"),
        check_vma=False,
    )
```

```python
import functools

import jax
import jax.numpy as jnp
from jax import lax
from jax.experimental import pallas as pl
from jax.experimental.pallas import tpu as pltpu
from jax.sharding import PartitionSpec as P

HEAD = 64
TILE = 256
PARTS = 1
VMEM_LIMIT = 24 * 1024 * 1024


THETA = 150000.0
ALPHA = 1.702
EPSILON = 1e-05


def exchange(value, axis, offset):
    if offset == 0:
        return value
    size = lax.axis_size(axis)
    return lax.ppermute(value, axis, [(i, i ^ offset) for i in range(size)])


NT = (((1,), (1,)), ((), ()))


def dot_nt(left, right):
    return lax.dot_general(left, right, NT, preferred_element_type=jnp.float32)


def swapped_halves(value):
    lanes = value.shape[1]
    lane = lax.broadcasted_iota(jnp.int32, value.shape, 1)
    return jnp.where(
        lane % HEAD < HEAD // 2,
        pltpu.roll(value, lanes - HEAD // 2, 1),
        pltpu.roll(value, HEAD // 2, 1),
    )


def local_kernel(sink_ref, query_ref, kv_ref, local_ref, cos_ref, sin_ref, rotated_ref, state_ref):
    tokens = query_ref.shape[0]
    pair = 2 * HEAD
    kv_heads = kv_ref.shape[1] // pair
    group_size = query_ref.shape[1] // HEAD // kv_heads
    rows = group_size * tokens
    cosine, sine = cos_ref[...], sin_ref[...]
    low = lax.broadcasted_iota(jnp.int32, (tokens, pair), 1) < HEAD
    lane = lax.broadcasted_iota(jnp.int32, (rows, pair), 1)

    def rotated(value):
        return value * cosine + swapped_halves(value) * sine

    token_row = lax.broadcasted_iota(jnp.int32, (rows, tokens), 0) % tokens
    causal = lax.broadcasted_iota(jnp.int32, (rows, tokens), 1) <= token_row
    for h in range(kv_heads):
        lanes = slice(h * pair, (h + 1) * pair)
        own = kv_ref[:, lanes]
        own = jnp.where(low, rotated(own.astype(jnp.float32)).astype(jnp.bfloat16), own)
        queries = []
        for i in range(group_size // 2):
            start = (h * group_size + 2 * i) * HEAD
            both = rotated(query_ref[:, start : start + pair].astype(jnp.float32)) * HEAD**-0.5
            queries.append(jnp.where(low, both, 0.0))
            queries.append(jnp.where(low, pltpu.roll(both, HEAD, 1), 0.0))
        query = jnp.concatenate(queries, axis=0).astype(jnp.bfloat16)
        sink = jnp.concatenate(
            [jnp.full((tokens, 1), sink_ref[h * group_size + i]) for i in range(group_size)], axis=0
        )
        sources = [local_ref[:, lanes], own]
        scores = [dot_nt(query, source) for source in sources]
        scores[1] = jnp.where(causal, scores[1], -jnp.inf)
        row_max = sink
        for score in scores:
            row_max = jnp.maximum(row_max, jnp.max(score, axis=1, keepdims=True))
        denominator = jnp.exp(sink - row_max)
        blended = None
        for score, source in zip(scores, sources):
            weights = jnp.exp(score - row_max)
            denominator = denominator + jnp.sum(weights, axis=1, keepdims=True)
            term = jnp.dot(weights.astype(jnp.bfloat16), source, preferred_element_type=jnp.float32)
            blended = term if blended is None else blended + term
        place = slice(h * rows, (h + 1) * rows)
        rotated_ref[place, :] = query
        state_ref[place, :] = jnp.where(lane == 0, row_max, jnp.where(lane == 1, denominator, blended))


def split_copies(source, target, sems, first, parts):
    rows = source.shape[0]
    step = rows if parts == 1 else -(-rows // parts) // 16 * 16 + 16
    return [
        pltpu.make_async_copy(
            source.at[start : min(start + step, rows)],
            target.at[start : min(start + step, rows)],
            sems.at[first + i],
        )
        for i, start in enumerate(range(0, rows, step))
    ]


def start_all(copies):
    for copy in copies:
        copy.start()


def wait_all(copies):
    for copy in copies:
        copy.wait()


def page_kernel(me_ref, weight_ref, rotated_ref, state_ref, page_ref, valid_ref, attended_ref, *refs):
    other_refs, held_ref, sems = refs[:-2], refs[-2], refs[-1]
    copies = [
        split_copies(weight_ref.at[me_ref[0] ^ (j + 1)], held_ref.at[j], sems, PARTS * j, PARTS)
        for j in range(len(other_refs))
    ]
    for some in copies:
        start_all(some)
    tokens = attended_ref.shape[0]
    pair = 2 * HEAD
    kv_heads = page_ref.shape[1] // pair
    rows = rotated_ref.shape[0] // kv_heads
    group_size = rows // tokens
    low = lax.broadcasted_iota(jnp.int32, (tokens, pair), 1) < HEAD
    page_valid = valid_ref[...] > 0.0
    for h in range(kv_heads):
        place = slice(h * rows, (h + 1) * rows)
        source = page_ref[:, h * pair : (h + 1) * pair]
        state = state_ref[place, :]
        score = jnp.where(page_valid, dot_nt(rotated_ref[place, :], source), -jnp.inf)
        row_max = jnp.maximum(state[:, 0:1], jnp.max(score, axis=1, keepdims=True))
        weights = jnp.exp(score - row_max)
        kept = jnp.exp(state[:, 0:1] - row_max)
        denominator = state[:, 1:2] * kept + jnp.sum(weights, axis=1, keepdims=True)
        term = jnp.dot(weights.astype(jnp.bfloat16), source, preferred_element_type=jnp.float32)
        blended = (state * kept + term) / denominator
        for i in range(group_size // 2):
            even = blended[2 * i * tokens : (2 * i + 1) * tokens]
            odd = blended[(2 * i + 1) * tokens : (2 * i + 2) * tokens]
            start = (h * group_size + 2 * i) * HEAD
            attended_ref[:, start : start + pair] = jnp.where(
                low, pltpu.roll(even, HEAD, 1), odd
            ).astype(jnp.bfloat16)
    attended = attended_ref[...]
    for j, ref in enumerate(other_refs):
        wait_all(copies[j])
        ref[...] = dot_nt(attended, held_ref[j]).astype(jnp.bfloat16)


def own_columns_kernel(me_ref, weight_ref, residual_ref, attended_ref, out_ref, held_ref, rows_ref, sems):
    copies = split_copies(weight_ref.at[me_ref[0]], held_ref, sems, 0, PARTS)
    copies.append(pltpu.make_async_copy(residual_ref, rows_ref, sems.at[PARTS]))
    start_all(copies)
    wait_all(copies)
    out_ref[...] = rows_ref[...].astype(jnp.float32) + dot_nt(attended_ref[...], held_ref[...])


def tiles(size):
    return [slice(start, min(start + TILE, size)) for start in range(0, size, TILE)]


def gate_up_kernel(parts, me_ref, gate_ref, up_ref, gain_ref, *refs):
    sets, (out_ref, place_ref, row_ref, gate_held, up_held, gain_held, sems) = refs[:-7], refs[-7:]
    rows, width = sets[0].shape[1:]
    features, hidden = gate_ref.shape[1], gate_ref.shape[0]
    gain_copy = pltpu.make_async_copy(gain_ref, gain_held, sems.at[0])
    gain_copy.start()
    copies = []
    for t, tile in enumerate(tiles(hidden)):
        some = split_copies(gate_ref.at[tile], gate_held.at[tile], sems, 1 + 4 * t, 2)
        some += split_copies(up_ref.at[tile], up_held.at[tile], sems, 3 + 4 * t, 2)
        start_all(some)
        copies.append(some)
    me = me_ref[0]
    gain_copy.wait()
    for s, ref in enumerate(sets):
        held = [ref[j].astype(jnp.float32) for j in range(parts)]
        square = sum(jnp.sum(h * h, axis=1, keepdims=True) for h in held)
        scale = lax.rsqrt(square / features + EPSILON)
        for j in range(parts):
            place_ref[me ^ j] = held[j] * scale
        whole = jnp.concatenate([place_ref[p] for p in range(parts)], axis=1)
        row_ref[pl.ds(s * rows, rows), :] = (whole * gain_held[...]).astype(jnp.bfloat16)
    for t, tile in enumerate(tiles(hidden)):
        wait_all(copies[t])
        gate_val = dot_nt(row_ref[...], gate_held[tile])
        up_val = dot_nt(row_ref[...], up_held[tile])
        active = gate_val * jax.nn.sigmoid(ALPHA * gate_val) * (up_val + 1.0)
        out_ref[:, tile] = active.astype(jnp.bfloat16)


def down_kernel(me_ref, down_ref, *refs):
    own_ref, other_ref, held_ref, total_ref, sems = refs[-5:]
    actives = refs[:-5]
    rows, width = own_ref.shape
    copies = [
        split_copies(down_ref.at[me_ref[0] ^ j], held_ref.at[j], sems, PARTS * j, PARTS)
        for j in range(len(actives))
    ]
    for some in copies:
        start_all(some)
    for j, ref in enumerate(actives):
        wait_all(copies[j])
        for tile in tiles(width):
            term = jnp.dot(ref[...], held_ref[j, :, tile], preferred_element_type=jnp.float32)
            if j > 0:
                term = term + total_ref[:, tile]
            if j < len(actives) - 1:
                total_ref[:, tile] = term
            else:
                own_ref[:, tile] = term[:rows].astype(jnp.bfloat16)
                other_ref[:, tile] = term[rows:].astype(jnp.bfloat16)


def kernel_call(kernel, out_types, scalars, sources, *operands, scratch=()):
    in_vmem = pl.BlockSpec(memory_space=pltpu.VMEM)
    in_hbm = pl.BlockSpec(memory_space=pltpu.HBM)
    return pl.pallas_call(
        kernel,
        out_shape=[pltpu.VMEM(shape, dtype) for shape, dtype in out_types],
        in_specs=[pl.BlockSpec(memory_space=pltpu.SMEM)] * len(scalars)
        + [in_hbm] * len(sources)
        + [in_vmem] * len(operands),
        out_specs=[in_vmem] * len(out_types),
        scratch_shapes=scratch,
        compiler_params=pltpu.CompilerParams(vmem_limit_bytes=VMEM_LIMIT),
    )(
        *scalars,
        *[pltpu.with_memory_space_constraint(value, pltpu.HBM) for value in sources],
        *[pltpu.with_memory_space_constraint(value, pltpu.VMEM) for value in operands],
    )


def on_device(
    queries,
    new_kv,
    local_cache,
    remote_pool,
    page_index,
    lengths,
    sinks,
    out_weight,
    residual,
    norm_gain,
    routes,
    route_weights,
    expert_gate,
    expert_up,
    expert_down,
):
    groups = lax.axis_size("group")
    tp = lax.axis_size("tp")
    me_tp = lax.axis_index("tp")
    experts = groups // 2
    me_expert = lax.axis_index("group") // 2
    tp_scalar = me_tp.astype(jnp.int32).reshape(1)
    lane_count = remote_pool.shape[1]
    local_len = local_cache.shape[0]
    fetched = lax.all_to_all(
        remote_pool.reshape(groups, -1, lane_count),
        "group",
        split_axis=0,
        concat_axis=0,
        tiled=True,
    )
    page_len = fetched.shape[1]
    length = lengths[0]
    offsets = jnp.arange(page_len, dtype=jnp.int32)
    remote_pos = local_len + page_index[0][:, None] * page_len + offsets[None, :]
    page_valid = (remote_pos < length).astype(jnp.float32).reshape(1, -1)
    block_len, width = residual.shape
    positions = (length + jnp.arange(block_len, dtype=jnp.int32)).astype(jnp.float32)
    lane = jnp.arange(2 * HEAD, dtype=jnp.int32) % HEAD
    inverse = THETA ** (-2.0 * (lane % (HEAD // 2)).astype(jnp.float32) / HEAD)
    angles = positions[:, None] * inverse[None, :]
    sine = jnp.where(lane < HEAD // 2, -1.0, 1.0)[None, :] * jnp.sin(angles)
    hidden = expert_gate.shape[2]
    weight = out_weight.T.reshape(tp, width, out_weight.shape[0])
    gate, up = expert_gate[0].T, expert_up[0].T
    down = expert_down.reshape(tp, hidden, width)
    gain = norm_gain.reshape(1, tp * width)
    dma = pltpu.SemaphoreType.DMA
    in_vmem = pl.BlockSpec(memory_space=pltpu.VMEM)
    states = block_len * queries.shape[1] // HEAD
    rotated, state = pl.pallas_call(
        local_kernel,
        out_shape=[
            pltpu.VMEM((states, 2 * HEAD), jnp.bfloat16),
            pltpu.VMEM((states, 2 * HEAD), jnp.float32),
        ],
        in_specs=[pl.BlockSpec(memory_space=pltpu.SMEM)] + [in_vmem] * 5,
        out_specs=[in_vmem] * 2,
        compiler_params=pltpu.CompilerParams(vmem_limit_bytes=VMEM_LIMIT),
    )(
        sinks,
        *[pltpu.with_memory_space_constraint(value, pltpu.HBM) for value in (queries, new_kv, local_cache)],
        *[pltpu.with_memory_space_constraint(value, pltpu.VMEM) for value in (jnp.cos(angles), sine)],
    )
    attended, *others = kernel_call(
        page_kernel,
        [(queries.shape, jnp.bfloat16)] + [(residual.shape, jnp.bfloat16)] * (tp - 1),
        [tp_scalar],
        [weight],
        rotated,
        state,
        fetched.reshape(-1, lane_count),
        page_valid,
        scratch=[pltpu.VMEM((tp - 1, *weight.shape[1:]), jnp.bfloat16), dma((PARTS * (tp - 1),))],
    )
    arriving = [exchange(other, "tp", j + 1) for j, other in enumerate(others)]
    (own_state,) = kernel_call(
        own_columns_kernel,
        [(residual.shape, jnp.float32)],
        [tp_scalar],
        [weight, residual],
        attended,
        scratch=[
            pltpu.VMEM(weight.shape[1:], jnp.bfloat16),
            pltpu.VMEM(residual.shape, jnp.bfloat16),
            dma((PARTS + 1,)),
        ],
    )
    own_columns = own_state
    own_terms = own_state.astype(jnp.bfloat16)
    for term in arriving:
        own_state = own_state + term.astype(jnp.float32)
    state_sent = own_state.astype(jnp.bfloat16)
    if tp == 2:
        other_state = exchange(own_terms, "tp", 1).astype(jnp.float32) + others[0].astype(jnp.float32)
        own_blocks = [state_sent, other_state.astype(jnp.bfloat16)]
    else:
        own_blocks = [exchange(state_sent, "tp", j) for j in range(tp)]

    top_count = routes.shape[1]
    capacity = 5 * block_len * top_count // (4 * experts)
    half = experts // 2
    mixing = route_weights / jnp.sum(route_weights, axis=1, keepdims=True)
    plan = jnp.concatenate([routes.astype(jnp.float32), mixing], axis=1)
    far_plan = exchange(lax.optimization_barrier((plan, own_columns))[0], "group", experts)

    def slots(chosen_experts, weights):
        chosen = (chosen_experts ^ me_expert)[:, :, None] == jnp.arange(half, dtype=jnp.int32)
        member = jnp.any(chosen, axis=1)
        mix = jnp.sum(jnp.where(chosen, weights[:, :, None], 0.0), axis=1)
        earlier = jnp.arange(block_len)[:, None] > jnp.arange(block_len)[None, :]
        rank = jnp.dot(
            earlier.astype(jnp.bfloat16), member.astype(jnp.bfloat16), preferred_element_type=jnp.float32
        ).astype(jnp.int32)
        hit = member.T[:, None, :] & (
            rank.T[:, None, :] == jnp.arange(capacity, dtype=jnp.int32)[None, :, None]
        )
        pick = hit.astype(jnp.bfloat16).reshape(half * capacity, block_len)
        spread = jnp.where(hit, mix.T[:, None, :], 0.0).reshape(half * capacity, block_len)
        high = spread.astype(jnp.bfloat16)
        return pick, (high, (spread - high.astype(jnp.float32)).astype(jnp.bfloat16))

    own_pick, own_spread = slots(routes, mixing)
    far_pick, far_spread = slots(
        far_plan[:, :top_count].astype(jnp.int32), far_plan[:, top_count:]
    )

    def after(value, *earlier):
        return lax.optimization_barrier((value, *earlier))[0]

    def whole(value):
        return [exchange(value, "tp", j) for j in range(tp)]

    def picked(pick, values):
        parts = [
            jnp.dot(pick, value, preferred_element_type=jnp.float32)
            .astype(jnp.bfloat16)
            .reshape(half, capacity, width)
            for value in values
        ]
        return jnp.stack(parts, axis=1)

    def send_rows(rows):
        return [exchange(rows[d], "group", 2 * d) for d in range(half)]

    def blend(spread, pieces):
        rows = jnp.concatenate(pieces, axis=0)
        rows_first = (((0,), (0,)), ((), ()))
        return sum(
            lax.dot_general(part, rows, rows_first, preferred_element_type=jnp.float32)
            for part in spread
        )

    def activate(sets):
        rows = sets[0].shape[1]
        (active,) = kernel_call(
            functools.partial(gate_up_kernel, tp),
            [((2 * rows, hidden), jnp.bfloat16)],
            [tp_scalar],
            [gate, up, gain],
            *sets,
            scratch=[
                pltpu.VMEM((tp, rows, width), jnp.float32),
                pltpu.VMEM((2 * rows, tp * width), jnp.bfloat16),
                pltpu.VMEM(gate.shape, jnp.bfloat16),
                pltpu.VMEM(up.shape, jnp.bfloat16),
                pltpu.VMEM(gain.shape, jnp.float32),
                dma((1 + 4 * len(tiles(hidden)),)),
            ],
        )
        return active

    def project_down(actives):
        rows = actives[0].shape[0] // 2
        return kernel_call(
            down_kernel,
            [((rows, width), jnp.bfloat16)] * 2,
            [tp_scalar],
            [down],
            *actives,
            scratch=[
                pltpu.VMEM(down.shape, jnp.bfloat16),
                pltpu.VMEM((2 * rows, width), jnp.float32),
                dma((PARTS * tp,)),
            ],
        )

    def send_back(mine, theirs):
        summed = mine.astype(jnp.float32) + exchange(theirs, "group", 1).astype(jnp.float32)
        summed = summed.astype(jnp.bfloat16).reshape(half, capacity, width)
        return [exchange(summed[d], "group", 2 * d) for d in range(half)]

    far_blocks = whole(exchange(state_sent, "group", experts))
    own_pieces = send_rows(picked(own_pick, own_blocks))
    far_sent = picked(far_pick, far_blocks)
    far_pieces = send_rows(far_sent)
    own_rows = jnp.concatenate([after(piece, far_sent) for piece in own_pieces], axis=1)
    own_active = activate([own_rows, exchange(own_rows, "group", 1)])
    own_actives = whole(own_active)
    far_rows = jnp.concatenate([after(piece, own_active) for piece in far_pieces], axis=1)
    far_active = activate([far_rows, exchange(far_rows, "group", 1)])
    far_actives = whole(far_active)
    own_actives[0] = after(own_actives[0], far_active)
    own_back = send_back(*project_down(own_actives))
    far_back = send_back(*project_down(far_actives))
    far_sum = exchange(blend(far_spread, far_back).astype(jnp.bfloat16), "group", experts)
    total = own_state + blend(own_spread, own_back) + far_sum.astype(jnp.float32)
    return total.astype(jnp.bfloat16)


def solution(mesh):
    return jax.shard_map(
        on_device,
        mesh=mesh,
        in_specs=(
            P("group", "tp"),
            P("group", "tp"),
            P("group", "tp"),
            P("group", "tp"),
            P("group", None),
            P("group"),
            P("tp"),
            P("tp", None),
            P("group", "tp"),
            P(),
            P("group", None),
            P("group", None),
            P("group", None, "tp"),
            P("group", None, "tp"),
            P("group", None, "tp"),
        ),
        out_specs=P("group", "tp"),
        check_vma=False,
    )
```

```python
import functools

import jax
import jax.numpy as jnp
from jax import lax
from jax.experimental import pallas as pl
from jax.experimental.pallas import tpu as pltpu
from jax.sharding import PartitionSpec as P

HEAD = 64
TILE = 256
PARTS = 1
VMEM_LIMIT = 24 * 1024 * 1024


THETA = 150000.0
ALPHA = 1.702
EPSILON = 1e-05


def exchange(value, axis, offset):
    if offset == 0:
        return value
    size = lax.axis_size(axis)
    return lax.ppermute(value, axis, [(i, i ^ offset) for i in range(size)])


NT = (((1,), (1,)), ((), ()))


def dot_nt(left, right):
    return lax.dot_general(left, right, NT, preferred_element_type=jnp.float32)


def swapped_halves(value):
    lanes = value.shape[1]
    lane = lax.broadcasted_iota(jnp.int32, value.shape, 1)
    return jnp.where(
        lane % HEAD < HEAD // 2,
        pltpu.roll(value, lanes - HEAD // 2, 1),
        pltpu.roll(value, HEAD // 2, 1),
    )


def local_kernel(sink_ref, query_ref, kv_ref, local_ref, cos_ref, sin_ref, rotated_ref, state_ref):
    tokens = query_ref.shape[0]
    pair = 2 * HEAD
    kv_heads = kv_ref.shape[1] // pair
    group_size = query_ref.shape[1] // HEAD // kv_heads
    rows = group_size * tokens
    cosine, sine = cos_ref[...], sin_ref[...]
    low = lax.broadcasted_iota(jnp.int32, (tokens, pair), 1) < HEAD
    lane = lax.broadcasted_iota(jnp.int32, (rows, pair), 1)

    def rotated(value):
        return value * cosine + swapped_halves(value) * sine

    token_row = lax.broadcasted_iota(jnp.int32, (rows, tokens), 0) % tokens
    causal = lax.broadcasted_iota(jnp.int32, (rows, tokens), 1) <= token_row
    for h in range(kv_heads):
        lanes = slice(h * pair, (h + 1) * pair)
        own = kv_ref[:, lanes]
        own = jnp.where(low, rotated(own.astype(jnp.float32)).astype(jnp.bfloat16), own)
        queries = []
        for i in range(group_size // 2):
            start = (h * group_size + 2 * i) * HEAD
            both = rotated(query_ref[:, start : start + pair].astype(jnp.float32)) * HEAD**-0.5
            queries.append(jnp.where(low, both, 0.0))
            queries.append(jnp.where(low, pltpu.roll(both, HEAD, 1), 0.0))
        query = jnp.concatenate(queries, axis=0).astype(jnp.bfloat16)
        sink = jnp.concatenate(
            [jnp.full((tokens, 1), sink_ref[h * group_size + i]) for i in range(group_size)], axis=0
        )
        sources = [local_ref[:, lanes], own]
        scores = [dot_nt(query, source) for source in sources]
        scores[1] = jnp.where(causal, scores[1], -jnp.inf)
        row_max = sink
        for score in scores:
            row_max = jnp.maximum(row_max, jnp.max(score, axis=1, keepdims=True))
        denominator = jnp.exp(sink - row_max)
        blended = None
        for score, source in zip(scores, sources):
            weights = jnp.exp(score - row_max)
            denominator = denominator + jnp.sum(weights, axis=1, keepdims=True)
            term = jnp.dot(weights.astype(jnp.bfloat16), source, preferred_element_type=jnp.float32)
            blended = term if blended is None else blended + term
        place = slice(h * rows, (h + 1) * rows)
        rotated_ref[place, :] = query
        state_ref[place, :] = jnp.where(lane == 0, row_max, jnp.where(lane == 1, denominator, blended))


def split_copies(source, target, sems, first, parts):
    rows = source.shape[0]
    step = rows if parts == 1 else -(-rows // parts) // 16 * 16 + 16
    return [
        pltpu.make_async_copy(
            source.at[start : min(start + step, rows)],
            target.at[start : min(start + step, rows)],
            sems.at[first + i],
        )
        for i, start in enumerate(range(0, rows, step))
    ]


def start_all(copies):
    for copy in copies:
        copy.start()


def wait_all(copies):
    for copy in copies:
        copy.wait()


def page_kernel(me_ref, weight_ref, rotated_ref, state_ref, page_ref, valid_ref, attended_ref, *refs):
    other_refs, held_ref, sems = refs[:-2], refs[-2], refs[-1]
    copies = [
        split_copies(weight_ref.at[me_ref[0] ^ (j + 1)], held_ref.at[j], sems, PARTS * j, PARTS)
        for j in range(len(other_refs))
    ]
    for some in copies:
        start_all(some)
    tokens = attended_ref.shape[0]
    pair = 2 * HEAD
    kv_heads = page_ref.shape[1] // pair
    rows = rotated_ref.shape[0] // kv_heads
    group_size = rows // tokens
    low = lax.broadcasted_iota(jnp.int32, (tokens, pair), 1) < HEAD
    page_valid = valid_ref[...] > 0.0
    for h in range(kv_heads):
        place = slice(h * rows, (h + 1) * rows)
        source = page_ref[:, h * pair : (h + 1) * pair]
        state = state_ref[place, :]
        score = jnp.where(page_valid, dot_nt(rotated_ref[place, :], source), -jnp.inf)
        row_max = jnp.maximum(state[:, 0:1], jnp.max(score, axis=1, keepdims=True))
        weights = jnp.exp(score - row_max)
        kept = jnp.exp(state[:, 0:1] - row_max)
        denominator = state[:, 1:2] * kept + jnp.sum(weights, axis=1, keepdims=True)
        term = jnp.dot(weights.astype(jnp.bfloat16), source, preferred_element_type=jnp.float32)
        blended = (state * kept + term) / denominator
        for i in range(group_size // 2):
            even = blended[2 * i * tokens : (2 * i + 1) * tokens]
            odd = blended[(2 * i + 1) * tokens : (2 * i + 2) * tokens]
            start = (h * group_size + 2 * i) * HEAD
            attended_ref[:, start : start + pair] = jnp.where(
                low, pltpu.roll(even, HEAD, 1), odd
            ).astype(jnp.bfloat16)
    attended = attended_ref[...]
    for j, ref in enumerate(other_refs):
        wait_all(copies[j])
        ref[...] = dot_nt(attended, held_ref[j]).astype(jnp.bfloat16)


def own_columns_kernel(
    me_ref, weight_ref, residual_ref, attended_ref, out_ref, sent_ref, held_ref, rows_ref, sems
):
    copies = split_copies(weight_ref.at[me_ref[0]], held_ref, sems, 0, PARTS)
    copies.append(pltpu.make_async_copy(residual_ref, rows_ref, sems.at[PARTS]))
    start_all(copies)
    wait_all(copies)
    terms = rows_ref[...].astype(jnp.float32) + dot_nt(attended_ref[...], held_ref[...])
    out_ref[...] = terms
    sent_ref[...] = terms.astype(jnp.bfloat16)


def tiles(size):
    return [slice(start, min(start + TILE, size)) for start in range(0, size, TILE)]


def gate_up_kernel(parts, me_ref, gate_ref, up_ref, gain_ref, *refs):
    sets, (out_ref, place_ref, row_ref, gate_held, up_held, gain_held, sems) = refs[:-7], refs[-7:]
    rows, width = sets[0].shape[1:]
    features, hidden = gate_ref.shape[1], gate_ref.shape[0]
    gain_copy = pltpu.make_async_copy(gain_ref, gain_held, sems.at[0])
    gain_copy.start()
    copies = []
    for t, tile in enumerate(tiles(hidden)):
        some = split_copies(gate_ref.at[tile], gate_held.at[tile], sems, 1 + 4 * t, 2)
        some += split_copies(up_ref.at[tile], up_held.at[tile], sems, 3 + 4 * t, 2)
        start_all(some)
        copies.append(some)
    me = me_ref[0]
    gain_copy.wait()
    for s, ref in enumerate(sets):
        held = [ref[j].astype(jnp.float32) for j in range(parts)]
        square = sum(jnp.sum(h * h, axis=1, keepdims=True) for h in held)
        scale = lax.rsqrt(square / features + EPSILON)
        for j in range(parts):
            place_ref[me ^ j] = held[j] * scale
        whole = jnp.concatenate([place_ref[p] for p in range(parts)], axis=1)
        row_ref[pl.ds(s * rows, rows), :] = (whole * gain_held[...]).astype(jnp.bfloat16)
    for t, tile in enumerate(tiles(hidden)):
        wait_all(copies[t])
        gate_val = dot_nt(row_ref[...], gate_held[tile])
        up_val = dot_nt(row_ref[...], up_held[tile])
        active = gate_val * jax.nn.sigmoid(ALPHA * gate_val) * (up_val + 1.0)
        out_ref[:, tile] = active.astype(jnp.bfloat16)


def down_kernel(me_ref, down_ref, *refs):
    own_ref, other_ref, held_ref, total_ref, sems = refs[-5:]
    actives = refs[:-5]
    rows, width = own_ref.shape
    copies = [
        split_copies(down_ref.at[me_ref[0] ^ j], held_ref.at[j], sems, PARTS * j, PARTS)
        for j in range(len(actives))
    ]
    for some in copies:
        start_all(some)
    for j, ref in enumerate(actives):
        wait_all(copies[j])
        for tile in tiles(width):
            term = jnp.dot(ref[...], held_ref[j, :, tile], preferred_element_type=jnp.float32)
            if j > 0:
                term = term + total_ref[:, tile]
            if j < len(actives) - 1:
                total_ref[:, tile] = term
            else:
                own_ref[:, tile] = term[:rows].astype(jnp.bfloat16)
                other_ref[:, tile] = term[rows:].astype(jnp.bfloat16)


def kernel_call(kernel, out_types, scalars, sources, *operands, scratch=()):
    in_vmem = pl.BlockSpec(memory_space=pltpu.VMEM)
    in_hbm = pl.BlockSpec(memory_space=pltpu.HBM)
    return pl.pallas_call(
        kernel,
        out_shape=[pltpu.VMEM(shape, dtype) for shape, dtype in out_types],
        in_specs=[pl.BlockSpec(memory_space=pltpu.SMEM)] * len(scalars)
        + [in_hbm] * len(sources)
        + [in_vmem] * len(operands),
        out_specs=[in_vmem] * len(out_types),
        scratch_shapes=scratch,
        compiler_params=pltpu.CompilerParams(vmem_limit_bytes=VMEM_LIMIT),
    )(
        *scalars,
        *[pltpu.with_memory_space_constraint(value, pltpu.HBM) for value in sources],
        *[pltpu.with_memory_space_constraint(value, pltpu.VMEM) for value in operands],
    )


def on_device(
    queries,
    new_kv,
    local_cache,
    remote_pool,
    page_index,
    lengths,
    sinks,
    out_weight,
    residual,
    norm_gain,
    routes,
    route_weights,
    expert_gate,
    expert_up,
    expert_down,
):
    groups = lax.axis_size("group")
    tp = lax.axis_size("tp")
    me_tp = lax.axis_index("tp")
    experts = groups // 2
    me_expert = lax.axis_index("group") // 2
    tp_scalar = me_tp.astype(jnp.int32).reshape(1)
    lane_count = remote_pool.shape[1]
    local_len = local_cache.shape[0]
    fetched = lax.all_to_all(
        remote_pool.reshape(groups, -1, lane_count),
        "group",
        split_axis=0,
        concat_axis=0,
        tiled=True,
    )
    page_len = fetched.shape[1]
    length = lengths[0]
    offsets = jnp.arange(page_len, dtype=jnp.int32)
    remote_pos = local_len + page_index[0][:, None] * page_len + offsets[None, :]
    page_valid = (remote_pos < length).astype(jnp.float32).reshape(1, -1)
    block_len, width = residual.shape
    positions = (length + jnp.arange(block_len, dtype=jnp.int32)).astype(jnp.float32)
    lane = jnp.arange(2 * HEAD, dtype=jnp.int32) % HEAD
    inverse = THETA ** (-2.0 * (lane % (HEAD // 2)).astype(jnp.float32) / HEAD)
    angles = positions[:, None] * inverse[None, :]
    sine = jnp.where(lane < HEAD // 2, -1.0, 1.0)[None, :] * jnp.sin(angles)
    hidden = expert_gate.shape[2]
    weight = out_weight.T.reshape(tp, width, out_weight.shape[0])
    gate, up = expert_gate[0].T, expert_up[0].T
    down = expert_down.reshape(tp, hidden, width)
    gain = norm_gain.reshape(1, tp * width)
    dma = pltpu.SemaphoreType.DMA
    in_vmem = pl.BlockSpec(memory_space=pltpu.VMEM)
    states = block_len * queries.shape[1] // HEAD
    rotated, state = pl.pallas_call(
        local_kernel,
        out_shape=[
            pltpu.VMEM((states, 2 * HEAD), jnp.bfloat16),
            pltpu.VMEM((states, 2 * HEAD), jnp.float32),
        ],
        in_specs=[pl.BlockSpec(memory_space=pltpu.SMEM)] + [in_vmem] * 5,
        out_specs=[in_vmem] * 2,
        compiler_params=pltpu.CompilerParams(vmem_limit_bytes=VMEM_LIMIT),
    )(
        sinks,
        *[pltpu.with_memory_space_constraint(value, pltpu.HBM) for value in (queries, new_kv, local_cache)],
        *[pltpu.with_memory_space_constraint(value, pltpu.VMEM) for value in (jnp.cos(angles), sine)],
    )
    attended, *others = kernel_call(
        page_kernel,
        [(queries.shape, jnp.bfloat16)] + [(residual.shape, jnp.bfloat16)] * (tp - 1),
        [tp_scalar],
        [weight],
        rotated,
        state,
        fetched.reshape(-1, lane_count),
        page_valid,
        scratch=[pltpu.VMEM((tp - 1, *weight.shape[1:]), jnp.bfloat16), dma((PARTS * (tp - 1),))],
    )
    arriving = [exchange(other, "tp", j + 1) for j, other in enumerate(others)]
    own_state, own_terms = kernel_call(
        own_columns_kernel,
        [(residual.shape, jnp.float32), (residual.shape, jnp.bfloat16)],
        [tp_scalar],
        [weight, residual],
        lax.optimization_barrier((attended, gain))[0],
        scratch=[
            pltpu.VMEM(weight.shape[1:], jnp.bfloat16),
            pltpu.VMEM(residual.shape, jnp.bfloat16),
            dma((PARTS + 1,)),
        ],
    )
    for term in arriving:
        own_state = own_state + term.astype(jnp.float32)
    state_sent = own_state.astype(jnp.bfloat16)
    if tp == 2:
        own_terms = lax.optimization_barrier((own_terms, state_sent))[0]
        other_state = exchange(own_terms, "tp", 1).astype(jnp.float32) + others[0].astype(jnp.float32)
        own_blocks = [state_sent, other_state.astype(jnp.bfloat16)]
    else:
        own_blocks = [exchange(state_sent, "tp", j) for j in range(tp)]

    top_count = routes.shape[1]
    capacity = 5 * block_len * top_count // (4 * experts)
    half = experts // 2
    mixing = route_weights / jnp.sum(route_weights, axis=1, keepdims=True)
    plan = jnp.concatenate([routes.astype(jnp.float32), mixing], axis=1)
    far_plan = exchange(lax.optimization_barrier((plan, own_blocks[-1]))[0], "group", experts)

    def slots(chosen_experts, weights):
        chosen = (chosen_experts ^ me_expert)[:, :, None] == jnp.arange(half, dtype=jnp.int32)
        member = jnp.any(chosen, axis=1)
        mix = jnp.sum(jnp.where(chosen, weights[:, :, None], 0.0), axis=1)
        earlier = jnp.arange(block_len)[:, None] > jnp.arange(block_len)[None, :]
        rank = jnp.dot(
            earlier.astype(jnp.bfloat16), member.astype(jnp.bfloat16), preferred_element_type=jnp.float32
        ).astype(jnp.int32)
        hit = member.T[:, None, :] & (
            rank.T[:, None, :] == jnp.arange(capacity, dtype=jnp.int32)[None, :, None]
        )
        pick = hit.astype(jnp.bfloat16).reshape(half * capacity, block_len)
        spread = jnp.where(hit, mix.T[:, None, :], 0.0).reshape(half * capacity, block_len)
        high = spread.astype(jnp.bfloat16)
        return pick, (high, (spread - high.astype(jnp.float32)).astype(jnp.bfloat16))

    own_pick, own_spread = slots(routes, mixing)
    far_pick, far_spread = slots(
        far_plan[:, :top_count].astype(jnp.int32), far_plan[:, top_count:]
    )

    def after(value, *earlier):
        return lax.optimization_barrier((value, *earlier))[0]

    def whole(value):
        return [exchange(value, "tp", j) for j in range(tp)]

    def picked(pick, values):
        parts = [
            jnp.dot(pick, value, preferred_element_type=jnp.float32)
            .astype(jnp.bfloat16)
            .reshape(half, capacity, width)
            for value in values
        ]
        return jnp.stack(parts, axis=1)

    def send_rows(rows):
        return [exchange(rows[d], "group", 2 * d) for d in range(half)]

    def blend(spread, pieces):
        rows = jnp.concatenate(pieces, axis=0)
        rows_first = (((0,), (0,)), ((), ()))
        return sum(
            lax.dot_general(part, rows, rows_first, preferred_element_type=jnp.float32)
            for part in spread
        )

    def activate(sets):
        rows = sets[0].shape[1]
        (active,) = kernel_call(
            functools.partial(gate_up_kernel, tp),
            [((2 * rows, hidden), jnp.bfloat16)],
            [tp_scalar],
            [gate, up, gain],
            *sets,
            scratch=[
                pltpu.VMEM((tp, rows, width), jnp.float32),
                pltpu.VMEM((2 * rows, tp * width), jnp.bfloat16),
                pltpu.VMEM(gate.shape, jnp.bfloat16),
                pltpu.VMEM(up.shape, jnp.bfloat16),
                pltpu.VMEM(gain.shape, jnp.float32),
                dma((1 + 4 * len(tiles(hidden)),)),
            ],
        )
        return active

    def project_down(actives):
        rows = actives[0].shape[0] // 2
        return kernel_call(
            down_kernel,
            [((rows, width), jnp.bfloat16)] * 2,
            [tp_scalar],
            [down],
            *actives,
            scratch=[
                pltpu.VMEM(down.shape, jnp.bfloat16),
                pltpu.VMEM((2 * rows, width), jnp.float32),
                dma((PARTS * tp,)),
            ],
        )

    def add_halves(mine, theirs):
        summed = mine.astype(jnp.float32) + exchange(theirs, "group", 1).astype(jnp.float32)
        return summed.astype(jnp.bfloat16).reshape(half, capacity, width)

    far_blocks = whole(exchange(state_sent, "group", experts))
    own_pieces = send_rows(picked(own_pick, own_blocks))
    far_sent = picked(far_pick, far_blocks)
    far_pieces = send_rows(far_sent)
    own_rows = jnp.concatenate([after(piece, far_sent) for piece in own_pieces], axis=1)
    own_active = activate([own_rows, exchange(own_rows, "group", 1)])
    own_actives = whole(own_active)
    far_rows = jnp.concatenate([after(piece, own_active) for piece in far_pieces], axis=1)
    far_active = activate([far_rows, exchange(far_rows, "group", 1)])
    far_actives = whole(far_active)
    own_actives[0] = after(own_actives[0], far_active)
    own_out = project_down(own_actives)
    far_actives[0] = after(far_actives[0], own_out[0])
    far_out = add_halves(*project_down(far_actives))
    own_out = add_halves(*own_out)
    far_sum = blend(far_spread, send_rows(far_out)).astype(jnp.bfloat16)
    own_back = send_rows(after(own_out, far_sum))
    far_sum = exchange(far_sum, "group", experts)
    own_back = [after(piece, far_sum) for piece in own_back]
    total = own_state + blend(own_spread, own_back) + far_sum.astype(jnp.float32)
    return total.astype(jnp.bfloat16)


def solution(mesh):
    return jax.shard_map(
        on_device,
        mesh=mesh,
        in_specs=(
            P("group", "tp"),
            P("group", "tp"),
            P("group", "tp"),
            P("group", "tp"),
            P("group", None),
            P("group"),
            P("tp"),
            P("tp", None),
            P("group", "tp"),
            P(),
            P("group", None),
            P("group", None),
            P("group", None, "tp"),
            P("group", None, "tp"),
            P("group", None, "tp"),
        ),
        out_specs=P("group", "tp"),
        check_vma=False,
    )
```

```python
import functools

import jax
import jax.numpy as jnp
from jax import lax
from jax.experimental import pallas as pl
from jax.experimental.pallas import tpu as pltpu
from jax.sharding import PartitionSpec as P

HEAD = 64
TILE = 256
PARTS = 1
VMEM_LIMIT = 24 * 1024 * 1024


THETA = 150000.0
ALPHA = 1.702
EPSILON = 1e-05


def exchange(value, axis, offset):
    if offset == 0:
        return value
    size = lax.axis_size(axis)
    return lax.ppermute(value, axis, [(i, i ^ offset) for i in range(size)])


NT = (((1,), (1,)), ((), ()))


def dot_nt(left, right):
    return lax.dot_general(left, right, NT, preferred_element_type=jnp.float32)


def swapped_halves(value):
    lanes = value.shape[1]
    lane = lax.broadcasted_iota(jnp.int32, value.shape, 1)
    return jnp.where(
        lane % HEAD < HEAD // 2,
        pltpu.roll(value, lanes - HEAD // 2, 1),
        pltpu.roll(value, HEAD // 2, 1),
    )


def local_kernel(sink_ref, query_ref, kv_ref, local_ref, cos_ref, sin_ref, rotated_ref, state_ref):
    tokens = query_ref.shape[0]
    pair = 2 * HEAD
    kv_heads = kv_ref.shape[1] // pair
    group_size = query_ref.shape[1] // HEAD // kv_heads
    rows = group_size * tokens
    cosine, sine = cos_ref[...], sin_ref[...]
    low = lax.broadcasted_iota(jnp.int32, (tokens, pair), 1) < HEAD
    lane = lax.broadcasted_iota(jnp.int32, (rows, pair), 1)

    def rotated(value):
        return value * cosine + swapped_halves(value) * sine

    token_row = lax.broadcasted_iota(jnp.int32, (rows, tokens), 0) % tokens
    causal = lax.broadcasted_iota(jnp.int32, (rows, tokens), 1) <= token_row
    for h in range(kv_heads):
        lanes = slice(h * pair, (h + 1) * pair)
        own = kv_ref[:, lanes]
        own = jnp.where(low, rotated(own.astype(jnp.float32)).astype(jnp.bfloat16), own)
        queries = []
        for i in range(group_size // 2):
            start = (h * group_size + 2 * i) * HEAD
            both = rotated(query_ref[:, start : start + pair].astype(jnp.float32)) * HEAD**-0.5
            queries.append(jnp.where(low, both, 0.0))
            queries.append(jnp.where(low, pltpu.roll(both, HEAD, 1), 0.0))
        query = jnp.concatenate(queries, axis=0).astype(jnp.bfloat16)
        sink = jnp.concatenate(
            [jnp.full((tokens, 1), sink_ref[h * group_size + i]) for i in range(group_size)], axis=0
        )
        sources = [local_ref[:, lanes], own]
        scores = [dot_nt(query, source) for source in sources]
        scores[1] = jnp.where(causal, scores[1], -jnp.inf)
        row_max = sink
        for score in scores:
            row_max = jnp.maximum(row_max, jnp.max(score, axis=1, keepdims=True))
        denominator = jnp.exp(sink - row_max)
        blended = None
        for score, source in zip(scores, sources):
            weights = jnp.exp(score - row_max)
            denominator = denominator + jnp.sum(weights, axis=1, keepdims=True)
            term = jnp.dot(weights.astype(jnp.bfloat16), source, preferred_element_type=jnp.float32)
            blended = term if blended is None else blended + term
        place = slice(h * rows, (h + 1) * rows)
        rotated_ref[place, :] = query
        state_ref[place, :] = jnp.where(lane == 0, row_max, jnp.where(lane == 1, denominator, blended))


def split_copies(source, target, sems, first, parts):
    rows = source.shape[0]
    step = rows if parts == 1 else -(-rows // parts) // 16 * 16 + 16
    return [
        pltpu.make_async_copy(
            source.at[start : min(start + step, rows)],
            target.at[start : min(start + step, rows)],
            sems.at[first + i],
        )
        for i, start in enumerate(range(0, rows, step))
    ]


def start_all(copies):
    for copy in copies:
        copy.start()


def wait_all(copies):
    for copy in copies:
        copy.wait()


def page_kernel(me_ref, weight_ref, rotated_ref, state_ref, page_ref, valid_ref, attended_ref, *refs):
    other_refs, held_ref, sems = refs[:-2], refs[-2], refs[-1]
    copies = [
        split_copies(weight_ref.at[me_ref[0] ^ (j + 1)], held_ref.at[j], sems, PARTS * j, PARTS)
        for j in range(len(other_refs))
    ]
    for some in copies:
        start_all(some)
    tokens = attended_ref.shape[0]
    pair = 2 * HEAD
    kv_heads = page_ref.shape[1] // pair
    rows = rotated_ref.shape[0] // kv_heads
    group_size = rows // tokens
    low = lax.broadcasted_iota(jnp.int32, (tokens, pair), 1) < HEAD
    page_valid = valid_ref[...] > 0.0
    for h in range(kv_heads):
        place = slice(h * rows, (h + 1) * rows)
        source = page_ref[:, h * pair : (h + 1) * pair]
        state = state_ref[place, :]
        score = jnp.where(page_valid, dot_nt(rotated_ref[place, :], source), -jnp.inf)
        row_max = jnp.maximum(state[:, 0:1], jnp.max(score, axis=1, keepdims=True))
        weights = jnp.exp(score - row_max)
        kept = jnp.exp(state[:, 0:1] - row_max)
        denominator = state[:, 1:2] * kept + jnp.sum(weights, axis=1, keepdims=True)
        term = jnp.dot(weights.astype(jnp.bfloat16), source, preferred_element_type=jnp.float32)
        blended = (state * kept + term) / denominator
        for i in range(group_size // 2):
            even = blended[2 * i * tokens : (2 * i + 1) * tokens]
            odd = blended[(2 * i + 1) * tokens : (2 * i + 2) * tokens]
            start = (h * group_size + 2 * i) * HEAD
            attended_ref[:, start : start + pair] = jnp.where(
                low, pltpu.roll(even, HEAD, 1), odd
            ).astype(jnp.bfloat16)
    attended = attended_ref[...]
    for j, ref in enumerate(other_refs):
        wait_all(copies[j])
        ref[...] = dot_nt(attended, held_ref[j]).astype(jnp.bfloat16)


def own_columns_kernel(me_ref, weight_ref, residual_ref, attended_ref, out_ref, held_ref, rows_ref, sems):
    copies = split_copies(weight_ref.at[me_ref[0]], held_ref, sems, 0, PARTS)
    copies.append(pltpu.make_async_copy(residual_ref, rows_ref, sems.at[PARTS]))
    start_all(copies)
    wait_all(copies)
    out_ref[...] = rows_ref[...].astype(jnp.float32) + dot_nt(attended_ref[...], held_ref[...])


def tiles(size):
    return [slice(start, min(start + TILE, size)) for start in range(0, size, TILE)]


def gate_up_kernel(parts, me_ref, gate_ref, up_ref, gain_ref, *refs):
    sets, (out_ref, place_ref, row_ref, gate_held, up_held, gain_held, sems) = refs[:-7], refs[-7:]
    rows = sets[0].shape[-2]
    if len(sets[0].shape) == 2:
        sets = [sets[s : s + parts] for s in range(0, len(sets), parts)]
    features, hidden = gate_ref.shape[1], gate_ref.shape[0]
    gain_copy = pltpu.make_async_copy(gain_ref, gain_held, sems.at[0])
    gain_copy.start()
    copies = []
    for t, tile in enumerate(tiles(hidden)):
        some = split_copies(gate_ref.at[tile], gate_held.at[tile], sems, 1 + 4 * t, 2)
        some += split_copies(up_ref.at[tile], up_held.at[tile], sems, 3 + 4 * t, 2)
        start_all(some)
        copies.append(some)
    me = me_ref[0]
    gain_copy.wait()
    for s, ref in enumerate(sets):
        held = [(ref[j][...] if isinstance(ref, tuple) else ref[j]).astype(jnp.float32) for j in range(parts)]
        square = sum(jnp.sum(h * h, axis=1, keepdims=True) for h in held)
        scale = lax.rsqrt(square / features + EPSILON)
        for j in range(parts):
            place_ref[me ^ j] = held[j] * scale
        whole = jnp.concatenate([place_ref[p] for p in range(parts)], axis=1)
        row_ref[pl.ds(s * rows, rows), :] = (whole * gain_held[...]).astype(jnp.bfloat16)
    for t, tile in enumerate(tiles(hidden)):
        wait_all(copies[t])
        gate_val = dot_nt(row_ref[...], gate_held[tile])
        up_val = dot_nt(row_ref[...], up_held[tile])
        active = gate_val * jax.nn.sigmoid(ALPHA * gate_val) * (up_val + 1.0)
        out_ref[:, tile] = active.astype(jnp.bfloat16)


def down_kernel(me_ref, down_ref, *refs):
    own_ref, other_ref, held_ref, total_ref, sems = refs[-5:]
    actives = refs[:-5]
    rows, width = own_ref.shape
    copies = [
        split_copies(down_ref.at[me_ref[0] ^ j], held_ref.at[j], sems, PARTS * j, PARTS)
        for j in range(len(actives))
    ]
    for some in copies:
        start_all(some)
    for j, ref in enumerate(actives):
        wait_all(copies[j])
        for tile in tiles(width):
            term = jnp.dot(ref[...], held_ref[j, :, tile], preferred_element_type=jnp.float32)
            if j > 0:
                term = term + total_ref[:, tile]
            if j < len(actives) - 1:
                total_ref[:, tile] = term
            else:
                own_ref[:, tile] = term[:rows].astype(jnp.bfloat16)
                other_ref[:, tile] = term[rows:].astype(jnp.bfloat16)


def kernel_call(kernel, out_types, scalars, sources, *operands, scratch=()):
    in_vmem = pl.BlockSpec(memory_space=pltpu.VMEM)
    in_hbm = pl.BlockSpec(memory_space=pltpu.HBM)
    return pl.pallas_call(
        kernel,
        out_shape=[pltpu.VMEM(shape, dtype) for shape, dtype in out_types],
        in_specs=[pl.BlockSpec(memory_space=pltpu.SMEM)] * len(scalars)
        + [in_hbm] * len(sources)
        + [in_vmem] * len(operands),
        out_specs=[in_vmem] * len(out_types),
        scratch_shapes=scratch,
        compiler_params=pltpu.CompilerParams(vmem_limit_bytes=VMEM_LIMIT),
    )(
        *scalars,
        *[pltpu.with_memory_space_constraint(value, pltpu.HBM) for value in sources],
        *[pltpu.with_memory_space_constraint(value, pltpu.VMEM) for value in operands],
    )


def on_device(
    queries,
    new_kv,
    local_cache,
    remote_pool,
    page_index,
    lengths,
    sinks,
    out_weight,
    residual,
    norm_gain,
    routes,
    route_weights,
    expert_gate,
    expert_up,
    expert_down,
):
    groups = lax.axis_size("group")
    tp = lax.axis_size("tp")
    me_tp = lax.axis_index("tp")
    experts = groups // 2
    me_expert = lax.axis_index("group") // 2
    tp_scalar = me_tp.astype(jnp.int32).reshape(1)
    lane_count = remote_pool.shape[1]
    local_len = local_cache.shape[0]
    fetched = lax.all_to_all(
        remote_pool.reshape(groups, -1, lane_count),
        "group",
        split_axis=0,
        concat_axis=0,
        tiled=True,
    )
    page_len = fetched.shape[1]
    length = lengths[0]
    offsets = jnp.arange(page_len, dtype=jnp.int32)
    remote_pos = local_len + page_index[0][:, None] * page_len + offsets[None, :]
    page_valid = (remote_pos < length).astype(jnp.float32).reshape(1, -1)
    block_len, width = residual.shape
    positions = (length + jnp.arange(block_len, dtype=jnp.int32)).astype(jnp.float32)
    lane = jnp.arange(2 * HEAD, dtype=jnp.int32) % HEAD
    inverse = THETA ** (-2.0 * (lane % (HEAD // 2)).astype(jnp.float32) / HEAD)
    angles = positions[:, None] * inverse[None, :]
    sine = jnp.where(lane < HEAD // 2, -1.0, 1.0)[None, :] * jnp.sin(angles)
    hidden = expert_gate.shape[2]
    weight = out_weight.T.reshape(tp, width, out_weight.shape[0])
    gate, up = expert_gate[0].T, expert_up[0].T
    down = expert_down.reshape(tp, hidden, width)
    gain = norm_gain.reshape(1, tp * width)
    dma = pltpu.SemaphoreType.DMA
    in_vmem = pl.BlockSpec(memory_space=pltpu.VMEM)
    states = block_len * queries.shape[1] // HEAD
    rotated, state = pl.pallas_call(
        local_kernel,
        out_shape=[
            pltpu.VMEM((states, 2 * HEAD), jnp.bfloat16),
            pltpu.VMEM((states, 2 * HEAD), jnp.float32),
        ],
        in_specs=[pl.BlockSpec(memory_space=pltpu.SMEM)] + [in_vmem] * 5,
        out_specs=[in_vmem] * 2,
        compiler_params=pltpu.CompilerParams(vmem_limit_bytes=VMEM_LIMIT),
    )(
        sinks,
        *[pltpu.with_memory_space_constraint(value, pltpu.HBM) for value in (queries, new_kv, local_cache)],
        *[pltpu.with_memory_space_constraint(value, pltpu.VMEM) for value in (jnp.cos(angles), sine)],
    )
    attended, *others = kernel_call(
        page_kernel,
        [(queries.shape, jnp.bfloat16)] + [(residual.shape, jnp.bfloat16)] * (tp - 1),
        [tp_scalar],
        [weight],
        rotated,
        state,
        fetched.reshape(-1, lane_count),
        page_valid,
        scratch=[pltpu.VMEM((tp - 1, *weight.shape[1:]), jnp.bfloat16), dma((PARTS * (tp - 1),))],
    )
    arriving = [exchange(other, "tp", j + 1) for j, other in enumerate(others)]
    (own_state,) = kernel_call(
        own_columns_kernel,
        [(residual.shape, jnp.float32)],
        [tp_scalar],
        [weight, residual],
        lax.optimization_barrier((attended, gain))[0],
        scratch=[
            pltpu.VMEM(weight.shape[1:], jnp.bfloat16),
            pltpu.VMEM(residual.shape, jnp.bfloat16),
            dma((PARTS + 1,)),
        ],
    )
    for term in arriving:
        own_state = own_state + term.astype(jnp.float32)
    state_sent = own_state.astype(jnp.bfloat16)

    top_count = routes.shape[1]
    capacity = 5 * block_len * top_count // (4 * experts)
    half = experts // 2
    mixing = route_weights / jnp.sum(route_weights, axis=1, keepdims=True)
    plan = jnp.concatenate([routes.astype(jnp.float32), mixing], axis=1)
    far_plan = exchange(lax.optimization_barrier((plan, state_sent))[0], "group", experts)

    def slots(chosen_experts, weights):
        chosen = (chosen_experts ^ me_expert)[:, :, None] == jnp.arange(half, dtype=jnp.int32)
        member = jnp.any(chosen, axis=1)
        mix = jnp.sum(jnp.where(chosen, weights[:, :, None], 0.0), axis=1)
        earlier = jnp.arange(block_len)[:, None] > jnp.arange(block_len)[None, :]
        rank = jnp.dot(
            earlier.astype(jnp.bfloat16), member.astype(jnp.bfloat16), preferred_element_type=jnp.float32
        ).astype(jnp.int32)
        hit = member.T[:, None, :] & (
            rank.T[:, None, :] == jnp.arange(capacity, dtype=jnp.int32)[None, :, None]
        )
        pick = hit.astype(jnp.bfloat16).reshape(half * capacity, block_len)
        spread = jnp.where(hit, mix.T[:, None, :], 0.0).reshape(half * capacity, block_len)
        high = spread.astype(jnp.bfloat16)
        return pick, (high, (spread - high.astype(jnp.float32)).astype(jnp.bfloat16))

    own_pick, own_spread = slots(routes, mixing)

    def after(value, *earlier):
        return lax.optimization_barrier((value, *earlier))[0]

    def whole(value):
        return [exchange(value, "tp", j) for j in range(tp)]

    def picked(pick, values):
        parts = [
            jnp.dot(pick, value, preferred_element_type=jnp.float32)
            .astype(jnp.bfloat16)
            .reshape(half, capacity, width)
            for value in values
        ]
        return jnp.stack(parts, axis=1)

    def send_rows(rows):
        return [exchange(rows[d], "group", 2 * d) for d in range(half)]

    def blend(spread, pieces):
        rows = jnp.concatenate(pieces, axis=0)
        rows_first = (((0,), (0,)), ((), ()))
        return sum(
            lax.dot_general(part, rows, rows_first, preferred_element_type=jnp.float32)
            for part in spread
        )

    def activate(sets):
        rows = sets[0].shape[-2]
        (active,) = kernel_call(
            functools.partial(gate_up_kernel, tp),
            [((2 * rows, hidden), jnp.bfloat16)],
            [tp_scalar],
            [gate, up, gain],
            *sets,
            scratch=[
                pltpu.VMEM((tp, rows, width), jnp.float32),
                pltpu.VMEM((2 * rows, tp * width), jnp.bfloat16),
                pltpu.VMEM(gate.shape, jnp.bfloat16),
                pltpu.VMEM(up.shape, jnp.bfloat16),
                pltpu.VMEM(gain.shape, jnp.float32),
                dma((1 + 4 * len(tiles(hidden)),)),
            ],
        )
        return active

    def project_down(actives):
        rows = actives[0].shape[0] // 2
        return kernel_call(
            down_kernel,
            [((rows, width), jnp.bfloat16)] * 2,
            [tp_scalar],
            [down],
            *actives,
            scratch=[
                pltpu.VMEM(down.shape, jnp.bfloat16),
                pltpu.VMEM((2 * rows, width), jnp.float32),
                dma((PARTS * tp,)),
            ],
        )

    def add_halves(mine, theirs):
        summed = mine.astype(jnp.float32) + exchange(theirs, "group", 1).astype(jnp.float32)
        return summed.astype(jnp.bfloat16).reshape(half, capacity, width)

    far_state = exchange(state_sent, "group", experts)
    own_pieces = send_rows(picked(own_pick, [state_sent]))
    own_rows = jnp.concatenate([after(piece[0], far_state) for piece in own_pieces], axis=0)
    far_plan = after(far_plan, own_rows)
    far_pick, far_spread = slots(
        far_plan[:, :top_count].astype(jnp.int32), far_plan[:, top_count:]
    )
    own_rows = whole(own_rows)
    far_sent = picked(far_pick, whole(far_state))
    far_pieces = send_rows(far_sent)
    own_pairs = [own_rows[0], *[after(rows, far_pieces[1]) for rows in own_rows[1:]]]
    own_active = activate([*own_rows, *[exchange(rows, "group", 1) for rows in own_pairs]])
    own_actives = whole(own_active)
    far_rows = jnp.concatenate([after(piece, own_active) for piece in far_pieces], axis=1)
    far_active = activate([far_rows, exchange(far_rows, "group", 1)])
    far_actives = whole(far_active)
    own_actives[0] = after(own_actives[0], far_active)
    own_out = project_down(own_actives)
    far_actives[0] = after(far_actives[0], own_out[0])
    far_out = add_halves(*project_down(far_actives))
    own_out = add_halves(*own_out)
    far_sum = blend(far_spread, send_rows(far_out)).astype(jnp.bfloat16)
    far_sum = exchange(far_sum, "group", experts)
    total = own_state + blend(own_spread, send_rows(own_out)) + far_sum.astype(jnp.float32)
    return total.astype(jnp.bfloat16)


def solution(mesh):
    return jax.shard_map(
        on_device,
        mesh=mesh,
        in_specs=(
            P("group", "tp"),
            P("group", "tp"),
            P("group", "tp"),
            P("group", "tp"),
            P("group", None),
            P("group"),
            P("tp"),
            P("tp", None),
            P("group", "tp"),
            P(),
            P("group", None),
            P("group", None),
            P("group", None, "tp"),
            P("group", None, "tp"),
            P("group", None, "tp"),
        ),
        out_specs=P("group", "tp"),
        check_vma=False,
    )
```

```python
import functools

import jax
import jax.numpy as jnp
from jax import lax
from jax.experimental import pallas as pl
from jax.experimental.pallas import tpu as pltpu
from jax.sharding import PartitionSpec as P

HEAD = 64
TILE = 256
PARTS = 1
VMEM_LIMIT = 24 * 1024 * 1024


THETA = 150000.0
ALPHA = 1.702
EPSILON = 1e-05


def exchange(value, axis, offset):
    if offset == 0:
        return value
    size = lax.axis_size(axis)
    return lax.ppermute(value, axis, [(i, i ^ offset) for i in range(size)])


NT = (((1,), (1,)), ((), ()))


def dot_nt(left, right):
    return lax.dot_general(left, right, NT, preferred_element_type=jnp.float32)


def swapped_halves(value):
    lanes = value.shape[1]
    lane = lax.broadcasted_iota(jnp.int32, value.shape, 1)
    return jnp.where(
        lane % HEAD < HEAD // 2,
        pltpu.roll(value, lanes - HEAD // 2, 1),
        pltpu.roll(value, HEAD // 2, 1),
    )


def local_kernel(sink_ref, query_ref, kv_ref, local_ref, cos_ref, sin_ref, rotated_ref, state_ref):
    tokens = query_ref.shape[0]
    pair = 2 * HEAD
    kv_heads = kv_ref.shape[1] // pair
    group_size = query_ref.shape[1] // HEAD // kv_heads
    rows = group_size * tokens
    cosine, sine = cos_ref[...], sin_ref[...]
    low = lax.broadcasted_iota(jnp.int32, (tokens, pair), 1) < HEAD
    lane = lax.broadcasted_iota(jnp.int32, (rows, pair), 1)

    def rotated(value):
        return value * cosine + swapped_halves(value) * sine

    token_row = lax.broadcasted_iota(jnp.int32, (rows, tokens), 0) % tokens
    causal = lax.broadcasted_iota(jnp.int32, (rows, tokens), 1) <= token_row
    for h in range(kv_heads):
        lanes = slice(h * pair, (h + 1) * pair)
        own = kv_ref[:, lanes]
        own = jnp.where(low, rotated(own.astype(jnp.float32)).astype(jnp.bfloat16), own)
        queries = []
        for i in range(group_size // 2):
            start = (h * group_size + 2 * i) * HEAD
            both = rotated(query_ref[:, start : start + pair].astype(jnp.float32)) * HEAD**-0.5
            queries.append(jnp.where(low, both, 0.0))
            queries.append(jnp.where(low, pltpu.roll(both, HEAD, 1), 0.0))
        query = jnp.concatenate(queries, axis=0).astype(jnp.bfloat16)
        sink = jnp.concatenate(
            [jnp.full((tokens, 1), sink_ref[h * group_size + i]) for i in range(group_size)], axis=0
        )
        sources = [local_ref[:, lanes], own]
        scores = [dot_nt(query, source) for source in sources]
        scores[1] = jnp.where(causal, scores[1], -jnp.inf)
        row_max = sink
        for score in scores:
            row_max = jnp.maximum(row_max, jnp.max(score, axis=1, keepdims=True))
        denominator = jnp.exp(sink - row_max)
        blended = None
        for score, source in zip(scores, sources):
            weights = jnp.exp(score - row_max)
            denominator = denominator + jnp.sum(weights, axis=1, keepdims=True)
            term = jnp.dot(weights.astype(jnp.bfloat16), source, preferred_element_type=jnp.float32)
            blended = term if blended is None else blended + term
        place = slice(h * rows, (h + 1) * rows)
        rotated_ref[place, :] = query
        state_ref[place, :] = jnp.where(lane == 0, row_max, jnp.where(lane == 1, denominator, blended))


def split_copies(source, target, sems, first, parts):
    rows = source.shape[0]
    step = rows if parts == 1 else -(-rows // parts) // 16 * 16 + 16
    return [
        pltpu.make_async_copy(
            source.at[start : min(start + step, rows)],
            target.at[start : min(start + step, rows)],
            sems.at[first + i],
        )
        for i, start in enumerate(range(0, rows, step))
    ]


def start_all(copies):
    for copy in copies:
        copy.start()


def wait_all(copies):
    for copy in copies:
        copy.wait()


def page_kernel(me_ref, weight_ref, rotated_ref, state_ref, page_ref, valid_ref, attended_ref, *refs):
    other_refs, held_ref, sems = refs[:-2], refs[-2], refs[-1]
    copies = [
        split_copies(weight_ref.at[me_ref[0] ^ (j + 1)], held_ref.at[j], sems, PARTS * j, PARTS)
        for j in range(len(other_refs))
    ]
    for some in copies:
        start_all(some)
    tokens = attended_ref.shape[0]
    pair = 2 * HEAD
    kv_heads = page_ref.shape[1] // pair
    rows = rotated_ref.shape[0] // kv_heads
    group_size = rows // tokens
    low = lax.broadcasted_iota(jnp.int32, (tokens, pair), 1) < HEAD
    page_valid = valid_ref[...] > 0.0
    for h in range(kv_heads):
        place = slice(h * rows, (h + 1) * rows)
        source = page_ref[:, h * pair : (h + 1) * pair]
        state = state_ref[place, :]
        score = jnp.where(page_valid, dot_nt(rotated_ref[place, :], source), -jnp.inf)
        row_max = jnp.maximum(state[:, 0:1], jnp.max(score, axis=1, keepdims=True))
        weights = jnp.exp(score - row_max)
        kept = jnp.exp(state[:, 0:1] - row_max)
        denominator = state[:, 1:2] * kept + jnp.sum(weights, axis=1, keepdims=True)
        term = jnp.dot(weights.astype(jnp.bfloat16), source, preferred_element_type=jnp.float32)
        blended = (state * kept + term) / denominator
        for i in range(group_size // 2):
            even = blended[2 * i * tokens : (2 * i + 1) * tokens]
            odd = blended[(2 * i + 1) * tokens : (2 * i + 2) * tokens]
            start = (h * group_size + 2 * i) * HEAD
            attended_ref[:, start : start + pair] = jnp.where(
                low, pltpu.roll(even, HEAD, 1), odd
            ).astype(jnp.bfloat16)
    attended = attended_ref[...]
    for j, ref in enumerate(other_refs):
        wait_all(copies[j])
        ref[...] = dot_nt(attended, held_ref[j]).astype(jnp.bfloat16)


def own_columns_kernel(
    me_ref, weight_ref, residual_ref, attended_ref, out_ref, sent_ref, held_ref, rows_ref, sems
):
    copies = split_copies(weight_ref.at[me_ref[0]], held_ref, sems, 0, PARTS)
    copies.append(pltpu.make_async_copy(residual_ref, rows_ref, sems.at[PARTS]))
    start_all(copies)
    wait_all(copies)
    terms = rows_ref[...].astype(jnp.float32) + dot_nt(attended_ref[...], held_ref[...])
    out_ref[...] = terms
    sent_ref[...] = terms.astype(jnp.bfloat16)


def tiles(size):
    return [slice(start, min(start + TILE, size)) for start in range(0, size, TILE)]


def gate_up_kernel(parts, me_ref, gate_ref, up_ref, gain_ref, *refs):
    sets, (out_ref, place_ref, row_ref, gate_held, up_held, gain_held, sems) = refs[:-7], refs[-7:]
    rows, width = sets[0].shape[1:]
    features, hidden = gate_ref.shape[1], gate_ref.shape[0]
    gain_copy = pltpu.make_async_copy(gain_ref, gain_held, sems.at[0])
    gain_copy.start()
    copies = []
    for t, tile in enumerate(tiles(hidden)):
        some = split_copies(gate_ref.at[tile], gate_held.at[tile], sems, 1 + 4 * t, 2)
        some += split_copies(up_ref.at[tile], up_held.at[tile], sems, 3 + 4 * t, 2)
        start_all(some)
        copies.append(some)
    me = me_ref[0]
    gain_copy.wait()
    for s, ref in enumerate(sets):
        held = [ref[j].astype(jnp.float32) for j in range(parts)]
        square = sum(jnp.sum(h * h, axis=1, keepdims=True) for h in held)
        scale = lax.rsqrt(square / features + EPSILON)
        for j in range(parts):
            place_ref[me ^ j] = held[j] * scale
        whole = jnp.concatenate([place_ref[p] for p in range(parts)], axis=1)
        row_ref[pl.ds(s * rows, rows), :] = (whole * gain_held[...]).astype(jnp.bfloat16)
    for t, tile in enumerate(tiles(hidden)):
        wait_all(copies[t])
        gate_val = dot_nt(row_ref[...], gate_held[tile])
        up_val = dot_nt(row_ref[...], up_held[tile])
        active = gate_val * jax.nn.sigmoid(ALPHA * gate_val) * (up_val + 1.0)
        out_ref[:, tile] = active.astype(jnp.bfloat16)


def down_kernel(me_ref, down_ref, *refs):
    own_ref, other_ref, held_ref, total_ref, sems = refs[-5:]
    actives = refs[:-5]
    rows, width = own_ref.shape
    copies = [
        split_copies(down_ref.at[me_ref[0] ^ j], held_ref.at[j], sems, PARTS * j, PARTS)
        for j in range(len(actives))
    ]
    for some in copies:
        start_all(some)
    for j, ref in enumerate(actives):
        wait_all(copies[j])
        for tile in tiles(width):
            term = jnp.dot(ref[...], held_ref[j, :, tile], preferred_element_type=jnp.float32)
            if j > 0:
                term = term + total_ref[:, tile]
            if j < len(actives) - 1:
                total_ref[:, tile] = term
            else:
                own_ref[:, tile] = term[:rows].astype(jnp.bfloat16)
                other_ref[:, tile] = term[rows:].astype(jnp.bfloat16)


def kernel_call(kernel, out_types, scalars, sources, *operands, scratch=()):
    in_vmem = pl.BlockSpec(memory_space=pltpu.VMEM)
    in_hbm = pl.BlockSpec(memory_space=pltpu.HBM)
    return pl.pallas_call(
        kernel,
        out_shape=[pltpu.VMEM(shape, dtype) for shape, dtype in out_types],
        in_specs=[pl.BlockSpec(memory_space=pltpu.SMEM)] * len(scalars)
        + [in_hbm] * len(sources)
        + [in_vmem] * len(operands),
        out_specs=[in_vmem] * len(out_types),
        scratch_shapes=scratch,
        compiler_params=pltpu.CompilerParams(vmem_limit_bytes=VMEM_LIMIT),
    )(
        *scalars,
        *[pltpu.with_memory_space_constraint(value, pltpu.HBM) for value in sources],
        *[pltpu.with_memory_space_constraint(value, pltpu.VMEM) for value in operands],
    )


def on_device(
    queries,
    new_kv,
    local_cache,
    remote_pool,
    page_index,
    lengths,
    sinks,
    out_weight,
    residual,
    norm_gain,
    routes,
    route_weights,
    expert_gate,
    expert_up,
    expert_down,
):
    groups = lax.axis_size("group")
    tp = lax.axis_size("tp")
    me_tp = lax.axis_index("tp")
    experts = groups // 2
    me_expert = lax.axis_index("group") // 2
    tp_scalar = me_tp.astype(jnp.int32).reshape(1)
    lane_count = remote_pool.shape[1]
    local_len = local_cache.shape[0]
    fetched = lax.all_to_all(
        remote_pool.reshape(groups, -1, lane_count),
        "group",
        split_axis=0,
        concat_axis=0,
        tiled=True,
    )
    page_len = fetched.shape[1]
    length = lengths[0]
    offsets = jnp.arange(page_len, dtype=jnp.int32)
    remote_pos = local_len + page_index[0][:, None] * page_len + offsets[None, :]
    page_valid = (remote_pos < length).astype(jnp.float32).reshape(1, -1)
    block_len, width = residual.shape
    positions = (length + jnp.arange(block_len, dtype=jnp.int32)).astype(jnp.float32)
    lane = jnp.arange(2 * HEAD, dtype=jnp.int32) % HEAD
    inverse = THETA ** (-2.0 * (lane % (HEAD // 2)).astype(jnp.float32) / HEAD)
    angles = positions[:, None] * inverse[None, :]
    sine = jnp.where(lane < HEAD // 2, -1.0, 1.0)[None, :] * jnp.sin(angles)
    hidden = expert_gate.shape[2]
    weight = out_weight.T.reshape(tp, width, out_weight.shape[0])
    gate, up = expert_gate[0].T, expert_up[0].T
    down = expert_down.reshape(tp, hidden, width)
    gain = norm_gain.reshape(1, tp * width)
    dma = pltpu.SemaphoreType.DMA
    in_vmem = pl.BlockSpec(memory_space=pltpu.VMEM)
    states = block_len * queries.shape[1] // HEAD
    rotated, state = pl.pallas_call(
        local_kernel,
        out_shape=[
            pltpu.VMEM((states, 2 * HEAD), jnp.bfloat16),
            pltpu.VMEM((states, 2 * HEAD), jnp.float32),
        ],
        in_specs=[pl.BlockSpec(memory_space=pltpu.SMEM)] + [in_vmem] * 5,
        out_specs=[in_vmem] * 2,
        compiler_params=pltpu.CompilerParams(vmem_limit_bytes=VMEM_LIMIT),
    )(
        sinks,
        *[pltpu.with_memory_space_constraint(value, pltpu.HBM) for value in (queries, new_kv, local_cache)],
        *[pltpu.with_memory_space_constraint(value, pltpu.VMEM) for value in (jnp.cos(angles), sine)],
    )
    attended, *others = kernel_call(
        page_kernel,
        [(queries.shape, jnp.bfloat16)] + [(residual.shape, jnp.bfloat16)] * (tp - 1),
        [tp_scalar],
        [weight],
        rotated,
        state,
        fetched.reshape(-1, lane_count),
        page_valid,
        scratch=[pltpu.VMEM((tp - 1, *weight.shape[1:]), jnp.bfloat16), dma((PARTS * (tp - 1),))],
    )
    arriving = [exchange(other, "tp", j + 1) for j, other in enumerate(others)]
    own_state, own_terms = kernel_call(
        own_columns_kernel,
        [(residual.shape, jnp.float32), (residual.shape, jnp.bfloat16)],
        [tp_scalar],
        [weight, residual],
        lax.optimization_barrier((attended, gain))[0],
        scratch=[
            pltpu.VMEM(weight.shape[1:], jnp.bfloat16),
            pltpu.VMEM(residual.shape, jnp.bfloat16),
            dma((PARTS + 1,)),
        ],
    )
    for term in arriving:
        own_state = own_state + term.astype(jnp.float32)
    state_sent = own_state.astype(jnp.bfloat16)
    if tp == 2:
        own_terms = lax.optimization_barrier((own_terms, state_sent))[0]
        other_state = exchange(own_terms, "tp", 1).astype(jnp.float32) + others[0].astype(jnp.float32)
        own_blocks = [state_sent, other_state.astype(jnp.bfloat16)]
    else:
        own_blocks = [exchange(state_sent, "tp", j) for j in range(tp)]

    top_count = routes.shape[1]
    capacity = 5 * block_len * top_count // (4 * experts)
    half = experts // 2
    mixing = route_weights / jnp.sum(route_weights, axis=1, keepdims=True)
    plan = jnp.concatenate([routes.astype(jnp.float32), mixing], axis=1)
    far_plan = exchange(lax.optimization_barrier((plan, own_blocks[-1]))[0], "group", experts)

    def slots(chosen_experts, weights):
        chosen = (chosen_experts ^ me_expert)[:, :, None] == jnp.arange(half, dtype=jnp.int32)
        member = jnp.any(chosen, axis=1)
        mix = jnp.sum(jnp.where(chosen, weights[:, :, None], 0.0), axis=1)
        earlier = jnp.arange(block_len)[:, None] > jnp.arange(block_len)[None, :]
        rank = jnp.dot(
            earlier.astype(jnp.bfloat16), member.astype(jnp.bfloat16), preferred_element_type=jnp.float32
        ).astype(jnp.int32)
        hit = member.T[:, None, :] & (
            rank.T[:, None, :] == jnp.arange(capacity, dtype=jnp.int32)[None, :, None]
        )
        pick = hit.astype(jnp.bfloat16).reshape(half * capacity, block_len)
        spread = jnp.where(hit, mix.T[:, None, :], 0.0).reshape(half * capacity, block_len)
        high = spread.astype(jnp.bfloat16)
        return pick, (high, (spread - high.astype(jnp.float32)).astype(jnp.bfloat16))

    own_pick, own_spread = slots(routes, mixing)

    def after(value, *earlier):
        return lax.optimization_barrier((value, *earlier))[0]

    def whole(value):
        return [exchange(value, "tp", j) for j in range(tp)]

    def picked(pick, values):
        parts = [
            jnp.dot(pick, value, preferred_element_type=jnp.float32)
            .astype(jnp.bfloat16)
            .reshape(half, capacity, width)
            for value in values
        ]
        return jnp.stack(parts, axis=1)

    def send_rows(rows):
        return [exchange(rows[d], "group", 2 * d) for d in range(half)]

    def blend(spread, pieces):
        rows = jnp.concatenate(pieces, axis=0)
        rows_first = (((0,), (0,)), ((), ()))
        return sum(
            lax.dot_general(part, rows, rows_first, preferred_element_type=jnp.float32)
            for part in spread
        )

    def activate(sets):
        rows = sets[0].shape[1]
        (active,) = kernel_call(
            functools.partial(gate_up_kernel, tp),
            [((2 * rows, hidden), jnp.bfloat16)],
            [tp_scalar],
            [gate, up, gain],
            *sets,
            scratch=[
                pltpu.VMEM((tp, rows, width), jnp.float32),
                pltpu.VMEM((2 * rows, tp * width), jnp.bfloat16),
                pltpu.VMEM(gate.shape, jnp.bfloat16),
                pltpu.VMEM(up.shape, jnp.bfloat16),
                pltpu.VMEM(gain.shape, jnp.float32),
                dma((1 + 4 * len(tiles(hidden)),)),
            ],
        )
        return active

    def project_down(actives):
        rows = actives[0].shape[0] // 2
        return kernel_call(
            down_kernel,
            [((rows, width), jnp.bfloat16)] * 2,
            [tp_scalar],
            [down],
            *actives,
            scratch=[
                pltpu.VMEM(down.shape, jnp.bfloat16),
                pltpu.VMEM((2 * rows, width), jnp.float32),
                dma((PARTS * tp,)),
            ],
        )

    def add_halves(mine, theirs):
        summed = mine.astype(jnp.float32) + exchange(theirs, "group", 1).astype(jnp.float32)
        return summed.astype(jnp.bfloat16).reshape(half, capacity, width)

    far_blocks = whole(exchange(state_sent, "group", experts))
    own_sent = picked(own_pick, own_blocks)
    own_pieces = send_rows(own_sent)
    far_plan = after(far_plan, own_pieces[1])
    far_pick, far_spread = slots(
        far_plan[:, :top_count].astype(jnp.int32), far_plan[:, top_count:]
    )
    far_sent = picked(far_pick, far_blocks)
    far_pieces = send_rows(far_sent)
    own_rows = jnp.concatenate([after(piece, far_sent) for piece in own_pieces], axis=1)
    own_active = activate([own_rows, exchange(own_rows, "group", 1)])
    own_actives = whole(own_active)
    far_rows = jnp.concatenate([after(piece, own_active) for piece in far_pieces], axis=1)
    far_active = activate([far_rows, exchange(far_rows, "group", 1)])
    far_actives = whole(far_active)
    own_actives[0] = after(own_actives[0], far_active)
    own_out = project_down(own_actives)
    far_actives[0] = after(far_actives[0], own_out[0])
    far_out = add_halves(*project_down(far_actives))
    own_out = add_halves(*own_out)
    far_sum = blend(far_spread, send_rows(far_out)).astype(jnp.bfloat16)
    far_sum = exchange(far_sum, "group", experts)
    total = own_state + blend(own_spread, send_rows(own_out)) + far_sum.astype(jnp.float32)
    return total.astype(jnp.bfloat16)


def solution(mesh):
    return jax.shard_map(
        on_device,
        mesh=mesh,
        in_specs=(
            P("group", "tp"),
            P("group", "tp"),
            P("group", "tp"),
            P("group", "tp"),
            P("group", None),
            P("group"),
            P("tp"),
            P("tp", None),
            P("group", "tp"),
            P(),
            P("group", None),
            P("group", None),
            P("group", None, "tp"),
            P("group", None, "tp"),
            P("group", None, "tp"),
        ),
        out_specs=P("group", "tp"),
        check_vma=False,
    )
```

```python
import functools

import jax
import jax.numpy as jnp
from jax import lax
from jax.experimental import pallas as pl
from jax.experimental.pallas import tpu as pltpu
from jax.sharding import PartitionSpec as P

HEAD = 64
TILE = 256
PARTS = 1
VMEM_LIMIT = 24 * 1024 * 1024


THETA = 150000.0
ALPHA = 1.702
EPSILON = 1e-05


def exchange(value, axis, offset):
    if offset == 0:
        return value
    size = lax.axis_size(axis)
    return lax.ppermute(value, axis, [(i, i ^ offset) for i in range(size)])


NT = (((1,), (1,)), ((), ()))


def dot_nt(left, right):
    return lax.dot_general(left, right, NT, preferred_element_type=jnp.float32)


def swapped_halves(value):
    lanes = value.shape[1]
    lane = lax.broadcasted_iota(jnp.int32, value.shape, 1)
    return jnp.where(
        lane % HEAD < HEAD // 2,
        pltpu.roll(value, lanes - HEAD // 2, 1),
        pltpu.roll(value, HEAD // 2, 1),
    )


def local_kernel(sink_ref, query_ref, kv_ref, local_ref, cos_ref, sin_ref, rotated_ref, state_ref):
    tokens = query_ref.shape[0]
    pair = 2 * HEAD
    kv_heads = kv_ref.shape[1] // pair
    group_size = query_ref.shape[1] // HEAD // kv_heads
    rows = group_size * tokens
    cosine, sine = cos_ref[...], sin_ref[...]
    low = lax.broadcasted_iota(jnp.int32, (tokens, pair), 1) < HEAD
    lane = lax.broadcasted_iota(jnp.int32, (rows, pair), 1)

    def rotated(value):
        return value * cosine + swapped_halves(value) * sine

    token_row = lax.broadcasted_iota(jnp.int32, (rows, tokens), 0) % tokens
    causal = lax.broadcasted_iota(jnp.int32, (rows, tokens), 1) <= token_row
    for h in range(kv_heads):
        lanes = slice(h * pair, (h + 1) * pair)
        own = kv_ref[:, lanes]
        own = jnp.where(low, rotated(own.astype(jnp.float32)).astype(jnp.bfloat16), own)
        queries = []
        for i in range(group_size // 2):
            start = (h * group_size + 2 * i) * HEAD
            both = rotated(query_ref[:, start : start + pair].astype(jnp.float32)) * HEAD**-0.5
            queries.append(jnp.where(low, both, 0.0))
            queries.append(jnp.where(low, pltpu.roll(both, HEAD, 1), 0.0))
        query = jnp.concatenate(queries, axis=0).astype(jnp.bfloat16)
        sink = jnp.concatenate(
            [jnp.full((tokens, 1), sink_ref[h * group_size + i]) for i in range(group_size)], axis=0
        )
        sources = [local_ref[:, lanes], own]
        scores = [dot_nt(query, source) for source in sources]
        scores[1] = jnp.where(causal, scores[1], -jnp.inf)
        row_max = sink
        for score in scores:
            row_max = jnp.maximum(row_max, jnp.max(score, axis=1, keepdims=True))
        denominator = jnp.exp(sink - row_max)
        blended = None
        for score, source in zip(scores, sources):
            weights = jnp.exp(score - row_max)
            denominator = denominator + jnp.sum(weights, axis=1, keepdims=True)
            term = jnp.dot(weights.astype(jnp.bfloat16), source, preferred_element_type=jnp.float32)
            blended = term if blended is None else blended + term
        place = slice(h * rows, (h + 1) * rows)
        rotated_ref[place, :] = query
        state_ref[place, :] = jnp.where(lane == 0, row_max, jnp.where(lane == 1, denominator, blended))


def split_copies(source, target, sems, first, parts):
    rows = source.shape[0]
    step = rows if parts == 1 else -(-rows // parts) // 16 * 16 + 16
    return [
        pltpu.make_async_copy(
            source.at[start : min(start + step, rows)],
            target.at[start : min(start + step, rows)],
            sems.at[first + i],
        )
        for i, start in enumerate(range(0, rows, step))
    ]


def start_all(copies):
    for copy in copies:
        copy.start()


def wait_all(copies):
    for copy in copies:
        copy.wait()


def page_kernel(me_ref, weight_ref, rotated_ref, state_ref, page_ref, valid_ref, attended_ref, *refs):
    other_refs, held_ref, sems = refs[:-2], refs[-2], refs[-1]
    copies = [
        split_copies(weight_ref.at[me_ref[0] ^ (j + 1)], held_ref.at[j], sems, 2 * j, 2)
        for j in range(len(other_refs))
    ]
    for some in copies:
        start_all(some)
    tokens = attended_ref.shape[0]
    pair = 2 * HEAD
    kv_heads = page_ref.shape[1] // pair
    rows = rotated_ref.shape[0] // kv_heads
    group_size = rows // tokens
    low = lax.broadcasted_iota(jnp.int32, (tokens, pair), 1) < HEAD
    page_valid = valid_ref[...] > 0.0
    for h in range(kv_heads):
        place = slice(h * rows, (h + 1) * rows)
        source = page_ref[:, h * pair : (h + 1) * pair]
        state = state_ref[place, :]
        score = jnp.where(page_valid, dot_nt(rotated_ref[place, :], source), -jnp.inf)
        row_max = jnp.maximum(state[:, 0:1], jnp.max(score, axis=1, keepdims=True))
        weights = jnp.exp(score - row_max)
        kept = jnp.exp(state[:, 0:1] - row_max)
        denominator = state[:, 1:2] * kept + jnp.sum(weights, axis=1, keepdims=True)
        term = jnp.dot(weights.astype(jnp.bfloat16), source, preferred_element_type=jnp.float32)
        blended = (state * kept + term) / denominator
        for i in range(group_size // 2):
            even = blended[2 * i * tokens : (2 * i + 1) * tokens]
            odd = blended[(2 * i + 1) * tokens : (2 * i + 2) * tokens]
            start = (h * group_size + 2 * i) * HEAD
            attended_ref[:, start : start + pair] = jnp.where(
                low, pltpu.roll(even, HEAD, 1), odd
            ).astype(jnp.bfloat16)
    attended = attended_ref[...]
    for j, ref in enumerate(other_refs):
        wait_all(copies[j])
        ref[...] = dot_nt(attended, held_ref[j]).astype(jnp.bfloat16)


def own_columns_kernel(
    me_ref, weight_ref, residual_ref, attended_ref, out_ref, sent_ref, held_ref, rows_ref, sems
):
    copies = split_copies(weight_ref.at[me_ref[0]], held_ref, sems, 0, PARTS)
    copies.append(pltpu.make_async_copy(residual_ref, rows_ref, sems.at[PARTS]))
    start_all(copies)
    wait_all(copies)
    terms = rows_ref[...].astype(jnp.float32) + dot_nt(attended_ref[...], held_ref[...])
    out_ref[...] = terms
    sent_ref[...] = terms.astype(jnp.bfloat16)


def tiles(size):
    return [slice(start, min(start + TILE, size)) for start in range(0, size, TILE)]


def gate_up_kernel(parts, me_ref, gate_ref, up_ref, gain_ref, *refs):
    sets, (out_ref, place_ref, row_ref, gate_held, up_held, gain_held, sems) = refs[:-7], refs[-7:]
    rows, width = sets[0].shape[1:]
    features, hidden = gate_ref.shape[1], gate_ref.shape[0]
    gain_copy = pltpu.make_async_copy(gain_ref, gain_held, sems.at[0])
    gain_copy.start()
    copies = []
    for t, tile in enumerate(tiles(hidden)):
        some = split_copies(gate_ref.at[tile], gate_held.at[tile], sems, 1 + 4 * t, 2)
        some += split_copies(up_ref.at[tile], up_held.at[tile], sems, 3 + 4 * t, 2)
        start_all(some)
        copies.append(some)
    me = me_ref[0]
    gain_copy.wait()
    for s, ref in enumerate(sets):
        held = [ref[j].astype(jnp.float32) for j in range(parts)]
        square = sum(jnp.sum(h * h, axis=1, keepdims=True) for h in held)
        scale = lax.rsqrt(square / features + EPSILON)
        for j in range(parts):
            place_ref[me ^ j] = held[j] * scale
        whole = jnp.concatenate([place_ref[p] for p in range(parts)], axis=1)
        row_ref[pl.ds(s * rows, rows), :] = (whole * gain_held[...]).astype(jnp.bfloat16)
    for t, tile in enumerate(tiles(hidden)):
        wait_all(copies[t])
        gate_val = dot_nt(row_ref[...], gate_held[tile])
        up_val = dot_nt(row_ref[...], up_held[tile])
        active = gate_val * jax.nn.sigmoid(ALPHA * gate_val) * (up_val + 1.0)
        out_ref[:, tile] = active.astype(jnp.bfloat16)


def down_kernel(me_ref, down_ref, *refs):
    own_ref, other_ref, held_ref, total_ref, sems = refs[-5:]
    actives = refs[:-5]
    rows, width = own_ref.shape
    copies = [
        split_copies(down_ref.at[me_ref[0] ^ j], held_ref.at[j], sems, PARTS * j, PARTS)
        for j in range(len(actives))
    ]
    for some in copies:
        start_all(some)
    for j, ref in enumerate(actives):
        wait_all(copies[j])
        for tile in tiles(width):
            term = jnp.dot(ref[...], held_ref[j, :, tile], preferred_element_type=jnp.float32)
            if j > 0:
                term = term + total_ref[:, tile]
            if j < len(actives) - 1:
                total_ref[:, tile] = term
            else:
                own_ref[:, tile] = term[:rows].astype(jnp.bfloat16)
                other_ref[:, tile] = term[rows:].astype(jnp.bfloat16)


def kernel_call(kernel, out_types, scalars, sources, *operands, scratch=()):
    in_vmem = pl.BlockSpec(memory_space=pltpu.VMEM)
    in_hbm = pl.BlockSpec(memory_space=pltpu.HBM)
    return pl.pallas_call(
        kernel,
        out_shape=[pltpu.VMEM(shape, dtype) for shape, dtype in out_types],
        in_specs=[pl.BlockSpec(memory_space=pltpu.SMEM)] * len(scalars)
        + [in_hbm] * len(sources)
        + [in_vmem] * len(operands),
        out_specs=[in_vmem] * len(out_types),
        scratch_shapes=scratch,
        compiler_params=pltpu.CompilerParams(vmem_limit_bytes=VMEM_LIMIT),
    )(
        *scalars,
        *[pltpu.with_memory_space_constraint(value, pltpu.HBM) for value in sources],
        *[pltpu.with_memory_space_constraint(value, pltpu.VMEM) for value in operands],
    )


def on_device(
    queries,
    new_kv,
    local_cache,
    remote_pool,
    page_index,
    lengths,
    sinks,
    out_weight,
    residual,
    norm_gain,
    routes,
    route_weights,
    expert_gate,
    expert_up,
    expert_down,
):
    groups = lax.axis_size("group")
    tp = lax.axis_size("tp")
    me_tp = lax.axis_index("tp")
    experts = groups // 2
    me_expert = lax.axis_index("group") // 2
    tp_scalar = me_tp.astype(jnp.int32).reshape(1)
    lane_count = remote_pool.shape[1]
    local_len = local_cache.shape[0]
    fetched = lax.all_to_all(
        remote_pool.reshape(groups, -1, lane_count),
        "group",
        split_axis=0,
        concat_axis=0,
        tiled=True,
    )
    page_len = fetched.shape[1]
    length = lengths[0]
    offsets = jnp.arange(page_len, dtype=jnp.int32)
    remote_pos = local_len + page_index[0][:, None] * page_len + offsets[None, :]
    page_valid = (remote_pos < length).astype(jnp.float32).reshape(1, -1)
    block_len, width = residual.shape
    positions = (length + jnp.arange(block_len, dtype=jnp.int32)).astype(jnp.float32)
    lane = jnp.arange(2 * HEAD, dtype=jnp.int32) % HEAD
    inverse = THETA ** (-2.0 * (lane % (HEAD // 2)).astype(jnp.float32) / HEAD)
    angles = positions[:, None] * inverse[None, :]
    sine = jnp.where(lane < HEAD // 2, -1.0, 1.0)[None, :] * jnp.sin(angles)
    hidden = expert_gate.shape[2]
    weight = out_weight.T.reshape(tp, width, out_weight.shape[0])
    gate, up = expert_gate[0].T, expert_up[0].T
    down = expert_down.reshape(tp, hidden, width)
    dma = pltpu.SemaphoreType.DMA
    in_vmem = pl.BlockSpec(memory_space=pltpu.VMEM)
    states = block_len * queries.shape[1] // HEAD
    rotated, state = pl.pallas_call(
        local_kernel,
        out_shape=[
            pltpu.VMEM((states, 2 * HEAD), jnp.bfloat16),
            pltpu.VMEM((states, 2 * HEAD), jnp.float32),
        ],
        in_specs=[pl.BlockSpec(memory_space=pltpu.SMEM)] + [in_vmem] * 5,
        out_specs=[in_vmem] * 2,
        compiler_params=pltpu.CompilerParams(vmem_limit_bytes=VMEM_LIMIT),
    )(
        sinks,
        *[pltpu.with_memory_space_constraint(value, pltpu.HBM) for value in (queries, new_kv, local_cache)],
        *[pltpu.with_memory_space_constraint(value, pltpu.VMEM) for value in (jnp.cos(angles), sine)],
    )
    attended, *others = kernel_call(
        page_kernel,
        [(queries.shape, jnp.bfloat16)] + [(residual.shape, jnp.bfloat16)] * (tp - 1),
        [tp_scalar],
        [weight],
        rotated,
        state,
        fetched.reshape(-1, lane_count),
        page_valid,
        scratch=[pltpu.VMEM((tp - 1, *weight.shape[1:]), jnp.bfloat16), dma((2 * (tp - 1),))],
    )
    arriving = [exchange(other, "tp", j + 1) for j, other in enumerate(others)]
    gain, route_weights, _ = lax.optimization_barrier((norm_gain, route_weights, attended))
    gain = gain.reshape(1, tp * width)
    own_state, own_terms = kernel_call(
        own_columns_kernel,
        [(residual.shape, jnp.float32), (residual.shape, jnp.bfloat16)],
        [tp_scalar],
        [weight, residual],
        lax.optimization_barrier((attended, gain))[0],
        scratch=[
            pltpu.VMEM(weight.shape[1:], jnp.bfloat16),
            pltpu.VMEM(residual.shape, jnp.bfloat16),
            dma((PARTS + 1,)),
        ],
    )
    for term in arriving:
        own_state = own_state + term.astype(jnp.float32)
    state_sent = own_state.astype(jnp.bfloat16)
    if tp == 2:
        own_terms = lax.optimization_barrier((own_terms, state_sent))[0]
        other_state = exchange(own_terms, "tp", 1).astype(jnp.float32) + others[0].astype(jnp.float32)
        own_blocks = [state_sent, other_state.astype(jnp.bfloat16)]
    else:
        own_blocks = [exchange(state_sent, "tp", j) for j in range(tp)]

    top_count = routes.shape[1]
    capacity = 5 * block_len * top_count // (4 * experts)
    half = experts // 2
    mixing = route_weights / jnp.sum(route_weights, axis=1, keepdims=True)
    plan = jnp.concatenate([routes.astype(jnp.float32), mixing], axis=1)
    far_plan = exchange(lax.optimization_barrier((plan, own_blocks[-1]))[0], "group", experts)

    def slots(chosen_experts, weights):
        chosen = (chosen_experts ^ me_expert)[:, :, None] == jnp.arange(half, dtype=jnp.int32)
        member = jnp.any(chosen, axis=1)
        mix = jnp.sum(jnp.where(chosen, weights[:, :, None], 0.0), axis=1)
        earlier = jnp.arange(block_len)[:, None] > jnp.arange(block_len)[None, :]
        rank = jnp.dot(
            earlier.astype(jnp.bfloat16), member.astype(jnp.bfloat16), preferred_element_type=jnp.float32
        ).astype(jnp.int32)
        hit = member.T[:, None, :] & (
            rank.T[:, None, :] == jnp.arange(capacity, dtype=jnp.int32)[None, :, None]
        )
        pick = hit.astype(jnp.bfloat16).reshape(half * capacity, block_len)
        spread = jnp.where(hit, mix.T[:, None, :], 0.0).reshape(half * capacity, block_len)
        high = spread.astype(jnp.bfloat16)
        return pick, (high, (spread - high.astype(jnp.float32)).astype(jnp.bfloat16))

    own_pick, own_spread = slots(routes, mixing)

    def after(value, *earlier):
        return lax.optimization_barrier((value, *earlier))[0]

    def whole(value):
        return [exchange(value, "tp", j) for j in range(tp)]

    def picked(pick, values):
        parts = [
            jnp.dot(pick, value, preferred_element_type=jnp.float32)
            .astype(jnp.bfloat16)
            .reshape(half, capacity, width)
            for value in values
        ]
        return jnp.stack(parts, axis=1)

    def send_rows(rows):
        return [exchange(rows[d], "group", 2 * d) for d in range(half)]

    def blend(spread, pieces):
        rows = jnp.concatenate(pieces, axis=0)
        rows_first = (((0,), (0,)), ((), ()))
        return sum(
            lax.dot_general(part, rows, rows_first, preferred_element_type=jnp.float32)
            for part in spread
        )

    def activate(sets):
        rows = sets[0].shape[1]
        (active,) = kernel_call(
            functools.partial(gate_up_kernel, tp),
            [((2 * rows, hidden), jnp.bfloat16)],
            [tp_scalar],
            [gate, up, gain],
            *sets,
            scratch=[
                pltpu.VMEM((tp, rows, width), jnp.float32),
                pltpu.VMEM((2 * rows, tp * width), jnp.bfloat16),
                pltpu.VMEM(gate.shape, jnp.bfloat16),
                pltpu.VMEM(up.shape, jnp.bfloat16),
                pltpu.VMEM(gain.shape, jnp.float32),
                dma((1 + 4 * len(tiles(hidden)),)),
            ],
        )
        return active

    def project_down(actives):
        rows = actives[0].shape[0] // 2
        return kernel_call(
            down_kernel,
            [((rows, width), jnp.bfloat16)] * 2,
            [tp_scalar],
            [down],
            *actives,
            scratch=[
                pltpu.VMEM(down.shape, jnp.bfloat16),
                pltpu.VMEM((2 * rows, width), jnp.float32),
                dma((PARTS * tp,)),
            ],
        )

    def add_halves(mine, theirs):
        summed = mine.astype(jnp.float32) + exchange(theirs, "group", 1).astype(jnp.float32)
        return summed.astype(jnp.bfloat16).reshape(half, capacity, width)

    far_blocks = whole(exchange(state_sent, "group", experts))
    own_sent = picked(own_pick, own_blocks)
    own_pieces = send_rows(own_sent)
    far_plan = after(far_plan, own_pieces[1])
    far_pick, far_spread = slots(
        far_plan[:, :top_count].astype(jnp.int32), far_plan[:, top_count:]
    )
    far_sent = picked(far_pick, far_blocks)
    far_pieces = send_rows(far_sent)
    own_rows = jnp.concatenate([after(piece, far_sent) for piece in own_pieces], axis=1)
    own_active = activate([own_rows, exchange(own_rows, "group", 1)])
    own_actives = whole(own_active)
    far_rows = jnp.concatenate([after(piece, own_active) for piece in far_pieces], axis=1)
    far_active = activate([far_rows, exchange(far_rows, "group", 1)])
    far_actives = whole(far_active)
    own_actives[0] = after(own_actives[0], far_active)
    own_out = project_down(own_actives)
    far_actives[0] = after(far_actives[0], own_out[0])
    far_out = add_halves(*project_down(far_actives))
    own_out = add_halves(*own_out)
    far_sum = blend(far_spread, send_rows(far_out)).astype(jnp.bfloat16)
    far_sum = exchange(far_sum, "group", experts)
    total = own_state + blend(own_spread, send_rows(own_out)) + far_sum.astype(jnp.float32)
    return total.astype(jnp.bfloat16)


def solution(mesh):
    return jax.shard_map(
        on_device,
        mesh=mesh,
        in_specs=(
            P("group", "tp"),
            P("group", "tp"),
            P("group", "tp"),
            P("group", "tp"),
            P("group", None),
            P("group"),
            P("tp"),
            P("tp", None),
            P("group", "tp"),
            P(),
            P("group", None),
            P("group", None),
            P("group", None, "tp"),
            P("group", None, "tp"),
            P("group", None, "tp"),
        ),
        out_specs=P("group", "tp"),
        check_vma=False,
    )
```

```python
import functools

import jax
import jax.numpy as jnp
from jax import lax
from jax.experimental import pallas as pl
from jax.experimental.pallas import tpu as pltpu
from jax.sharding import PartitionSpec as P

HEAD = 64
TILE = 256
VMEM_LIMIT = 24 * 1024 * 1024


THETA = 150000.0
ALPHA = 1.702
EPSILON = 1e-05


def exchange(value, axis, offset):
    if offset == 0:
        return value
    size = lax.axis_size(axis)
    return lax.ppermute(value, axis, [(i, i ^ offset) for i in range(size)])


NT = (((1,), (1,)), ((), ()))


def dot_nt(left, right):
    return lax.dot_general(left, right, NT, preferred_element_type=jnp.float32)


def swapped_halves(value):
    lanes = value.shape[1]
    lane = lax.broadcasted_iota(jnp.int32, value.shape, 1)
    return jnp.where(
        lane % HEAD < HEAD // 2,
        pltpu.roll(value, lanes - HEAD // 2, 1),
        pltpu.roll(value, HEAD // 2, 1),
    )


def local_kernel(sink_ref, query_ref, kv_ref, local_ref, cos_ref, sin_ref, rotated_ref, state_ref):
    tokens = query_ref.shape[0]
    pair = 2 * HEAD
    kv_heads = kv_ref.shape[1] // pair
    group_size = query_ref.shape[1] // HEAD // kv_heads
    rows = group_size * tokens
    cosine, sine = cos_ref[...], sin_ref[...]
    low = lax.broadcasted_iota(jnp.int32, (tokens, pair), 1) < HEAD
    lane = lax.broadcasted_iota(jnp.int32, (rows, pair), 1)

    def rotated(value):
        return value * cosine + swapped_halves(value) * sine

    token_row = lax.broadcasted_iota(jnp.int32, (rows, tokens), 0) % tokens
    causal = lax.broadcasted_iota(jnp.int32, (rows, tokens), 1) <= token_row
    for h in range(kv_heads):
        lanes = slice(h * pair, (h + 1) * pair)
        own = kv_ref[:, lanes]
        own = jnp.where(low, rotated(own.astype(jnp.float32)).astype(jnp.bfloat16), own)
        queries = []
        for i in range(group_size // 2):
            start = (h * group_size + 2 * i) * HEAD
            both = rotated(query_ref[:, start : start + pair].astype(jnp.float32)) * HEAD**-0.5
            queries.append(jnp.where(low, both, 0.0))
            queries.append(jnp.where(low, pltpu.roll(both, HEAD, 1), 0.0))
        query = jnp.concatenate(queries, axis=0).astype(jnp.bfloat16)
        sink = jnp.concatenate(
            [jnp.full((tokens, 1), sink_ref[h * group_size + i]) for i in range(group_size)], axis=0
        )
        sources = [local_ref[:, lanes], own]
        scores = [dot_nt(query, source) for source in sources]
        scores[1] = jnp.where(causal, scores[1], -jnp.inf)
        row_max = sink
        for score in scores:
            row_max = jnp.maximum(row_max, jnp.max(score, axis=1, keepdims=True))
        denominator = jnp.exp(sink - row_max)
        blended = None
        for score, source in zip(scores, sources):
            weights = jnp.exp(score - row_max)
            denominator = denominator + jnp.sum(weights, axis=1, keepdims=True)
            term = jnp.dot(weights.astype(jnp.bfloat16), source, preferred_element_type=jnp.float32)
            blended = term if blended is None else blended + term
        place = slice(h * rows, (h + 1) * rows)
        rotated_ref[place, :] = query
        state_ref[place, :] = jnp.where(lane == 0, row_max, jnp.where(lane == 1, denominator, blended))


def start_all(copies):
    for copy in copies:
        copy.start()


def wait_all(copies):
    for copy in copies:
        copy.wait()


def page_kernel(me_ref, weight_ref, rotated_ref, state_ref, page_ref, valid_ref, attended_ref, *refs):
    other_refs, held_ref, sems = refs[:-2], refs[-2], refs[-1]
    copies = [
        pltpu.make_async_copy(weight_ref.at[me_ref[0] ^ (j + 1)], held_ref.at[j], sems.at[j])
        for j in range(len(other_refs))
    ]
    start_all(copies)
    tokens = attended_ref.shape[0]
    pair = 2 * HEAD
    kv_heads = page_ref.shape[1] // pair
    rows = rotated_ref.shape[0] // kv_heads
    group_size = rows // tokens
    low = lax.broadcasted_iota(jnp.int32, (tokens, pair), 1) < HEAD
    page_valid = valid_ref[...] > 0.0
    for h in range(kv_heads):
        place = slice(h * rows, (h + 1) * rows)
        source = page_ref[:, h * pair : (h + 1) * pair]
        state = state_ref[place, :]
        score = jnp.where(page_valid, dot_nt(rotated_ref[place, :], source), -jnp.inf)
        row_max = jnp.maximum(state[:, 0:1], jnp.max(score, axis=1, keepdims=True))
        weights = jnp.exp(score - row_max)
        kept = jnp.exp(state[:, 0:1] - row_max)
        denominator = state[:, 1:2] * kept + jnp.sum(weights, axis=1, keepdims=True)
        term = jnp.dot(weights.astype(jnp.bfloat16), source, preferred_element_type=jnp.float32)
        blended = (state * kept + term) / denominator
        for i in range(group_size // 2):
            even = blended[2 * i * tokens : (2 * i + 1) * tokens]
            odd = blended[(2 * i + 1) * tokens : (2 * i + 2) * tokens]
            start = (h * group_size + 2 * i) * HEAD
            attended_ref[:, start : start + pair] = jnp.where(
                low, pltpu.roll(even, HEAD, 1), odd
            ).astype(jnp.bfloat16)
    attended = attended_ref[...]
    for j, ref in enumerate(other_refs):
        copies[j].wait()
        ref[...] = dot_nt(attended, held_ref[j]).astype(jnp.bfloat16)


def own_columns_kernel(
    me_ref, weight_ref, residual_ref, attended_ref, out_ref, sent_ref, held_ref, rows_ref, sems
):
    copies = [
        pltpu.make_async_copy(weight_ref.at[me_ref[0]], held_ref, sems.at[0]),
        pltpu.make_async_copy(residual_ref, rows_ref, sems.at[1]),
    ]
    start_all(copies)
    wait_all(copies)
    terms = rows_ref[...].astype(jnp.float32) + dot_nt(attended_ref[...], held_ref[...])
    out_ref[...] = terms
    sent_ref[...] = terms.astype(jnp.bfloat16)


def tiles(size):
    return [slice(start, min(start + TILE, size)) for start in range(0, size, TILE)]


def gate_up_kernel(parts, me_ref, gate_ref, up_ref, gain_ref, *refs):
    sets, (out_ref, place_ref, row_ref, gate_held, up_held, gain_held, sems) = refs[:-7], refs[-7:]
    rows, width = sets[0].shape[1:]
    blocks, block, features = gate_ref.shape
    gain_copy = pltpu.make_async_copy(gain_ref, gain_held, sems.at[0])
    gain_copy.start()
    copies = []
    for t in range(blocks):
        copies.append(
            [
                pltpu.make_async_copy(gate_ref.at[t], gate_held.at[t], sems.at[1 + 2 * t]),
                pltpu.make_async_copy(up_ref.at[t], up_held.at[t], sems.at[2 + 2 * t]),
            ]
        )
        start_all(copies[-1])
    me = me_ref[0]
    gain_copy.wait()
    for s, ref in enumerate(sets):
        held = [ref[j].astype(jnp.float32) for j in range(parts)]
        square = sum(jnp.sum(h * h, axis=1, keepdims=True) for h in held)
        scale = lax.rsqrt(square / features + EPSILON)
        for j in range(parts):
            place_ref[me ^ j] = held[j] * scale
        whole = jnp.concatenate([place_ref[p] for p in range(parts)], axis=1)
        row_ref[pl.ds(s * rows, rows), :] = (whole * gain_held[...]).astype(jnp.bfloat16)
    for t in range(blocks):
        wait_all(copies[t])
        gate_val = dot_nt(row_ref[...], gate_held[t])
        up_val = dot_nt(row_ref[...], up_held[t])
        active = gate_val * jax.nn.sigmoid(ALPHA * gate_val) * (up_val + 1.0)
        out_ref[:, t * block : (t + 1) * block] = active.astype(jnp.bfloat16)


def down_kernel(me_ref, down_ref, *refs):
    own_ref, other_ref, held_ref, total_ref, sems = refs[-5:]
    actives = refs[:-5]
    rows, width = own_ref.shape
    copies = [
        pltpu.make_async_copy(down_ref.at[me_ref[0] ^ j], held_ref.at[j], sems.at[j])
        for j in range(len(actives))
    ]
    start_all(copies)
    for j, ref in enumerate(actives):
        copies[j].wait()
        for tile in tiles(width):
            term = jnp.dot(ref[...], held_ref[j, :, tile], preferred_element_type=jnp.float32)
            if j > 0:
                term = term + total_ref[:, tile]
            if j < len(actives) - 1:
                total_ref[:, tile] = term
            else:
                own_ref[:, tile] = term[:rows].astype(jnp.bfloat16)
                other_ref[:, tile] = term[rows:].astype(jnp.bfloat16)


def kernel_call(kernel, out_types, scalars, sources, *operands, scratch=()):
    in_vmem = pl.BlockSpec(memory_space=pltpu.VMEM)
    in_hbm = pl.BlockSpec(memory_space=pltpu.HBM)
    return pl.pallas_call(
        kernel,
        out_shape=[pltpu.VMEM(shape, dtype) for shape, dtype in out_types],
        in_specs=[pl.BlockSpec(memory_space=pltpu.SMEM)] * len(scalars)
        + [in_hbm] * len(sources)
        + [in_vmem] * len(operands),
        out_specs=[in_vmem] * len(out_types),
        scratch_shapes=scratch,
        compiler_params=pltpu.CompilerParams(vmem_limit_bytes=VMEM_LIMIT),
    )(
        *scalars,
        *[pltpu.with_memory_space_constraint(value, pltpu.HBM) for value in sources],
        *[pltpu.with_memory_space_constraint(value, pltpu.VMEM) for value in operands],
    )


def on_device(
    queries,
    new_kv,
    local_cache,
    remote_pool,
    page_index,
    lengths,
    sinks,
    out_weight,
    residual,
    norm_gain,
    routes,
    route_weights,
    expert_gate,
    expert_up,
    expert_down,
):
    groups = lax.axis_size("group")
    tp = lax.axis_size("tp")
    me_tp = lax.axis_index("tp")
    experts = groups // 2
    me_expert = lax.axis_index("group") // 2
    tp_scalar = me_tp.astype(jnp.int32).reshape(1)
    lane_count = remote_pool.shape[1]
    local_len = local_cache.shape[0]
    fetched = lax.all_to_all(
        remote_pool.reshape(groups, -1, lane_count),
        "group",
        split_axis=0,
        concat_axis=0,
        tiled=True,
    )
    page_len = fetched.shape[1]
    length = lengths[0]
    offsets = jnp.arange(page_len, dtype=jnp.int32)
    remote_pos = local_len + page_index[0][:, None] * page_len + offsets[None, :]
    page_valid = (remote_pos < length).astype(jnp.float32).reshape(1, -1)
    block_len, width = residual.shape
    positions = (length + jnp.arange(block_len, dtype=jnp.int32)).astype(jnp.float32)
    lane = jnp.arange(2 * HEAD, dtype=jnp.int32) % HEAD
    inverse = THETA ** (-2.0 * (lane % (HEAD // 2)).astype(jnp.float32) / HEAD)
    angles = positions[:, None] * inverse[None, :]
    sine = jnp.where(lane < HEAD // 2, -1.0, 1.0)[None, :] * jnp.sin(angles)
    hidden = expert_gate.shape[2]
    weight = out_weight.T.reshape(tp, width, out_weight.shape[0])
    blocks = 3 if hidden % 48 == 0 else 1
    gate, up = [
        value[0].T.reshape(blocks, hidden // blocks, tp * width) for value in (expert_gate, expert_up)
    ]
    down = expert_down.reshape(tp, hidden, width)
    dma = pltpu.SemaphoreType.DMA
    in_vmem = pl.BlockSpec(memory_space=pltpu.VMEM)
    states = block_len * queries.shape[1] // HEAD
    rotated, state = pl.pallas_call(
        local_kernel,
        out_shape=[
            pltpu.VMEM((states, 2 * HEAD), jnp.bfloat16),
            pltpu.VMEM((states, 2 * HEAD), jnp.float32),
        ],
        in_specs=[pl.BlockSpec(memory_space=pltpu.SMEM)] + [in_vmem] * 5,
        out_specs=[in_vmem] * 2,
        compiler_params=pltpu.CompilerParams(vmem_limit_bytes=VMEM_LIMIT),
    )(
        sinks,
        *[pltpu.with_memory_space_constraint(value, pltpu.HBM) for value in (queries, new_kv, local_cache)],
        *[pltpu.with_memory_space_constraint(value, pltpu.VMEM) for value in (jnp.cos(angles), sine)],
    )
    attended, *others = kernel_call(
        page_kernel,
        [(queries.shape, jnp.bfloat16)] + [(residual.shape, jnp.bfloat16)] * (tp - 1),
        [tp_scalar],
        [weight],
        rotated,
        state,
        fetched.reshape(-1, lane_count),
        page_valid,
        scratch=[pltpu.VMEM((tp - 1, *weight.shape[1:]), jnp.bfloat16), dma((tp - 1,))],
    )
    arriving = [exchange(other, "tp", j + 1) for j, other in enumerate(others)]
    gain, route_weights, _ = lax.optimization_barrier((norm_gain, route_weights, attended))
    gain = gain.reshape(1, tp * width)
    own_state, own_terms = kernel_call(
        own_columns_kernel,
        [(residual.shape, jnp.float32), (residual.shape, jnp.bfloat16)],
        [tp_scalar],
        [weight, residual],
        lax.optimization_barrier((attended, gain))[0],
        scratch=[
            pltpu.VMEM(weight.shape[1:], jnp.bfloat16),
            pltpu.VMEM(residual.shape, jnp.bfloat16),
            dma((2,)),
        ],
    )
    for term in arriving:
        own_state = own_state + term.astype(jnp.float32)
    state_sent = own_state.astype(jnp.bfloat16)
    if tp == 2:
        own_terms = lax.optimization_barrier((own_terms, state_sent))[0]
        other_state = exchange(own_terms, "tp", 1).astype(jnp.float32) + others[0].astype(jnp.float32)
        own_blocks = [state_sent, other_state.astype(jnp.bfloat16)]
    else:
        own_blocks = [exchange(state_sent, "tp", j) for j in range(tp)]

    top_count = routes.shape[1]
    capacity = 5 * block_len * top_count // (4 * experts)
    half = experts // 2
    mixing = route_weights / jnp.sum(route_weights, axis=1, keepdims=True)
    plan = jnp.concatenate([routes.astype(jnp.float32), mixing], axis=1)
    far_plan = exchange(lax.optimization_barrier((plan, own_blocks[-1]))[0], "group", experts)

    def slots(chosen_experts, weights):
        chosen = (chosen_experts ^ me_expert)[:, :, None] == jnp.arange(half, dtype=jnp.int32)
        member = jnp.any(chosen, axis=1)
        mix = jnp.sum(jnp.where(chosen, weights[:, :, None], 0.0), axis=1)
        earlier = jnp.arange(block_len)[:, None] > jnp.arange(block_len)[None, :]
        rank = jnp.dot(
            earlier.astype(jnp.bfloat16), member.astype(jnp.bfloat16), preferred_element_type=jnp.float32
        ).astype(jnp.int32)
        hit = member.T[:, None, :] & (
            rank.T[:, None, :] == jnp.arange(capacity, dtype=jnp.int32)[None, :, None]
        )
        pick = hit.astype(jnp.bfloat16).reshape(half * capacity, block_len)
        spread = jnp.where(hit, mix.T[:, None, :], 0.0).reshape(half * capacity, block_len)
        high = spread.astype(jnp.bfloat16)
        return pick, (high, (spread - high.astype(jnp.float32)).astype(jnp.bfloat16))

    own_pick, own_spread = slots(routes, mixing)

    def after(value, *earlier):
        return lax.optimization_barrier((value, *earlier))[0]

    def whole(value):
        return [exchange(value, "tp", j) for j in range(tp)]

    def picked(pick, values):
        parts = [
            jnp.dot(pick, value, preferred_element_type=jnp.float32)
            .astype(jnp.bfloat16)
            .reshape(half, capacity, width)
            for value in values
        ]
        return jnp.stack(parts, axis=1)

    def send_rows(rows):
        return [exchange(rows[d], "group", 2 * d) for d in range(half)]

    def blend(spread, pieces):
        rows = jnp.concatenate(pieces, axis=0)
        rows_first = (((0,), (0,)), ((), ()))
        return sum(
            lax.dot_general(part, rows, rows_first, preferred_element_type=jnp.float32)
            for part in spread
        )

    def activate(sets):
        rows = sets[0].shape[1]
        (active,) = kernel_call(
            functools.partial(gate_up_kernel, tp),
            [((2 * rows, hidden), jnp.bfloat16)],
            [tp_scalar],
            [gate, up, gain],
            *sets,
            scratch=[
                pltpu.VMEM((tp, rows, width), jnp.float32),
                pltpu.VMEM((2 * rows, tp * width), jnp.bfloat16),
                pltpu.VMEM(gate.shape, jnp.bfloat16),
                pltpu.VMEM(up.shape, jnp.bfloat16),
                pltpu.VMEM(gain.shape, jnp.float32),
                dma((1 + 2 * blocks,)),
            ],
        )
        return active

    def project_down(actives):
        rows = actives[0].shape[0] // 2
        return kernel_call(
            down_kernel,
            [((rows, width), jnp.bfloat16)] * 2,
            [tp_scalar],
            [down],
            *actives,
            scratch=[
                pltpu.VMEM(down.shape, jnp.bfloat16),
                pltpu.VMEM((2 * rows, width), jnp.float32),
                dma((tp,)),
            ],
        )

    def add_halves(mine, theirs):
        summed = mine.astype(jnp.float32) + exchange(theirs, "group", 1).astype(jnp.float32)
        return summed.astype(jnp.bfloat16).reshape(half, capacity, width)

    far_blocks = whole(exchange(state_sent, "group", experts))
    own_sent = picked(own_pick, own_blocks)
    own_pieces = send_rows(own_sent)
    far_plan = after(far_plan, own_pieces[1])
    far_pick, far_spread = slots(
        far_plan[:, :top_count].astype(jnp.int32), far_plan[:, top_count:]
    )
    far_sent = picked(far_pick, far_blocks)
    far_pieces = send_rows(far_sent)
    own_rows = jnp.concatenate([after(piece, far_sent) for piece in own_pieces], axis=1)
    own_active = activate([own_rows, exchange(own_rows, "group", 1)])
    own_actives = whole(own_active)
    far_rows = jnp.concatenate([after(piece, own_active) for piece in far_pieces], axis=1)
    far_active = activate([far_rows, exchange(far_rows, "group", 1)])
    far_actives = whole(far_active)
    own_actives[0] = after(own_actives[0], far_active)
    own_out = project_down(own_actives)
    far_actives[0] = after(far_actives[0], own_out[0])
    far_out = add_halves(*project_down(far_actives))
    own_out = add_halves(*own_out)
    far_sum = blend(far_spread, send_rows(far_out)).astype(jnp.bfloat16)
    far_sum = exchange(far_sum, "group", experts)
    total = own_state + blend(own_spread, send_rows(own_out)) + far_sum.astype(jnp.float32)
    return total.astype(jnp.bfloat16)


def solution(mesh):
    return jax.shard_map(
        on_device,
        mesh=mesh,
        in_specs=(
            P("group", "tp"),
            P("group", "tp"),
            P("group", "tp"),
            P("group", "tp"),
            P("group", None),
            P("group"),
            P("tp"),
            P("tp", None),
            P("group", "tp"),
            P(),
            P("group", None),
            P("group", None),
            P("group", None, "tp"),
            P("group", None, "tp"),
            P("group", None, "tp"),
        ),
        out_specs=P("group", "tp"),
        check_vma=False,
    )
```

```python
import functools

import jax
import jax.numpy as jnp
from jax import lax
from jax.experimental import pallas as pl
from jax.experimental.pallas import tpu as pltpu
from jax.sharding import PartitionSpec as P

HEAD = 64
TILE = 256
VMEM_LIMIT = 24 * 1024 * 1024


THETA = 150000.0
ALPHA = 1.702
EPSILON = 1e-05


def exchange(value, axis, offset):
    if offset == 0:
        return value
    size = lax.axis_size(axis)
    return lax.ppermute(value, axis, [(i, i ^ offset) for i in range(size)])


NT = (((1,), (1,)), ((), ()))


def dot_nt(left, right):
    return lax.dot_general(left, right, NT, preferred_element_type=jnp.float32)


def swapped_halves(value):
    lanes = value.shape[1]
    lane = lax.broadcasted_iota(jnp.int32, value.shape, 1)
    return jnp.where(
        lane % HEAD < HEAD // 2,
        pltpu.roll(value, lanes - HEAD // 2, 1),
        pltpu.roll(value, HEAD // 2, 1),
    )


def local_kernel(sink_ref, query_ref, kv_ref, local_ref, cos_ref, sin_ref, rotated_ref, state_ref):
    tokens = query_ref.shape[0]
    pair = 2 * HEAD
    kv_heads = kv_ref.shape[1] // pair
    group_size = query_ref.shape[1] // HEAD // kv_heads
    rows = group_size * tokens
    cosine, sine = cos_ref[...], sin_ref[...]
    low = lax.broadcasted_iota(jnp.int32, (tokens, pair), 1) < HEAD
    lane = lax.broadcasted_iota(jnp.int32, (rows, pair), 1)

    def rotated(value):
        return value * cosine + swapped_halves(value) * sine

    token_row = lax.broadcasted_iota(jnp.int32, (rows, tokens), 0) % tokens
    causal = lax.broadcasted_iota(jnp.int32, (rows, tokens), 1) <= token_row
    for h in range(kv_heads):
        lanes = slice(h * pair, (h + 1) * pair)
        own = kv_ref[:, lanes]
        own = jnp.where(low, rotated(own.astype(jnp.float32)).astype(jnp.bfloat16), own)
        queries = []
        for i in range(group_size // 2):
            start = (h * group_size + 2 * i) * HEAD
            both = rotated(query_ref[:, start : start + pair].astype(jnp.float32)) * HEAD**-0.5
            queries.append(jnp.where(low, both, 0.0))
            queries.append(jnp.where(low, pltpu.roll(both, HEAD, 1), 0.0))
        query = jnp.concatenate(queries, axis=0).astype(jnp.bfloat16)
        sink = jnp.concatenate(
            [jnp.full((tokens, 1), sink_ref[h * group_size + i]) for i in range(group_size)], axis=0
        )
        sources = [local_ref[:, lanes], own]
        scores = [dot_nt(query, source) for source in sources]
        scores[1] = jnp.where(causal, scores[1], -jnp.inf)
        row_max = sink
        for score in scores:
            row_max = jnp.maximum(row_max, jnp.max(score, axis=1, keepdims=True))
        denominator = jnp.exp(sink - row_max)
        blended = None
        for score, source in zip(scores, sources):
            weights = jnp.exp(score - row_max)
            denominator = denominator + jnp.sum(weights, axis=1, keepdims=True)
            term = jnp.dot(weights.astype(jnp.bfloat16), source, preferred_element_type=jnp.float32)
            blended = term if blended is None else blended + term
        place = slice(h * rows, (h + 1) * rows)
        rotated_ref[place, :] = query
        state_ref[place, :] = jnp.where(lane == 0, row_max, jnp.where(lane == 1, denominator, blended))


def start_all(copies):
    for copy in copies:
        copy.start()


def wait_all(copies):
    for copy in copies:
        copy.wait()


def page_kernel(me_ref, weight_ref, rotated_ref, state_ref, page_ref, valid_ref, attended_ref, *refs):
    other_refs, held_ref, sems = refs[:-2], refs[-2], refs[-1]
    copies = [
        pltpu.make_async_copy(weight_ref.at[me_ref[0] ^ (j + 1)], held_ref.at[j], sems.at[j])
        for j in range(len(other_refs))
    ]
    start_all(copies)
    tokens = attended_ref.shape[0]
    pair = 2 * HEAD
    kv_heads = page_ref.shape[1] // pair
    rows = rotated_ref.shape[0] // kv_heads
    group_size = rows // tokens
    low = lax.broadcasted_iota(jnp.int32, (tokens, pair), 1) < HEAD
    page_valid = valid_ref[...] > 0.0
    for h in range(kv_heads):
        place = slice(h * rows, (h + 1) * rows)
        source = page_ref[:, h * pair : (h + 1) * pair]
        state = state_ref[place, :]
        score = jnp.where(page_valid, dot_nt(rotated_ref[place, :], source), -jnp.inf)
        row_max = jnp.maximum(state[:, 0:1], jnp.max(score, axis=1, keepdims=True))
        weights = jnp.exp(score - row_max)
        kept = jnp.exp(state[:, 0:1] - row_max)
        denominator = state[:, 1:2] * kept + jnp.sum(weights, axis=1, keepdims=True)
        term = jnp.dot(weights.astype(jnp.bfloat16), source, preferred_element_type=jnp.float32)
        blended = (state * kept + term) / denominator
        for i in range(group_size // 2):
            even = blended[2 * i * tokens : (2 * i + 1) * tokens]
            odd = blended[(2 * i + 1) * tokens : (2 * i + 2) * tokens]
            start = (h * group_size + 2 * i) * HEAD
            attended_ref[:, start : start + pair] = jnp.where(
                low, pltpu.roll(even, HEAD, 1), odd
            ).astype(jnp.bfloat16)
    attended = attended_ref[...]
    for j, ref in enumerate(other_refs):
        copies[j].wait()
        ref[...] = dot_nt(attended, held_ref[j]).astype(jnp.bfloat16)


def own_columns_kernel(
    me_ref, weight_ref, residual_ref, attended_ref, out_ref, sent_ref, held_ref, rows_ref, sems
):
    copies = [
        pltpu.make_async_copy(weight_ref.at[me_ref[0]], held_ref, sems.at[0]),
        pltpu.make_async_copy(residual_ref, rows_ref, sems.at[1]),
    ]
    start_all(copies)
    wait_all(copies)
    terms = rows_ref[...].astype(jnp.float32) + dot_nt(attended_ref[...], held_ref[...])
    out_ref[...] = terms
    sent_ref[...] = terms.astype(jnp.bfloat16)


def tiles(size):
    return [slice(start, min(start + TILE, size)) for start in range(0, size, TILE)]


def gate_up_kernel(parts, me_ref, gate_ref, up_ref, gain_ref, *refs):
    sets, (out_ref, place_ref, row_ref, gate_held, up_held, gain_held, sems) = refs[:-7], refs[-7:]
    rows, width = sets[0].shape[1:]
    blocks, block, features = gate_ref.shape
    gain_copy = pltpu.make_async_copy(gain_ref, gain_held, sems.at[0])
    gain_copy.start()
    copies = []
    for t in range(blocks):
        copies.append(
            [
                pltpu.make_async_copy(gate_ref.at[t], gate_held.at[t], sems.at[1 + 2 * t]),
                pltpu.make_async_copy(up_ref.at[t], up_held.at[t], sems.at[2 + 2 * t]),
            ]
        )
        start_all(copies[-1])
    me = me_ref[0]
    gain_copy.wait()
    for s, ref in enumerate(sets):
        held = [ref[j].astype(jnp.float32) for j in range(parts)]
        square = sum(jnp.sum(h * h, axis=1, keepdims=True) for h in held)
        scale = lax.rsqrt(square / features + EPSILON)
        for j in range(parts):
            place_ref[me ^ j] = held[j] * scale
        whole = jnp.concatenate([place_ref[p] for p in range(parts)], axis=1)
        row_ref[pl.ds(s * rows, rows), :] = (whole * gain_held[...]).astype(jnp.bfloat16)
    for t in range(blocks):
        wait_all(copies[t])
        gate_val = dot_nt(row_ref[...], gate_held[t])
        up_val = dot_nt(row_ref[...], up_held[t])
        active = gate_val * jax.nn.sigmoid(ALPHA * gate_val) * (up_val + 1.0)
        out_ref[:, t * block : (t + 1) * block] = active.astype(jnp.bfloat16)


def down_kernel(me_ref, down_ref, *refs):
    own_ref, other_ref, held_ref, total_ref, sems = refs[-5:]
    actives = refs[:-5]
    rows, width = own_ref.shape
    copies = [
        pltpu.make_async_copy(down_ref.at[me_ref[0] ^ j], held_ref.at[j], sems.at[j])
        for j in range(len(actives))
    ]
    start_all(copies)
    for j, ref in enumerate(actives):
        copies[j].wait()
        for tile in tiles(width):
            term = jnp.dot(ref[...], held_ref[j, :, tile], preferred_element_type=jnp.float32)
            if j > 0:
                term = term + total_ref[:, tile]
            if j < len(actives) - 1:
                total_ref[:, tile] = term
            else:
                own_ref[:, tile] = term[:rows].astype(jnp.bfloat16)
                other_ref[:, tile] = term[rows:].astype(jnp.bfloat16)


def kernel_call(kernel, out_types, scalars, sources, *operands, scratch=()):
    in_vmem = pl.BlockSpec(memory_space=pltpu.VMEM)
    in_hbm = pl.BlockSpec(memory_space=pltpu.HBM)
    return pl.pallas_call(
        kernel,
        out_shape=[pltpu.VMEM(shape, dtype) for shape, dtype in out_types],
        in_specs=[pl.BlockSpec(memory_space=pltpu.SMEM)] * len(scalars)
        + [in_hbm] * len(sources)
        + [in_vmem] * len(operands),
        out_specs=[in_vmem] * len(out_types),
        scratch_shapes=scratch,
        compiler_params=pltpu.CompilerParams(vmem_limit_bytes=VMEM_LIMIT),
    )(
        *scalars,
        *[pltpu.with_memory_space_constraint(value, pltpu.HBM) for value in sources],
        *[pltpu.with_memory_space_constraint(value, pltpu.VMEM) for value in operands],
    )


def on_device(
    queries,
    new_kv,
    local_cache,
    remote_pool,
    page_index,
    lengths,
    sinks,
    out_weight,
    residual,
    norm_gain,
    routes,
    route_weights,
    expert_gate,
    expert_up,
    expert_down,
):
    groups = lax.axis_size("group")
    tp = lax.axis_size("tp")
    me_tp = lax.axis_index("tp")
    experts = groups // 2
    me_expert = lax.axis_index("group") // 2
    tp_scalar = me_tp.astype(jnp.int32).reshape(1)
    lane_count = remote_pool.shape[1]
    local_len = local_cache.shape[0]
    fetched = lax.all_to_all(
        remote_pool.reshape(groups, -1, lane_count),
        "group",
        split_axis=0,
        concat_axis=0,
        tiled=True,
    )
    page_len = fetched.shape[1]
    length = lengths[0]
    offsets = jnp.arange(page_len, dtype=jnp.int32)
    remote_pos = local_len + page_index[0][:, None] * page_len + offsets[None, :]
    page_valid = (remote_pos < length).astype(jnp.float32).reshape(1, -1)
    block_len, width = residual.shape
    positions = (length + jnp.arange(block_len, dtype=jnp.int32)).astype(jnp.float32)
    lane = jnp.arange(2 * HEAD, dtype=jnp.int32) % HEAD
    inverse = THETA ** (-2.0 * (lane % (HEAD // 2)).astype(jnp.float32) / HEAD)
    angles = positions[:, None] * inverse[None, :]
    sine = jnp.where(lane < HEAD // 2, -1.0, 1.0)[None, :] * jnp.sin(angles)
    hidden = expert_gate.shape[2]
    weight = out_weight.T.reshape(tp, width, out_weight.shape[0])
    blocks = 3 if hidden % 48 == 0 else 1
    gate, up = [
        value[0].T.reshape(blocks, hidden // blocks, tp * width) for value in (expert_gate, expert_up)
    ]
    down = expert_down.reshape(tp, hidden, width)
    dma = pltpu.SemaphoreType.DMA
    in_vmem = pl.BlockSpec(memory_space=pltpu.VMEM)
    states = block_len * queries.shape[1] // HEAD
    rotated, state = pl.pallas_call(
        local_kernel,
        out_shape=[
            pltpu.VMEM((states, 2 * HEAD), jnp.bfloat16),
            pltpu.VMEM((states, 2 * HEAD), jnp.float32),
        ],
        in_specs=[pl.BlockSpec(memory_space=pltpu.SMEM)] + [in_vmem] * 5,
        out_specs=[in_vmem] * 2,
        compiler_params=pltpu.CompilerParams(vmem_limit_bytes=VMEM_LIMIT),
    )(
        sinks,
        *[pltpu.with_memory_space_constraint(value, pltpu.HBM) for value in (queries, new_kv, local_cache)],
        *[pltpu.with_memory_space_constraint(value, pltpu.VMEM) for value in (jnp.cos(angles), sine)],
    )
    attended, *others = kernel_call(
        page_kernel,
        [(queries.shape, jnp.bfloat16)] + [(residual.shape, jnp.bfloat16)] * (tp - 1),
        [tp_scalar],
        [weight],
        rotated,
        state,
        fetched.reshape(-1, lane_count),
        page_valid,
        scratch=[pltpu.VMEM((tp - 1, *weight.shape[1:]), jnp.bfloat16), dma((tp - 1,))],
    )
    arriving = [exchange(other, "tp", j + 1) for j, other in enumerate(others)]
    gain, route_weights, _ = lax.optimization_barrier((norm_gain, route_weights, attended))
    gain = gain.reshape(1, tp * width)
    own_state, own_terms = kernel_call(
        own_columns_kernel,
        [(residual.shape, jnp.float32), (residual.shape, jnp.bfloat16)],
        [tp_scalar],
        [weight, residual],
        lax.optimization_barrier((attended, gain))[0],
        scratch=[
            pltpu.VMEM(weight.shape[1:], jnp.bfloat16),
            pltpu.VMEM(residual.shape, jnp.bfloat16),
            dma((2,)),
        ],
    )
    for term in arriving:
        own_state = own_state + term.astype(jnp.float32)
    state_sent = own_state.astype(jnp.bfloat16)
    if tp == 2:
        own_terms = lax.optimization_barrier((own_terms, state_sent))[0]
        other_state = exchange(own_terms, "tp", 1).astype(jnp.float32) + others[0].astype(jnp.float32)
        own_blocks = [state_sent, other_state.astype(jnp.bfloat16)]
    else:
        own_blocks = [exchange(state_sent, "tp", j) for j in range(tp)]

    top_count = routes.shape[1]
    capacity = 5 * block_len * top_count // (4 * experts)
    half = experts // 2
    mixing = route_weights / jnp.sum(route_weights, axis=1, keepdims=True)
    plan = jnp.concatenate([routes.astype(jnp.float32), mixing], axis=1)
    far_plan = exchange(lax.optimization_barrier((plan, own_blocks[-1]))[0], "group", experts)

    def slots(chosen_experts, weights):
        chosen = (chosen_experts ^ me_expert)[:, :, None] == jnp.arange(half, dtype=jnp.int32)
        member = jnp.any(chosen, axis=1)
        mix = jnp.sum(jnp.where(chosen, weights[:, :, None], 0.0), axis=1)
        earlier = jnp.arange(block_len)[:, None] > jnp.arange(block_len)[None, :]
        rank = jnp.dot(
            earlier.astype(jnp.bfloat16), member.astype(jnp.bfloat16), preferred_element_type=jnp.float32
        ).astype(jnp.int32)
        hit = member.T[:, None, :] & (
            rank.T[:, None, :] == jnp.arange(capacity, dtype=jnp.int32)[None, :, None]
        )
        pick = hit.astype(jnp.bfloat16).reshape(half * capacity, block_len)
        spread = jnp.where(hit, mix.T[:, None, :], 0.0).reshape(half * capacity, block_len)
        high = spread.astype(jnp.bfloat16)
        return pick, (high, (spread - high.astype(jnp.float32)).astype(jnp.bfloat16))

    own_pick, own_spread = slots(routes, mixing)

    def after(value, *earlier):
        return lax.optimization_barrier((value, *earlier))[0]

    def whole(value):
        return [exchange(value, "tp", j) for j in range(tp)]

    def picked(pick, values):
        parts = [
            jnp.dot(pick, value, preferred_element_type=jnp.float32)
            .astype(jnp.bfloat16)
            .reshape(half, capacity, width)
            for value in values
        ]
        return jnp.stack(parts, axis=1)

    def send_rows(rows):
        return [exchange(rows[d], "group", 2 * d) for d in range(half)]

    def blend(spread, pieces):
        rows = jnp.concatenate(pieces, axis=0)
        rows_first = (((0,), (0,)), ((), ()))
        return sum(
            lax.dot_general(part, rows, rows_first, preferred_element_type=jnp.float32)
            for part in spread
        )

    def activate(sets):
        rows = sets[0].shape[1]
        (active,) = kernel_call(
            functools.partial(gate_up_kernel, tp),
            [((2 * rows, hidden), jnp.bfloat16)],
            [tp_scalar],
            [gate, up, gain],
            *sets,
            scratch=[
                pltpu.VMEM((tp, rows, width), jnp.float32),
                pltpu.VMEM((2 * rows, tp * width), jnp.bfloat16),
                pltpu.VMEM(gate.shape, jnp.bfloat16),
                pltpu.VMEM(up.shape, jnp.bfloat16),
                pltpu.VMEM(gain.shape, jnp.float32),
                dma((1 + 2 * blocks,)),
            ],
        )
        return active

    def project_down(actives):
        rows = actives[0].shape[0] // 2
        return kernel_call(
            down_kernel,
            [((rows, width), jnp.bfloat16)] * 2,
            [tp_scalar],
            [down],
            *actives,
            scratch=[
                pltpu.VMEM(down.shape, jnp.bfloat16),
                pltpu.VMEM((2 * rows, width), jnp.float32),
                dma((tp,)),
            ],
        )

    def add_halves(mine, theirs):
        summed = mine.astype(jnp.float32) + exchange(theirs, "group", 1).astype(jnp.float32)
        return summed.astype(jnp.bfloat16).reshape(half, capacity, width)

    far_blocks = whole(exchange(state_sent, "group", experts))
    own_sent = picked(own_pick, own_blocks)
    own_pieces = send_rows(own_sent)
    far_plan = after(far_plan, own_pieces[half // 2])
    far_pick, far_spread = slots(
        far_plan[:, :top_count].astype(jnp.int32), far_plan[:, top_count:]
    )
    far_sent = picked(far_pick, far_blocks)
    far_pieces = send_rows(far_sent)
    own_rows = jnp.concatenate([after(piece, far_sent) for piece in own_pieces], axis=1)
    own_active = activate([own_rows, exchange(own_rows, "group", 1)])
    own_actives = whole(own_active)
    far_rows = jnp.concatenate([after(piece, own_active) for piece in far_pieces], axis=1)
    far_active = activate([far_rows, exchange(far_rows, "group", 1)])
    far_actives = whole(far_active)
    own_actives[0] = after(own_actives[0], far_active)
    own_out = project_down(own_actives)
    far_actives[0] = after(far_actives[0], own_out[0])
    far_out = add_halves(*project_down(far_actives))
    own_out = add_halves(*own_out)
    far_sum = blend(far_spread, send_rows(far_out)).astype(jnp.bfloat16)
    far_sum = exchange(far_sum, "group", experts)
    total = own_state + blend(own_spread, send_rows(own_out)) + far_sum.astype(jnp.float32)
    return total.astype(jnp.bfloat16)


def solution(mesh):
    return jax.shard_map(
        on_device,
        mesh=mesh,
        in_specs=(
            P("group", "tp"),
            P("group", "tp"),
            P("group", "tp"),
            P("group", "tp"),
            P("group", None),
            P("group"),
            P("tp"),
            P("tp", None),
            P("group", "tp"),
            P(),
            P("group", None),
            P("group", None),
            P("group", None, "tp"),
            P("group", None, "tp"),
            P("group", None, "tp"),
        ),
        out_specs=P("group", "tp"),
        check_vma=False,
    )
```
